32 devices in a mesh: seq: 4 (over z), fsdp: 8 (over y, x, core).
Axes of the slice: x: 2, y: 2, z: 4, core: 2. Of those that a mesh axis runs over, the one named last changes fastest.
Arguments:
- history: bfloat16 [9, 8, 512, 2048], P(None, 'fsdp', 'seq'), may hold values from -6 to 6
- cotangent: bfloat16 [8, 512, 2048], P('fsdp', 'seq'), may hold values from -6 to 6
- seq_lengths: int32 [8, 3], P('fsdp'), may hold values from 1 to 510, as said below
- wq: float32 [2048, 2048], P('fsdp'), may hold values from -0.125 to 0.125
- wk: float32 [2048, 2048], P('fsdp'), may hold values from -0.125 to 0.125
- wv: float32 [2048, 2048], P('fsdp'), may hold values from -0.125 to 0.125
- wo: float32 [2048, 2048], P('fsdp'), may hold values from -2 to 2
- w_in: float32 [2048, 8192], P('fsdp'), may hold values from -0.125 to 0.125
- w_out: float32 [8192, 2048], P('fsdp'), may hold values from -0.125 to 0.125
- mix_in: float32 [2048, 100], replicated, may hold values from -0.125 to 0.125
- mix_out: float32 [100, 36], replicated, may hold values from -0.625 to 0.625
- attn_gain: float32 [2048], replicated, may hold values from 0.25 to 1.75
- mlp_gain: float32 [2048], replicated, may hold values from 0.25 to 1.75
- mix_gain: float32 [2048], replicated, may hold values from 0.25 to 1.75
Outputs:
- layer_out: bfloat16 [8, 512, 2048], P('fsdp', 'seq')
- history_grad: bfloat16 [9, 8, 512, 2048], P(None, 'fsdp', 'seq')
- wq_grad: float32 [2048, 2048], P('fsdp')
- wk_grad: float32 [2048, 2048], P('fsdp')
- wv_grad: float32 [2048, 2048], P('fsdp')
- wo_grad: float32 [2048, 2048], P('fsdp')
- w_in_grad: float32 [2048, 8192], P('fsdp')
- w_out_grad: float32 [8192, 2048], P('fsdp')
- mix_in_grad: float32 [2048, 100], replicated
- mix_out_grad: float32 [100, 36], replicated
- attn_gain_grad: float32 [2048], replicated
- mlp_gain_grad: float32 [2048], replicated
- mix_gain_grad: float32 [2048], replicated
The draws below stay inside these ranges and needn't reach their ends.
Inputs may be any that keep to these rules, and one draw needn't show every extreme that they name: `seq_lengths`: each group packs three sequences in order; the first and the last have fewer than 128 tokens, and the three sum to 512.
All inputs are finite; a program needn't handle non-finite values.
Results may differ from the reference program's by a relative error of at most 0.018.
The reference program's roundings to bfloat16 on the way count: a program that leaves them out, or rounds other values in their place, can miss the bound.
Values may be sent and summed in bfloat16 or wider, within the bound.
A program may use at most 576 MiB of HBM per device.

```python
from functools import partial
import jax
import jax.numpy as jnp
from jax import lax

D = 2048
HEADS = 16
HEAD = 128
ROT = 32
FF = 8192
MIXH = 100
HIST = 9
STREAMS = 4
TOK_DEV = 128
GROUP_TOK = 512
GROUPS = 8


def draw_seq_lengths(key, part):
    key = jax.random.fold_in(key, 7)
    first_key, last_key, pick_key = jax.random.split(key, 3)
    first_len = jax.random.randint(first_key, (GROUPS, 1), 1, TOK_DEV, dtype=jnp.int32)
    last_len = jax.random.randint(last_key, (GROUPS, 1), 1, TOK_DEV, dtype=jnp.int32)
    chosen = jax.random.randint(pick_key, (), 0, GROUPS, dtype=jnp.int32)
    marked = (jnp.arange(GROUPS, dtype=jnp.int32) == chosen)[:, None]
    first_len = jnp.where(marked, 1, first_len)
    last_len = jnp.where(marked, 1, last_len)
    middle_len = GROUP_TOK - first_len - last_len
    return jnp.concatenate([first_len, middle_len, last_len], axis=1).astype(jnp.int32)


def steps_of(stream_key, extent, cuts, low, high):
    level, own = 1.0, jax.random.fold_in(stream_key, 6)
    for position, shards_of in cuts:
        heights = jnp.exp(jax.random.uniform(jax.random.fold_in(own, position), (shards_of,), jnp.float32, low / len(cuts), high / len(cuts)))
        level = level * jnp.repeat(heights, extent[position] // shards_of).reshape([-1 if axis == position else 1 for axis in range(len(extent))])
    return level


def normal_values(stream_key, extent, deviation, bound, cuts=(), held_as=jnp.bfloat16):
    values = deviation * jax.random.normal(stream_key, extent, jnp.float32)
    if cuts:
        values = values * steps_of(stream_key, extent, cuts, -0.22, 0.18)
    return jnp.clip(values, -bound, bound).astype(held_as)


def setup_inputs(seed: int = 0) -> dict:
    keys = jax.random.split(jax.random.key(seed), 15)
    return {
        "history": normal_values(keys[0], (HIST, GROUPS, GROUP_TOK, D), 1.0, 6.0, ((1, 8), (2, 4))),
        "cotangent": normal_values(keys[1], (GROUPS, GROUP_TOK, D), 1.0, 6.0, ((0, 8), (1, 4))),
        "seq_lengths": draw_seq_lengths(jax.random.fold_in(keys[14], 71), 0),
        "wq": normal_values(keys[3], (D, D), D ** -0.5, 0.125, ((0, 8),), jnp.float32),
        "wk": normal_values(keys[4], (D, D), D ** -0.5, 0.125, ((0, 8),), jnp.float32),
        "wv": normal_values(keys[5], (D, D), D ** -0.5, 0.125, ((0, 8),), jnp.float32),
        "wo": normal_values(keys[6], (D, D), (max(D // 256, 1)) ** -0.5, 2.0, ((0, 8),), jnp.float32),
        "w_in": normal_values(keys[7], (D, FF), D ** -0.5, 0.125, ((0, 8),), jnp.float32),
        "w_out": normal_values(keys[8], (FF, D), (FF // 4) ** -0.5, 0.125, ((0, 8),), jnp.float32),
        "mix_in": normal_values(keys[9], (D, MIXH), D ** -0.5, 0.125, (), jnp.float32),
        "mix_out": normal_values(keys[10], (MIXH, STREAMS * HIST), MIXH ** -0.5, 0.625, (), jnp.float32),
        "attn_gain": jnp.clip(1.0 + 0.15 * jax.random.normal(keys[11], (D,), jnp.float32), 0.25, 1.75),
        "mlp_gain": jnp.clip(1.0 + 0.15 * jax.random.normal(keys[12], (D,), jnp.float32), 0.25, 1.75),
        "mix_gain": jnp.clip(1.0 + 0.15 * jax.random.normal(keys[13], (D,), jnp.float32), 0.25, 1.75),
    }


EPSILON = 1e-05
NEGATIVE = -1e+30

@jax.custom_vjp
def low(v):
    return lax.optimization_barrier(v.astype(jnp.bfloat16)).astype(jnp.float32)

@jax.custom_vjp
def low_back(v):
    return v

def low_keep(v):
    return (low(v), None)

def low_pass(kept, grad):
    return (grad,)

def back_keep(v):
    return (v, None)

def back_low(kept, grad):
    return (low(grad),)
low.defvjp(low_keep, low_pass)
low_back.defvjp(back_keep, back_low)

def matmul_hi(left_op, right_op):
    return jnp.dot(left_op, right_op, precision=lax.Precision.HIGHEST, preferred_element_type=jnp.float32)

def token_marks(tok_index, lengths):
    first_end = lengths[0]
    second_end = lengths[0] + lengths[1]
    segment = (tok_index >= first_end).astype(jnp.int32) + (tok_index >= second_end).astype(jnp.int32)
    seq_begin = jnp.where(segment == 0, 0, jnp.where(segment == 1, first_end, second_end))
    return (segment, (tok_index - seq_begin).astype(jnp.int32))

def rope_tables(tok_place):
    inverse = 10000.0 ** (-jnp.arange(0, ROT, 2, dtype=jnp.float32) / ROT)
    angles = tok_place.astype(jnp.float32)[:, None] * inverse[None, :]
    angles = jnp.concatenate([angles, angles], axis=1)
    return (jnp.cos(angles), jnp.sin(angles))

def rotate(values, cosine_table, sine_table):
    half_rot = ROT // 2
    rot_part = values[..., :ROT]
    turned = jnp.concatenate([-rot_part[..., half_rot:], rot_part[..., :half_rot]], axis=-1)
    moved = rot_part * cosine_table[:, None, :] + turned * sine_table[:, None, :]
    return jnp.concatenate([moved, values[..., ROT:]], axis=-1)

def norm_rows(values, gain_vec):
    inverse = lax.rsqrt(lax.optimization_barrier(jnp.mean(values * values, axis=-1, keepdims=True)) + EPSILON)
    return values * inverse * gain_vec

def gelu_exact(values):
    return jax.nn.gelu(values, approximate=False)

def attend_head(allowed, group_item):
    queries, keys_low, values_low = group_item
    scores = low_back(matmul_hi(queries, keys_low.T) * HEAD ** (-0.5))
    scores = jnp.where(allowed, scores, NEGATIVE)
    prob_rows = jax.nn.softmax(scores, axis=1)
    return matmul_hi(low(prob_rows), values_low)

def block_forward(entries, weight_list, cosine_table, sine_table, allowed):
    wq, wk, wv, wo, w_in, w_out, mix_in, mix_out, attn_gain, mlp_gain, mix_gain = weight_list
    tokens = entries.shape[1]
    last_entry = entries[HIST - 1]
    mix_pre = low_back(matmul_hi(low(norm_rows(last_entry, mix_gain)), low(mix_in)))
    mix_coef = low_back(matmul_hi(low(gelu_exact(mix_pre)), low(mix_out))).reshape(tokens, STREAMS, HIST)
    stream = jnp.einsum('ncj,jnd->cnd', mix_coef, entries, precision=lax.Precision.HIGHEST)
    q_lin = low_back(matmul_hi(low(norm_rows(stream[0], attn_gain)), low(wq))).reshape(tokens, HEADS, HEAD)
    queries = low_back(low(rotate(q_lin, cosine_table, sine_table)))
    k_lin = low_back(matmul_hi(low(norm_rows(stream[1], attn_gain)), low(wk))).reshape(tokens, HEADS, HEAD)
    keys_low = low_back(low(rotate(k_lin, cosine_table, sine_table)))
    values_low = low_back(low(matmul_hi(low(norm_rows(stream[2], attn_gain)), low(wv)))).reshape(tokens, HEADS, HEAD)
    head_fn = jax.checkpoint(partial(attend_head, allowed))
    head_outs = lax.map(head_fn, (queries.transpose(1, 0, 2), keys_low.transpose(1, 0, 2), values_low.transpose(1, 0, 2)))
    attended = low_back(low(head_outs.transpose(1, 0, 2).reshape(tokens, D)))
    attn_out = matmul_hi(attended, low(wo))
    up_proj = low_back(matmul_hi(low(norm_rows(stream[3], mlp_gain)), low(w_in)))
    mlp_out = matmul_hi(low(gelu_exact(up_proj)), low(w_out))
    return stream[3] + attn_out + mlp_out

def reference(history, cotangent, seq_lengths, wq, wk, wv, wo, w_in, w_out, mix_in, mix_out, attn_gain, mlp_gain, mix_gain):
    params = (wq, wk, wv, wo, w_in, w_out, mix_in, mix_out, attn_gain, mlp_gain, mix_gain)
    entries_all = jnp.transpose(history.astype(jnp.float32), (1, 0, 2, 3))
    cot_all = cotangent.astype(jnp.float32)

    def group_step(totals, group_item):
        entries, cot_rows, lengths = group_item
        tok_index = jnp.arange(GROUP_TOK, dtype=jnp.int32)
        segment, tok_place = token_marks(tok_index, lengths)
        cosine_table, sine_table = rope_tables(tok_place)
        allowed = (segment[:, None] == segment[None, :]) & (tok_index[:, None] >= tok_index[None, :])

        def forward_fn(entries_in, *weight_list):
            return block_forward(entries_in, weight_list, cosine_table, sine_table, allowed)
        out_rows, pullback = jax.vjp(forward_fn, entries, *params)
        grad_list = pullback(cot_rows)
        totals = tuple((t_sum + g_part for t_sum, g_part in zip(totals, grad_list[1:])))
        return (totals, (out_rows.astype(jnp.bfloat16), grad_list[0].astype(jnp.bfloat16)))
    zero_list = tuple((jnp.zeros(p_arr.shape, jnp.float32) for p_arr in params))
    totals, (group_outs, hist_grads) = lax.scan(group_step, zero_list, (entries_all, cot_all, seq_lengths))
    return (group_outs, jnp.transpose(hist_grads, (1, 0, 2, 3)), totals[0], totals[1], totals[2], totals[3], totals[4], totals[5], totals[6], totals[7], totals[8], totals[9], totals[10])
```

```python
from functools import partial

import jax
import jax.numpy as jnp
from jax import lax
from jax.experimental import pallas as pl
from jax.experimental.pallas import tpu as pltpu
from jax.sharding import PartitionSpec as P

D = 2048
HEADS = 16
HEAD = 128
ROT = 32
HIST = 9
STREAMS = 4
EPSILON = 1e-05
NEGATIVE = -1e30
MESH = pl.DeviceIdType.MESH
BF = jnp.bfloat16
F32 = jnp.float32
MIB = 2**20


def token_marks(tok_index, lengths):
    first_end = lengths[..., 0]
    second_end = first_end + lengths[..., 1]
    segment = (tok_index >= first_end).astype(jnp.int32) + (tok_index >= second_end).astype(
        jnp.int32
    )
    seq_begin = jnp.where(segment == 0, 0, jnp.where(segment == 1, first_end, second_end))
    return (segment, tok_index - seq_begin)


def rope_planes(tok_place):
    inverse = 10000.0 ** (-jnp.arange(0, ROT, 2, dtype=F32) / ROT)
    angles = tok_place.astype(F32)[:, None] * inverse[None, :]
    cosine, sine = jnp.cos(angles), jnp.sin(angles)
    rows = tok_place.shape[0]
    ones = jnp.ones((rows, HEAD - ROT), F32)
    none = jnp.zeros((rows, HEAD - ROT // 2), F32)
    gap = jnp.zeros((rows, ROT // 2), F32)
    return jnp.stack(
        [
            jnp.concatenate([cosine, cosine, ones], axis=1),
            jnp.concatenate([-sine, none], axis=1),
            jnp.concatenate([gap, sine, none[:, : HEAD - ROT]], axis=1),
        ]
    )


def norm_rows(values, gain_vec):
    inverse = lax.rsqrt(jnp.mean(values * values, axis=-1, keepdims=True) + EPSILON)
    return values * inverse * gain_vec


def norm_back(values, gain_vec, grads):
    _, pullback = jax.vjp(norm_rows, values, gain_vec)
    return pullback(grads)


def gelu_exact(values):
    return jax.nn.gelu(values, approximate=False)


def gelu_back(values, grads):
    _, pullback = jax.vjp(gelu_exact, values)
    return pullback(grads)[0]


def dot(left_op, right_op, left_dim=1, right_dim=0):
    return lax.dot_general(
        left_op, right_op, (((left_dim,), (right_dim,)), ((), ())), preferred_element_type=F32
    )


def wrap(value, extent):
    return lax.rem(value + extent, extent)


def tile(index, extent):
    return pl.ds(pl.multiple_of(index * extent, extent), extent)


class Plane:
    def __init__(self, nf):
        self.nf = nf
        self.chips = nf // 2
        self.me = lax.axis_index("fsdp")
        self.chip = self.me // 2
        self.core = lax.rem(self.me, 2)

    def on(self, step, other=0):
        core = 1 - self.core if other else self.core
        return wrap(self.chip + step, self.chips) * 2 + core


def greet(nf, ns=1):
    barrier = pltpu.get_barrier_semaphore()
    for axis, extent in (("fsdp", nf), ("seq", ns)):
        for step in range(1, extent):
            pl.semaphore_signal(
                barrier,
                inc=1,
                device_id={axis: wrap(lax.axis_index(axis) + step, extent)},
                device_id_type=MESH,
            )
    pl.semaphore_wait(barrier, nf - 1 + ns - 1)


def send(src, dst, sems, slot, axis, target):
    return pltpu.make_async_remote_copy(
        src_ref=src,
        dst_ref=dst,
        send_sem=sems[0].at[slot],
        recv_sem=sems[1].at[slot],
        device_id={axis: target},
        device_id_type=MESH,
    )


class Gather:
    def __init__(self, plane, buf, sems, base):
        self.plane, self.buf, self.sems, self.base = plane, buf, sems, base

    def direct(self, step, slot=None):
        slot = self.plane.me if slot is None else slot
        block = self.buf.at[slot]
        return send(
            block, block, self.sems, self.base + step - 1, "fsdp", self.plane.on(step)
        )

    def across(self, step, slot=None):
        slot = self.plane.on(-step) if slot is None else slot
        block = self.buf.at[slot]
        base = self.base + self.plane.chips - 1
        return send(block, block, self.sems, base + step, "fsdp", self.plane.on(0, 1))

    def start(self):
        for step in range(1, self.plane.chips):
            self.direct(step).start()
        self.across(0).start()

    def forward(self):
        for step in range(1, self.plane.chips):
            self.direct(step, self.plane.on(-step)).wait_recv()
            self.across(step).start()

    def finish(self):
        for step in range(self.plane.chips):
            self.across(step, self.plane.on(-step, 1)).wait_recv()

    def drain(self):
        for step in range(1, self.plane.chips):
            self.direct(step).wait_send()
        for step in range(self.plane.chips):
            self.across(step).wait_send()


def gather_sems(nf):
    return nf - 1


class Turn:
    def __init__(self, plane, rows_ref, full_ref, sems, base, chunks):
        self.plane, self.sems, self.base, self.chunks = plane, sems, base, chunks
        self.rows_ref, self.full_ref = rows_ref, full_ref
        self.height = rows_ref.shape[0]
        self.width = full_ref.shape[1]
        self.part = self.width // chunks

    def copy(self, chunk, step, source=None):
        nf = self.plane.nf
        target = wrap(self.plane.me + step, nf)
        source = self.plane.me if source is None else source
        begin = pl.multiple_of(target * self.width + chunk * self.part, self.part)
        return send(
            self.rows_ref.at[:, pl.ds(begin, self.part)],
            self.full_ref.at[tile(source, self.height), tile(chunk, self.part)],
            self.sems,
            self.base + chunk * (nf - 1) + step - 1,
            "fsdp",
            target,
        )

    def start(self, chunk):
        for step in range(1, self.plane.nf):
            self.copy(chunk, step).start()

    def own(self):
        self.full_ref[tile(self.plane.me, self.height), :] = self.rows_ref[
            :, tile(self.plane.me, self.width)
        ]

    def arrive(self, chunk):
        for step in range(1, self.plane.nf):
            self.copy(chunk, step, wrap(self.plane.me - step, self.plane.nf)).wait_recv()

    def drain(self, chunk):
        for step in range(1, self.plane.nf):
            self.copy(chunk, step).wait_send()


class Scatter:
    def __init__(self, plane, part, sib, rec, sems, base, chunks):
        self.plane, self.part, self.sib, self.rec = plane, part, sib, rec
        self.sems, self.base, self.chunks = sems, base, chunks
        self.width = part.shape[-1] // chunks

    def across(self, chunk, step):
        cols = tile(chunk, self.width)
        return send(
            self.part.at[self.plane.on(step, 1), :, cols],
            self.sib.at[wrap(self.plane.chip + step, self.plane.chips), :, cols],
            self.sems,
            self.base + chunk * (self.plane.nf - 1) + step,
            "fsdp",
            self.plane.on(0, 1),
        )

    def direct(self, chunk, step):
        cols = tile(chunk, self.width)
        return send(
            self.part.at[self.plane.on(step), :, cols],
            self.rec.at[step - 1, :, cols],
            self.sems,
            self.base + chunk * (self.plane.nf - 1) + self.plane.chips + step - 1,
            "fsdp",
            self.plane.on(step),
        )

    def start(self, chunk):
        for step in range(self.plane.chips):
            self.across(chunk, step).start()

    def combine(self, chunk):
        cols = tile(chunk, self.width)
        for step in range(1, self.plane.chips):
            chip = wrap(self.plane.chip + step, self.plane.chips)
            mine = self.plane.on(step)
            self.across(chunk, step).wait_recv()
            total = self.part[mine, :, cols].astype(F32) + self.sib[chip, :, cols].astype(F32)
            self.part[mine, :, cols] = total.astype(BF)
            self.direct(chunk, step).start()
        self.across(chunk, 0).wait_recv()

    def total(self, chunk):
        cols = tile(chunk, self.width)
        total = self.part[self.plane.me, :, cols].astype(F32)
        total += self.sib[self.plane.chip, :, cols].astype(F32)
        for step in range(1, self.plane.chips):
            self.direct(chunk, step).wait_recv()
            total += self.rec[step - 1, :, cols].astype(F32)
        return total

    def drain(self, chunk):
        for step in range(self.plane.chips):
            self.across(chunk, step).wait_send()
        for step in range(1, self.plane.chips):
            self.direct(chunk, step).wait_send()


def loop(extent, body):
    lax.fori_loop(0, extent, lambda i, c: (body(i), c)[1], 0)


def rows_of(ref3, begin, count):
    value = ref3[pl.ds(begin, count)]
    return value.reshape(count * value.shape[1], value.shape[2])


CHUNKS = 4


def mlp_kernel(
    nf,
    x_ref,
    g_ref,
    win_ref,
    wout_ref,
    gg_out,
    h_ref,
    dwin_ref,
    dwout_ref,
    dx_ref,
    xg,
    gg,
    wfull,
    dup,
    part,
    sib,
    rec,
    send_sem,
    recv_sem,
    copy_sem,
):
    plane = Plane(nf)
    sems = (send_sem, recv_sem)
    width = wfull.shape[1] // CHUNKS
    blocks = min(4, nf)
    tok = x_ref.shape[0]
    greet(nf)
    xg[plane.me] = x_ref[...]
    gg[plane.me] = g_ref[...]
    ag_x = Gather(plane, xg, sems, 0)
    ag_g = Gather(plane, gg, sems, nf - 1)
    turn = Turn(plane, win_ref, wfull, sems, 2 * (nf - 1), CHUNKS)
    scat = Scatter(plane, part, sib, rec, sems, (2 + CHUNKS) * (nf - 1), CHUNKS)
    ag_x.start()
    ag_g.start()
    turn.own()
    ag_x.forward()
    turn.start(0)
    ag_g.forward()
    for chunk in range(1, CHUNKS):
        turn.start(chunk)
    ag_x.finish()
    ag_g.finish()
    keep = pltpu.make_async_copy(gg, gg_out, copy_sem.at[0])
    keep.start()

    def mlp_chunk(chunk):
        turn.arrive(chunk)
        cols = tile(chunk, width)

        def rows_step(i):
            rows = tile(i, blocks * tok)
            up = dot(rows_of(xg, i * blocks, blocks), wfull[:, cols])
            dh = dot(rows_of(gg, i * blocks, blocks), wout_ref[cols, :], 1, 1)
            cdf = 0.5 * (1.0 + lax.erf(up * (0.5**0.5)))
            slope = cdf + up * jnp.exp(-0.5 * up * up) * 0.3989422804014327
            h_ref[rows, cols] = (up * cdf).astype(BF)
            dup[rows, cols] = (dh * slope).astype(BF)

        loop(nf // blocks, rows_step)

        def grad_step(i):
            feats = tile(i, 512)
            every = gg[:, :, feats].reshape(nf * tok, 512)
            dwout_ref[cols, feats] = dot(h_ref[:, cols], every, 0, 0).astype(BF)
            every = xg[:, :, feats].reshape(nf * tok, 512)
            dwin_ref[feats, cols] = dot(every, dup[:, cols], 0, 0).astype(BF)

        loop(D // 512, grad_step)

    loop(CHUNKS, mlp_chunk)

    def dx_chunk(chunk):
        feats = tile(chunk, D // CHUNKS)
        value = dot(dup[...], wfull[feats, :], 1, 1).astype(BF)
        part[:, :, feats] = value.reshape(nf, tok, D // CHUNKS)
        scat.start(chunk)

        @pl.when(chunk > 0)
        def _():
            scat.combine(chunk - 1)

    loop(CHUNKS, dx_chunk)
    scat.combine(CHUNKS - 1)

    def end_chunk(chunk):
        dx_ref[:, tile(chunk, D // CHUNKS)] = scat.total(chunk)
        scat.drain(chunk)
        turn.drain(chunk)

    loop(CHUNKS, end_chunk)
    ag_x.drain()
    ag_g.drain()
    keep.wait()


def rotated(value, planes):
    return value * planes[0] + pltpu.roll(value, HEAD - ROT // 2, 1) * planes[1] + pltpu.roll(
        value, ROT // 2, 1
    ) * planes[2]


def rotated_back(value, planes):
    return value * planes[0] - pltpu.roll(value, HEAD - ROT // 2, 1) * planes[1] - pltpu.roll(
        value, ROT // 2, 1
    ) * planes[2]


class Exchange:
    def __init__(self, ns, sems, base):
        self.ns, self.sems, self.base = ns, sems, base
        self.me = lax.axis_index("seq")

    def copy(self, src, dst, lane, step):
        return send(
            src,
            dst,
            self.sems,
            self.base + lane * (self.ns - 1) + step - 1,
            "seq",
            wrap(self.me + step, self.ns),
        )


def attend_kernel(
    nf,
    ns,
    x_refs,
    w_refs,
    wo_ref,
    planes_ref,
    gg_ref,
    lens_ref,
    xg_outs,
    wfull,
    att_ref,
    dq_ref,
    dk_ref,
    dv_ref,
    xg,
    gg,
    qkva,
    zin,
    zout,
    zback,
    dkv,
    send_sem,
    recv_sem,
    copy_sem,
):
    plane = Plane(nf)
    sems = (send_sem, recv_sem)
    tok = x_refs[0].shape[0]
    wide = wo_ref.shape[0]
    heads = wide // HEAD
    per = nf // ns
    slab = per * tok
    group_tok = ns * tok
    sq = lax.axis_index("seq")
    greet(nf, ns)
    load = pltpu.make_async_copy(gg_ref, gg, copy_sem.at[3])
    load.start()
    gathers = [Gather(plane, xg.at[i], sems, i * (nf - 1)) for i in range(3)]
    turns = [Turn(plane, w_refs[i], wfull.at[i], sems, (3 + i) * (nf - 1), 1) for i in range(3)]
    there = Exchange(ns, sems, 6 * (nf - 1))
    home = Exchange(ns, sems, 6 * (nf - 1) + 4 * (ns - 1))
    for i in range(3):
        xg[i, plane.me] = x_refs[i][...]
        gathers[i].start()
        turns[i].start(0)
        turns[i].own()

    def ship(i):
        for step in range(1, ns):
            target = wrap(sq + step, ns)
            there.copy(qkva.at[i, tile(target, slab), :], zin.at[i, sq], i, step).start()
        zin[i, sq] = qkva[i, tile(sq, slab), :]

    load.wait()

    def da_step(i):
        rows = tile(i, 4 * tok)
        qkva[3, rows, :] = dot(rows_of(gg, i * 4, 4), wo_ref[...], 1, 1).astype(BF)

    loop(nf // 4, da_step)
    ship(3)
    keeps = []
    for i in range(3):
        gathers[i].forward()
        turns[i].arrive(0)
        gathers[i].finish()
        keeps.append(pltpu.make_async_copy(xg.at[i], xg_outs[i], copy_sem.at[i]))
        keeps[i].start()

        def lin_step(r, i=i):
            rows = tile(r, 4 * tok)
            lin = dot(rows_of(xg.at[i], r * 4, 4), wfull[i])
            for head in range(heads):
                cols = slice(head * HEAD, head * HEAD + HEAD)
                piece = lin[:, cols]
                if i < 2:
                    piece = rotated(piece, [planes_ref[k, rows, :] for k in range(3)])
                qkva[i, rows, cols] = piece.astype(BF)

        loop(nf // 4, lin_step)
        ship(i)
    for i in range(4):
        for step in range(1, ns):
            there.copy(zin.at[i, 0], zin.at[i, wrap(sq - step, ns)], i, step).wait_recv()

    scale = HEAD ** (-0.5)
    queries = min(256, group_tok)
    q_slabs = queries // tok

    def pair_step(pair):
        grp = pair // heads
        head = lax.rem(pair, heads)
        cols = tile(head, HEAD)
        toks = tile(grp, tok)
        first_end = lens_ref[sq * per + grp, 0]
        second_end = first_end + lens_ref[sq * per + grp, 1]

        def part_of(i, begin, count):
            return zin[i, pl.ds(begin, count), toks, cols].reshape(count * tok, HEAD)

        keys, values = part_of(1, 0, ns), part_of(2, 0, ns)
        dkv[...] = jnp.zeros_like(dkv)

        def query_step(j):
            begin = j * q_slabs
            query, d_att = part_of(0, begin, q_slabs), part_of(3, begin, q_slabs)
            qi = j * queries + lax.broadcasted_iota(jnp.int32, (queries, group_tok), 0)
            ki = lax.broadcasted_iota(jnp.int32, (queries, group_tok), 1)
            seg_q = (qi >= first_end).astype(jnp.int32) + (qi >= second_end).astype(jnp.int32)
            seg_k = (ki >= first_end).astype(jnp.int32) + (ki >= second_end).astype(jnp.int32)
            allowed = (seg_q == seg_k) & (qi >= ki)
            scores = jnp.where(allowed, dot(query, keys, 1, 1) * scale, NEGATIVE)
            top = jnp.max(scores, axis=1, keepdims=True)
            expo = jnp.where(allowed, jnp.exp(scores - top), 0.0)
            prob = expo / jnp.sum(expo, axis=1, keepdims=True)
            prob_low = prob.astype(BF)
            attended = dot(prob_low, values)
            delta = jnp.sum(d_att.astype(F32) * attended, axis=1, keepdims=True)
            d_score = (prob * (dot(d_att, values, 1, 1) - delta)).astype(BF)
            d_query = dot(d_score, keys) * scale
            dkv[0] += dot(d_score, query, 0, 0)
            dkv[1] += dot(prob_low, d_att, 0, 0)
            where = pl.ds(begin, q_slabs)
            zout[0, where, toks, cols] = attended.astype(BF).reshape(q_slabs, tok, HEAD)
            zout[1, where, toks, cols] = d_query.astype(BF).reshape(q_slabs, tok, HEAD)

        loop(group_tok // queries, query_step)
        zout[2, :, toks, cols] = (dkv[0] * scale).astype(BF).reshape(ns, tok, HEAD)
        zout[3, :, toks, cols] = dkv[1].astype(BF).reshape(ns, tok, HEAD)

    loop(per * heads, pair_step)

    for i in range(4):
        for step in range(1, ns):
            target = wrap(sq + step, ns)
            home.copy(zout.at[i, target], zback.at[i, tile(sq, slab), :], i, step).start()
        zback[i, tile(sq, slab), :] = zout[i, sq]
    outs = (att_ref, dq_ref, dk_ref, dv_ref)
    for i in (1, 2, 3, 0):
        for step in range(1, ns):
            source = wrap(sq - step, ns)
            home.copy(zout.at[i, 0], zback.at[i, tile(source, slab), :], i, step).wait_recv()
        if i in (0, 3):
            outs[i][...] = zback[i]
        else:

            def back_step(r, i=i):
                rows = tile(r, tok)
                for head in range(heads):
                    cols = slice(head * HEAD, head * HEAD + HEAD)
                    piece = zback[i, rows, cols].astype(F32)
                    piece = rotated_back(piece, [planes_ref[k, rows, :] for k in range(3)])
                    outs[i][rows, cols] = piece.astype(BF)

            loop(nf, back_step)
    for i in range(3):
        gathers[i].drain()
        turns[i].drain(0)
        keeps[i].wait()
    for i in range(4):
        for step in range(1, ns):
            there.copy(zin.at[i, 0], zin.at[i, 0], i, step).wait_send()
            home.copy(zout.at[i, 0], zout.at[i, 0], i, step).wait_send()


def return_kernel(
    nf,
    att_ref,
    d_refs,
    wfull,
    wo_ref,
    wout_ref,
    h_ref,
    gg_ref,
    xg_refs,
    y_ref,
    dx_ref,
    dw_ref,
    dwo_ref,
    stage,
    part,
    sib,
    rec,
    send_sem,
    recv_sem,
    copy_sem,
    credit,
):
    plane = Plane(nf)
    sems = (send_sem, recv_sem)
    tok = y_ref.shape[0]
    parts, sibs = part.shape[0], sib.shape[0]
    greet(nf)
    sources = list(xg_refs) + [gg_ref]
    load = pltpu.make_async_copy(sources[0], stage, copy_sem)
    load.start()
    scats = [
        Scatter(
            plane,
            part.at[t % parts],
            sib.at[t % sibs],
            rec.at[t],
            sems,
            t * CHUNKS * (nf - 1),
            CHUNKS,
        )
        for t in range(4)
    ]
    for t in range(4):
        if t >= sibs:
            pl.semaphore_wait(credit, 1)

        def chunk_step(chunk, t=t):
            feats = tile(chunk, D // CHUNKS)
            if t >= parts:
                scats[t - parts].drain(chunk)
            if t < 3:
                value = dot(d_refs[t][...], wfull[t, feats, :], 1, 1)
            else:
                value = dot(att_ref[...], wo_ref[:, feats]) + dot(h_ref[...], wout_ref[:, feats])
            scats[t].part[:, :, feats] = value.astype(BF).reshape(nf, tok, D // CHUNKS)
            scats[t].start(chunk)

            @pl.when(chunk > 0)
            def _():
                scats[t].combine(chunk - 1)

        loop(CHUNKS, chunk_step)
        scats[t].combine(CHUNKS - 1)
        pltpu.make_async_copy(sources[t], stage, copy_sem).wait()

        def grad_step(i, t=t):
            feats = tile(i, 512)
            every = stage[:, :, feats].reshape(nf * tok, 512)
            if t < 3:
                dw_ref[t, feats, :] = dot(every, d_refs[t][...], 0, 0).astype(BF)
            else:
                dwo_ref[:, feats] = dot(att_ref[...], every, 0, 0).astype(BF)

        loop(D // 512, grad_step)
        if t < 3:
            pltpu.make_async_copy(sources[t + 1], stage, copy_sem).start()

        def total_step(chunk, t=t):
            feats = tile(chunk, D // CHUNKS)
            if t < 3:
                dx_ref[t, :, feats] = scats[t].total(chunk)
            else:
                y_ref[:, feats] = scats[t].total(chunk)

        loop(CHUNKS, total_step)
        if t + sibs < 4:
            pl.semaphore_signal(
                credit, inc=1, device_id={"fsdp": plane.on(0, 1)}, device_id_type=MESH
            )
    for t in range(4 - parts, 4):
        loop(CHUNKS, scats[t].drain)


def vmem():
    return pl.BlockSpec(memory_space=pltpu.VMEM)


def hbm():
    return pl.BlockSpec(memory_space=pltpu.HBM)


def shape(dims, dtype=BF):
    return jax.ShapeDtypeStruct(tuple(dims), dtype)


def params(ident, limit=62):
    return pltpu.CompilerParams(
        collective_id=ident, has_side_effects=True, vmem_limit_bytes=limit * MIB
    )


def run_mlp(nf, x_own, g_own, win, wout):
    tok = x_own.shape[0]
    hidden = wout.shape[0]
    chips = nf // 2
    count = (2 + 2 * CHUNKS) * (nf - 1)
    return pl.pallas_call(
        partial(mlp_kernel, nf),
        out_shape=(
            shape((nf, tok, D)),
            shape((nf * tok, hidden)),
            shape((D, hidden)),
            shape((hidden, D)),
            shape((tok, D), F32),
        ),
        in_specs=[vmem()] * 4,
        out_specs=(hbm(), vmem(), vmem(), vmem(), vmem()),
        scratch_shapes=[
            pltpu.VMEM((nf, tok, D), BF),
            pltpu.VMEM((nf, tok, D), BF),
            pltpu.VMEM((D, hidden), BF),
            pltpu.VMEM((nf * tok, hidden), BF),
            pltpu.VMEM((nf, tok, D), BF),
            pltpu.VMEM((chips, tok, D), BF),
            pltpu.VMEM((chips - 1, tok, D), BF),
            pltpu.SemaphoreType.DMA((count,)),
            pltpu.SemaphoreType.DMA((count,)),
            pltpu.SemaphoreType.DMA((1,)),
        ],
        compiler_params=params(1),
        name="mlp",
    )(x_own, g_own, win, wout)


def run_attend(nf, ns, xs, ws, wo, planes, gg, lens):
    tok = xs[0].shape[0]
    wide = wo.shape[0]
    count = 6 * (nf - 1) + 8 * (ns - 1)
    flat = shape((nf * tok, wide))

    def kernel(*refs):
        attend_kernel(
            nf, ns, refs[0:3], refs[3:6], *refs[6:10], refs[10:13], *refs[13:]
        )

    return pl.pallas_call(
        kernel,
        out_shape=(shape((nf, tok, D)),) * 3 + (shape((3, D, wide)), flat, flat, flat, flat),
        in_specs=[vmem()] * 8 + [hbm(), pl.BlockSpec(memory_space=pltpu.SMEM)],
        out_specs=(hbm(),) * 3 + (vmem(),) * 5,
        scratch_shapes=[
            pltpu.VMEM((3, nf, tok, D), BF),
            pltpu.VMEM((nf, tok, D), BF),
            pltpu.VMEM((4, nf * tok, wide), BF),
            pltpu.VMEM((4, ns, nf // ns * tok, wide), BF),
            pltpu.VMEM((4, ns, nf // ns * tok, wide), BF),
            pltpu.VMEM((4, nf * tok, wide), BF),
            pltpu.VMEM((2, ns * tok, HEAD), F32),
            pltpu.SemaphoreType.DMA((count,)),
            pltpu.SemaphoreType.DMA((count,)),
            pltpu.SemaphoreType.DMA((4,)),
        ],
        compiler_params=params(2),
        name="attend",
    )(*xs, *ws, wo, planes, gg, lens)


def run_return(nf, att, ds, wfull, wo, wout, h, gg, xgs):
    tok = gg.shape[1]
    wide = wo.shape[0]
    chips = nf // 2
    count = 4 * CHUNKS * (nf - 1)
    parts = 2 if nf <= 8 else 1

    def kernel(*refs):
        return_kernel(nf, refs[0], refs[1:4], *refs[4:9], refs[9:12], *refs[12:])

    return pl.pallas_call(
        kernel,
        out_shape=(
            shape((tok, D), F32),
            shape((3, tok, D), F32),
            shape((3, D, wide)),
            shape((wide, D)),
        ),
        in_specs=[vmem()] * 8 + [hbm()] * 4,
        out_specs=(vmem(),) * 4,
        scratch_shapes=[
            pltpu.VMEM((nf, tok, D), BF),
            pltpu.VMEM((parts, nf, tok, D), BF),
            pltpu.VMEM((2, chips, tok, D), BF),
            pltpu.VMEM((4, chips - 1, tok, D), BF),
            pltpu.SemaphoreType.DMA((count,)),
            pltpu.SemaphoreType.DMA((count,)),
            pltpu.SemaphoreType.DMA,
            pltpu.SemaphoreType.REGULAR,
        ],
        compiler_params=params(3),
        name="give_back",
    )(att, *ds, wfull, wo, wout, h, gg, *xgs)


def turn_back(nf, ns, grad):
    rows, cols = grad.shape
    piece = rows // nf // ns
    split = grad.reshape(nf, ns, piece, cols)
    split = lax.psum_scatter(split, "seq", scatter_dimension=1, tiled=True)
    split = lax.all_to_all(split, "fsdp", split_axis=0, concat_axis=0, tiled=True)
    whole = lax.all_gather(split, "seq", axis=1, tiled=True)
    return whole.transpose(1, 2, 0, 3).reshape(ns * piece, nf * cols)


def local(
    nf,
    ns,
    history,
    cotangent,
    seq_lengths,
    wq,
    wk,
    wv,
    wo,
    w_in,
    w_out,
    mix_in,
    mix_out,
    attn_gain,
    mlp_gain,
    mix_gain,
):
    entries = history[:, 0].astype(F32)
    tok_rows = entries.shape[1]
    lens = lax.all_gather(seq_lengths, "fsdp", axis=0, tiled=True)
    slab_index = lax.axis_index("seq") * tok_rows + jnp.arange(tok_rows, dtype=jnp.int32)
    every_index = jnp.tile(slab_index, nf)
    _, place = token_marks(every_index, jnp.repeat(lens, tok_rows, axis=0))
    planes = rope_planes(place)

    last_entry = entries[HIST - 1]
    mixed_low = norm_rows(last_entry, mix_gain).astype(BF)
    mix_in_low = mix_in.astype(BF)
    mix_out_low = mix_out.astype(BF)
    mix_pre = dot(mixed_low, mix_in_low)
    act_low = gelu_exact(mix_pre).astype(BF)
    mix_coef = dot(act_low, mix_out_low).reshape(tok_rows, STREAMS, HIST)
    stream = jnp.einsum("ncj,jnd->cnd", mix_coef, entries, precision=lax.Precision.HIGHEST)
    gains = (attn_gain, attn_gain, attn_gain, mlp_gain)
    normed = [norm_rows(stream[c], gains[c]).astype(BF) for c in range(STREAMS)]
    grad_out = cotangent[0]
    ws = [w.astype(BF) for w in (wq, wk, wv)]
    wo_low, win_low, wout_low = wo.astype(BF), w_in.astype(BF), w_out.astype(BF)

    gg, hidden, dwin, dwout, dx_r = run_mlp(nf, normed[3], grad_out, win_low, wout_low)
    *xgs, wfull, att, dq, dk, dv = run_attend(
        nf, ns, normed[:3], ws, wo_low, planes, gg, lens
    )
    y_sum, dx, dw, dwo = run_return(
        nf, att, (dq, dk, dv), wfull, wo_low, wout_low, hidden, gg, xgs
    )
    layer_out = (stream[3] + y_sum).astype(BF)[None]
    backs = [norm_back(stream[c], gains[c], dx[c] if c < 3 else dx_r) for c in range(STREAMS)]
    grad_stream = jnp.stack(
        [backs[0][0], backs[1][0], backs[2][0], backs[3][0] + grad_out.astype(F32)], axis=0
    )
    grad_coef = (
        jnp.einsum("cnd,jnd->ncj", grad_stream, entries, precision=lax.Precision.HIGHEST)
        .reshape(tok_rows, STREAMS * HIST)
        .astype(BF)
    )
    grad_entries = jnp.einsum(
        "ncj,cnd->jnd", mix_coef, grad_stream, precision=lax.Precision.HIGHEST
    )
    grad_pre = gelu_back(mix_pre, dot(grad_coef, mix_out_low, 1, 1)).astype(BF)
    grad_last, gain_mix = norm_back(last_entry, mix_gain, dot(grad_pre, mix_in_low, 1, 1))
    history_grad = jnp.concatenate(
        [grad_entries[: HIST - 1], (grad_entries[HIST - 1] + grad_last)[None]], axis=0
    ).astype(BF)[:, None]
    small = lax.psum(
        (
            dot(mixed_low, grad_pre, 0, 0),
            dot(act_low, grad_coef, 0, 0),
            backs[0][1] + backs[1][1] + backs[2][1],
            backs[3][1],
            gain_mix,
        ),
        ("seq", "fsdp"),
    )
    dw_in = turn_back(nf, ns, dwin).astype(F32)
    dw_qkv = [turn_back(nf, ns, dw[i]).astype(F32) for i in range(3)]
    dwout = lax.psum(dwout, "seq").astype(F32)
    dwo = lax.psum(dwo, "seq").astype(F32)
    return (layer_out, history_grad, *dw_qkv, dwo, dw_in, dwout, *small)


def solution(mesh):
    rows, rep = P("fsdp", None), P()
    in_specs = (
        P(None, "fsdp", "seq", None),
        P("fsdp", "seq", None),
    ) + (rows,) * 7 + (rep,) * 5
    out_specs = (
        P("fsdp", "seq", None),
        P(None, "fsdp", "seq", None),
    ) + (rows,) * 6 + (rep,) * 5
    body = partial(local, mesh.shape["fsdp"], mesh.shape["seq"])
    return jax.shard_map(body, mesh=mesh, in_specs=in_specs, out_specs=out_specs, check_vma=False)
```

```python
from functools import partial

import jax
import jax.numpy as jnp
from jax import lax
from jax.experimental import pallas as pl
from jax.experimental.pallas import tpu as pltpu
from jax.sharding import PartitionSpec as P

D = 2048
HEADS = 16
HEAD = 128
ROT = 32
HIST = 9
STREAMS = 4
EPSILON = 1e-05
NEGATIVE = -1e30
MESH = pl.DeviceIdType.MESH
BF = jnp.bfloat16
F32 = jnp.float32
MIB = 2**20


def token_marks(tok_index, lengths):
    first_end = lengths[..., 0]
    second_end = first_end + lengths[..., 1]
    segment = (tok_index >= first_end).astype(jnp.int32) + (tok_index >= second_end).astype(
        jnp.int32
    )
    seq_begin = jnp.where(segment == 0, 0, jnp.where(segment == 1, first_end, second_end))
    return (segment, tok_index - seq_begin)


def rope_planes(tok_place):
    inverse = 10000.0 ** (-jnp.arange(0, ROT, 2, dtype=F32) / ROT)
    angles = tok_place.astype(F32)[:, None] * inverse[None, :]
    cosine, sine = jnp.cos(angles), jnp.sin(angles)
    rows = tok_place.shape[0]
    ones = jnp.ones((rows, HEAD - ROT), F32)
    none = jnp.zeros((rows, HEAD - ROT // 2), F32)
    gap = jnp.zeros((rows, ROT // 2), F32)
    return jnp.stack(
        [
            jnp.concatenate([cosine, cosine, ones], axis=1),
            jnp.concatenate([-sine, none], axis=1),
            jnp.concatenate([gap, sine, none[:, : HEAD - ROT]], axis=1),
        ]
    )


def norm_rows(values, gain_vec):
    inverse = lax.rsqrt(jnp.mean(values * values, axis=-1, keepdims=True) + EPSILON)
    return values * inverse * gain_vec


def norm_back(values, gain_vec, grads):
    _, pullback = jax.vjp(norm_rows, values, gain_vec)
    return pullback(grads)


def gelu_exact(values):
    return jax.nn.gelu(values, approximate=False)


def gelu_back(values, grads):
    _, pullback = jax.vjp(gelu_exact, values)
    return pullback(grads)[0]


def dot(left_op, right_op, left_dim=1, right_dim=0):
    return lax.dot_general(
        left_op, right_op, (((left_dim,), (right_dim,)), ((), ())), preferred_element_type=F32
    )


def wrap(value, extent):
    return lax.rem(value + extent, extent)


def tile(index, extent):
    return pl.ds(pl.multiple_of(index * extent, extent), extent)


class Plane:
    def __init__(self, nf):
        self.nf = nf
        self.chips = nf // 2
        self.me = lax.axis_index("fsdp")
        self.chip = self.me // 2
        self.core = lax.rem(self.me, 2)

    def on(self, step, other=0):
        core = 1 - self.core if other else self.core
        return wrap(self.chip + step, self.chips) * 2 + core


def greet(nf, ns=1):
    barrier = pltpu.get_barrier_semaphore()
    for axis, extent in (("fsdp", nf), ("seq", ns)):
        for step in range(1, extent):
            pl.semaphore_signal(
                barrier,
                inc=1,
                device_id={axis: wrap(lax.axis_index(axis) + step, extent)},
                device_id_type=MESH,
            )
    pl.semaphore_wait(barrier, nf - 1 + ns - 1)


def send(src, dst, sems, slot, axis, target):
    return pltpu.make_async_remote_copy(
        src_ref=src,
        dst_ref=dst,
        send_sem=sems[0].at[slot],
        recv_sem=sems[1].at[slot],
        device_id={axis: target},
        device_id_type=MESH,
    )


class Gather:
    def __init__(self, plane, buf, sems, base):
        self.plane, self.buf, self.sems, self.base = plane, buf, sems, base

    def direct(self, step, slot=None):
        slot = self.plane.me if slot is None else slot
        block = self.buf.at[slot]
        return send(
            block, block, self.sems, self.base + step - 1, "fsdp", self.plane.on(step)
        )

    def across(self, step, slot=None):
        slot = self.plane.on(-step) if slot is None else slot
        block = self.buf.at[slot]
        base = self.base + self.plane.chips - 1
        return send(block, block, self.sems, base + step, "fsdp", self.plane.on(0, 1))

    def start(self):
        for step in range(1, self.plane.chips):
            self.direct(step).start()
        self.across(0).start()

    def forward(self):
        for step in range(1, self.plane.chips):
            self.direct(step, self.plane.on(-step)).wait_recv()
            self.across(step).start()

    def finish(self):
        for step in range(self.plane.chips):
            self.across(step, self.plane.on(-step, 1)).wait_recv()

    def drain(self):
        for step in range(1, self.plane.chips):
            self.direct(step).wait_send()
        for step in range(self.plane.chips):
            self.across(step).wait_send()


def gather_sems(nf):
    return nf - 1


class Turn:
    def __init__(self, plane, rows_ref, full_ref, sems, base, chunks):
        self.plane, self.sems, self.base, self.chunks = plane, sems, base, chunks
        self.rows_ref, self.full_ref = rows_ref, full_ref
        self.height = rows_ref.shape[0]
        self.width = full_ref.shape[1]
        self.part = self.width // chunks

    def copy(self, chunk, step, source=None):
        nf = self.plane.nf
        target = wrap(self.plane.me + step, nf)
        source = self.plane.me if source is None else source
        begin = pl.multiple_of(target * self.width + chunk * self.part, self.part)
        return send(
            self.rows_ref.at[:, pl.ds(begin, self.part)],
            self.full_ref.at[tile(source, self.height), tile(chunk, self.part)],
            self.sems,
            self.base + chunk * (nf - 1) + step - 1,
            "fsdp",
            target,
        )

    def start(self, chunk):
        for step in range(1, self.plane.nf):
            self.copy(chunk, step).start()

    def own(self):
        self.full_ref[tile(self.plane.me, self.height), :] = self.rows_ref[
            :, tile(self.plane.me, self.width)
        ]

    def arrive(self, chunk):
        for step in range(1, self.plane.nf):
            self.copy(chunk, step, wrap(self.plane.me - step, self.plane.nf)).wait_recv()

    def drain(self, chunk):
        for step in range(1, self.plane.nf):
            self.copy(chunk, step).wait_send()


class Scatter:
    def __init__(self, plane, part, sib, rec, sems, base, chunks):
        self.plane, self.part, self.sib, self.rec = plane, part, sib, rec
        self.sems, self.base, self.chunks = sems, base, chunks
        self.width = part.shape[-1] // chunks

    def across(self, chunk, step):
        cols = tile(chunk, self.width)
        return send(
            self.part.at[self.plane.on(step, 1), :, cols],
            self.sib.at[wrap(self.plane.chip + step, self.plane.chips), :, cols],
            self.sems,
            self.base + chunk * (self.plane.nf - 1) + step,
            "fsdp",
            self.plane.on(0, 1),
        )

    def direct(self, chunk, step):
        cols = tile(chunk, self.width)
        return send(
            self.part.at[self.plane.on(step), :, cols],
            self.rec.at[step - 1, :, cols],
            self.sems,
            self.base + chunk * (self.plane.nf - 1) + self.plane.chips + step - 1,
            "fsdp",
            self.plane.on(step),
        )

    def start(self, chunk):
        for step in range(self.plane.chips):
            self.across(chunk, step).start()

    def combine(self, chunk):
        cols = tile(chunk, self.width)
        for step in range(1, self.plane.chips):
            chip = wrap(self.plane.chip + step, self.plane.chips)
            mine = self.plane.on(step)
            self.across(chunk, step).wait_recv()
            total = self.part[mine, :, cols].astype(F32) + self.sib[chip, :, cols].astype(F32)
            self.part[mine, :, cols] = total.astype(BF)
            self.direct(chunk, step).start()
        self.across(chunk, 0).wait_recv()

    def total(self, chunk):
        cols = tile(chunk, self.width)
        total = self.part[self.plane.me, :, cols].astype(F32)
        total += self.sib[self.plane.chip, :, cols].astype(F32)
        for step in range(1, self.plane.chips):
            self.direct(chunk, step).wait_recv()
            total += self.rec[step - 1, :, cols].astype(F32)
        return total

    def drain(self, chunk):
        for step in range(self.plane.chips):
            self.across(chunk, step).wait_send()
        for step in range(1, self.plane.chips):
            self.direct(chunk, step).wait_send()


def loop(extent, body):
    lax.fori_loop(0, extent, lambda i, c: (body(i), c)[1], 0)


def rows_of(ref3, begin, count):
    value = ref3[pl.ds(begin, count)]
    return value.reshape(count * value.shape[1], value.shape[2])


CHUNKS = 4


def mlp_kernel(
    nf,
    x_ref,
    g_ref,
    win_ref,
    wout_ref,
    gg_out,
    h_ref,
    dwin_ref,
    dwout_ref,
    dx_ref,
    xg,
    gg,
    wfull,
    dup,
    part,
    sib,
    rec,
    send_sem,
    recv_sem,
    copy_sem,
):
    plane = Plane(nf)
    sems = (send_sem, recv_sem)
    width = wfull.shape[1] // CHUNKS
    blocks = min(4, nf)
    tok = x_ref.shape[0]
    greet(nf)
    xg[plane.me] = x_ref[...]
    gg[plane.me] = g_ref[...]
    ag_x = Gather(plane, xg, sems, 0)
    ag_g = Gather(plane, gg, sems, nf - 1)
    turn = Turn(plane, win_ref, wfull, sems, 2 * (nf - 1), CHUNKS)
    scat = Scatter(plane, part, sib, rec, sems, (2 + CHUNKS) * (nf - 1), CHUNKS)
    ag_x.start()
    ag_g.start()
    turn.own()
    ag_x.forward()
    turn.start(0)
    ag_g.forward()
    for chunk in range(1, CHUNKS):
        turn.start(chunk)
    ag_x.finish()
    ag_g.finish()
    keep = pltpu.make_async_copy(gg, gg_out, copy_sem.at[0])
    keep.start()

    def mlp_chunk(chunk):
        turn.arrive(chunk)
        cols = tile(chunk, width)

        def rows_step(i):
            rows = tile(i, blocks * tok)
            up = dot(rows_of(xg, i * blocks, blocks), wfull[:, cols])
            dh = dot(rows_of(gg, i * blocks, blocks), wout_ref[cols, :], 1, 1)
            cdf = 0.5 * (1.0 + lax.erf(up * (0.5**0.5)))
            slope = cdf + up * jnp.exp(-0.5 * up * up) * 0.3989422804014327
            h_ref[rows, cols] = (up * cdf).astype(BF)
            dup[rows, cols] = (dh * slope).astype(BF)

        loop(nf // blocks, rows_step)

        def grad_step(i):
            feats = tile(i, 512)
            every = gg[:, :, feats].reshape(nf * tok, 512)
            dwout_ref[cols, feats] = dot(h_ref[:, cols], every, 0, 0).astype(BF)
            every = xg[:, :, feats].reshape(nf * tok, 512)
            dwin_ref[feats, cols] = dot(every, dup[:, cols], 0, 0).astype(BF)

        loop(D // 512, grad_step)

    loop(CHUNKS, mlp_chunk)

    def dx_chunk(chunk):
        feats = tile(chunk, D // CHUNKS)
        value = dot(dup[...], wfull[feats, :], 1, 1).astype(BF)
        part[:, :, feats] = value.reshape(nf, tok, D // CHUNKS)
        scat.start(chunk)

        @pl.when(chunk > 0)
        def _():
            scat.combine(chunk - 1)

    loop(CHUNKS, dx_chunk)
    scat.combine(CHUNKS - 1)

    def end_chunk(chunk):
        dx_ref[:, tile(chunk, D // CHUNKS)] = scat.total(chunk)
        scat.drain(chunk)
        turn.drain(chunk)

    loop(CHUNKS, end_chunk)
    ag_x.drain()
    ag_g.drain()
    keep.wait()


def rotated(value, planes):
    return value * planes[0] + pltpu.roll(value, HEAD - ROT // 2, 1) * planes[1] + pltpu.roll(
        value, ROT // 2, 1
    ) * planes[2]


def rotated_back(value, planes):
    return value * planes[0] - pltpu.roll(value, HEAD - ROT // 2, 1) * planes[1] - pltpu.roll(
        value, ROT // 2, 1
    ) * planes[2]


class Exchange:
    def __init__(self, ns, sems, base):
        self.ns, self.sems, self.base = ns, sems, base
        self.me = lax.axis_index("seq")

    def copy(self, src, dst, lane, step):
        return send(
            src,
            dst,
            self.sems,
            self.base + lane * (self.ns - 1) + step - 1,
            "seq",
            wrap(self.me + step, self.ns),
        )


def attend_kernel(
    nf,
    ns,
    x_refs,
    w_refs,
    wo_ref,
    planes_ref,
    gg_ref,
    lens_ref,
    xg_outs,
    wfull,
    att_ref,
    dq_ref,
    dk_ref,
    dv_ref,
    xg,
    gg,
    qkva,
    zin,
    zout,
    zback,
    dkv,
    send_sem,
    recv_sem,
    copy_sem,
):
    plane = Plane(nf)
    sems = (send_sem, recv_sem)
    tok = x_refs[0].shape[0]
    wide = wo_ref.shape[0]
    heads = wide // HEAD
    per = nf // ns
    slab = per * tok
    group_tok = ns * tok
    sq = lax.axis_index("seq")
    greet(nf, ns)
    load = pltpu.make_async_copy(gg_ref, gg, copy_sem.at[3])
    load.start()
    gathers = [Gather(plane, xg.at[i], sems, i * (nf - 1)) for i in range(3)]
    turns = [Turn(plane, w_refs[i], wfull.at[i], sems, (3 + i) * (nf - 1), 1) for i in range(3)]
    there = Exchange(ns, sems, 6 * (nf - 1))
    home = Exchange(ns, sems, 6 * (nf - 1) + 4 * (ns - 1))
    for i in range(3):
        xg[i, plane.me] = x_refs[i][...]
        gathers[i].start()
        turns[i].start(0)
        turns[i].own()

    def ship(i):
        for step in range(1, ns):
            target = wrap(sq + step, ns)
            there.copy(qkva.at[i, tile(target, slab), :], zin.at[i, sq], i, step).start()
        zin[i, sq] = qkva[i, tile(sq, slab), :]

    load.wait()

    def da_step(i):
        rows = tile(i, 4 * tok)
        qkva[3, rows, :] = dot(rows_of(gg, i * 4, 4), wo_ref[...], 1, 1).astype(BF)

    loop(nf // 4, da_step)
    ship(3)
    keeps = []
    for i in range(3):
        gathers[i].forward()
        turns[i].arrive(0)
        gathers[i].finish()
        keeps.append(pltpu.make_async_copy(xg.at[i], xg_outs[i], copy_sem.at[i]))
        keeps[i].start()

        def lin_step(r, i=i):
            rows = tile(r, 4 * tok)
            lin = dot(rows_of(xg.at[i], r * 4, 4), wfull[i])
            for head in range(heads):
                cols = slice(head * HEAD, head * HEAD + HEAD)
                piece = lin[:, cols]
                if i < 2:
                    piece = rotated(piece, [planes_ref[k, rows, :] for k in range(3)])
                qkva[i, rows, cols] = piece.astype(BF)

        loop(nf // 4, lin_step)
        ship(i)
    for i in range(4):
        for step in range(1, ns):
            there.copy(zin.at[i, 0], zin.at[i, wrap(sq - step, ns)], i, step).wait_recv()

    scale = HEAD ** (-0.5)
    queries = min(256, group_tok)
    q_slabs = queries // tok

    def pair_step(pair):
        grp = pair // heads
        head = lax.rem(pair, heads)
        cols = tile(head, HEAD)
        toks = tile(grp, tok)
        first_end = lens_ref[sq * per + grp, 0]
        second_end = first_end + lens_ref[sq * per + grp, 1]

        def part_of(i, begin, count):
            return zin[i, pl.ds(begin, count), toks, cols].reshape(count * tok, HEAD)

        keys, values = part_of(1, 0, ns), part_of(2, 0, ns)
        dkv[...] = jnp.zeros_like(dkv)

        def query_step(j):
            begin = j * q_slabs
            query, d_att = part_of(0, begin, q_slabs), part_of(3, begin, q_slabs)
            qi = j * queries + lax.broadcasted_iota(jnp.int32, (queries, group_tok), 0)
            ki = lax.broadcasted_iota(jnp.int32, (queries, group_tok), 1)
            seg_q = (qi >= first_end).astype(jnp.int32) + (qi >= second_end).astype(jnp.int32)
            seg_k = (ki >= first_end).astype(jnp.int32) + (ki >= second_end).astype(jnp.int32)
            allowed = (seg_q == seg_k) & (qi >= ki)
            scores = jnp.where(allowed, dot(query, keys, 1, 1) * scale, NEGATIVE)
            top = jnp.max(scores, axis=1, keepdims=True)
            expo = jnp.where(allowed, jnp.exp(scores - top), 0.0)
            prob = expo / jnp.sum(expo, axis=1, keepdims=True)
            prob_low = prob.astype(BF)
            attended = dot(prob_low, values)
            delta = jnp.sum(d_att.astype(F32) * attended, axis=1, keepdims=True)
            d_score = (prob * (dot(d_att, values, 1, 1) - delta)).astype(BF)
            d_query = dot(d_score, keys) * scale
            dkv[0] += dot(d_score, query, 0, 0)
            dkv[1] += dot(prob_low, d_att, 0, 0)
            where = pl.ds(begin, q_slabs)
            zout[0, where, toks, cols] = attended.astype(BF).reshape(q_slabs, tok, HEAD)
            zout[1, where, toks, cols] = d_query.astype(BF).reshape(q_slabs, tok, HEAD)

        loop(group_tok // queries, query_step)
        zout[2, :, toks, cols] = (dkv[0] * scale).astype(BF).reshape(ns, tok, HEAD)
        zout[3, :, toks, cols] = dkv[1].astype(BF).reshape(ns, tok, HEAD)

    loop(per * heads, pair_step)

    for i in range(4):
        for step in range(1, ns):
            target = wrap(sq + step, ns)
            home.copy(zout.at[i, target], zback.at[i, tile(sq, slab), :], i, step).start()
        zback[i, tile(sq, slab), :] = zout[i, sq]
    outs = (att_ref, dq_ref, dk_ref, dv_ref)
    for i in (1, 2, 3, 0):
        for step in range(1, ns):
            source = wrap(sq - step, ns)
            home.copy(zout.at[i, 0], zback.at[i, tile(source, slab), :], i, step).wait_recv()
        if i in (0, 3):
            outs[i][...] = zback[i]
        else:

            def back_step(r, i=i):
                rows = tile(r, tok)
                for head in range(heads):
                    cols = slice(head * HEAD, head * HEAD + HEAD)
                    piece = zback[i, rows, cols].astype(F32)
                    piece = rotated_back(piece, [planes_ref[k, rows, :] for k in range(3)])
                    outs[i][rows, cols] = piece.astype(BF)

            loop(nf, back_step)
    for i in range(3):
        gathers[i].drain()
        turns[i].drain(0)
        keeps[i].wait()
    for i in range(4):
        for step in range(1, ns):
            there.copy(zin.at[i, 0], zin.at[i, 0], i, step).wait_send()
            home.copy(zout.at[i, 0], zout.at[i, 0], i, step).wait_send()


def return_kernel(
    nf,
    att_ref,
    d_refs,
    wfull,
    wo_ref,
    wout_ref,
    h_ref,
    gg_ref,
    xg_refs,
    y_ref,
    dx_ref,
    dw_ref,
    dwo_ref,
    stage,
    part,
    sib,
    rec,
    send_sem,
    recv_sem,
    copy_sem,
    credit,
):
    plane = Plane(nf)
    sems = (send_sem, recv_sem)
    tok = y_ref.shape[0]
    parts, sibs = part.shape[0], sib.shape[0]
    greet(nf)
    sources = list(xg_refs) + [gg_ref]
    load = pltpu.make_async_copy(sources[0], stage, copy_sem)
    load.start()
    scats = [
        Scatter(
            plane,
            part.at[t % parts],
            sib.at[t % sibs],
            rec.at[t],
            sems,
            t * CHUNKS * (nf - 1),
            CHUNKS,
        )
        for t in range(4)
    ]
    for t in range(4):
        if t >= sibs:
            pl.semaphore_wait(credit, 1)

        def chunk_step(chunk, t=t):
            feats = tile(chunk, D // CHUNKS)
            if t >= parts:
                scats[t - parts].drain(chunk)
            if t < 3:
                value = dot(d_refs[t][...], wfull[t, feats, :], 1, 1)
            else:
                value = dot(att_ref[...], wo_ref[:, feats]) + dot(h_ref[...], wout_ref[:, feats])
            scats[t].part[:, :, feats] = value.astype(BF).reshape(nf, tok, D // CHUNKS)
            scats[t].start(chunk)

            @pl.when(chunk > 0)
            def _():
                scats[t].combine(chunk - 1)

        loop(CHUNKS, chunk_step)
        scats[t].combine(CHUNKS - 1)
        pltpu.make_async_copy(sources[t], stage, copy_sem).wait()

        def grad_step(i, t=t):
            feats = tile(i, 512)
            every = stage[:, :, feats].reshape(nf * tok, 512)
            if t < 3:
                dw_ref[t, feats, :] = dot(every, d_refs[t][...], 0, 0).astype(BF)
            else:
                dwo_ref[:, feats] = dot(att_ref[...], every, 0, 0).astype(BF)

        loop(D // 512, grad_step)
        if t < 3:
            pltpu.make_async_copy(sources[t + 1], stage, copy_sem).start()

        def total_step(chunk, t=t):
            feats = tile(chunk, D // CHUNKS)
            if t < 3:
                dx_ref[t, :, feats] = scats[t].total(chunk)
            else:
                y_ref[:, feats] = scats[t].total(chunk)

        loop(CHUNKS, total_step)
        if t + sibs < 4:
            pl.semaphore_signal(
                credit, inc=1, device_id={"fsdp": plane.on(0, 1)}, device_id_type=MESH
            )
    for t in range(4 - parts, 4):
        loop(CHUNKS, scats[t].drain)


def vmem():
    return pl.BlockSpec(memory_space=pltpu.VMEM)


def hbm():
    return pl.BlockSpec(memory_space=pltpu.HBM)


def shape(dims, dtype=BF):
    return jax.ShapeDtypeStruct(tuple(dims), dtype)


def params(ident, limit=62):
    return pltpu.CompilerParams(
        collective_id=ident, has_side_effects=True, vmem_limit_bytes=limit * MIB
    )


def run_mlp(nf, x_own, g_own, win, wout):
    tok = x_own.shape[0]
    hidden = wout.shape[0]
    chips = nf // 2
    count = (2 + 2 * CHUNKS) * (nf - 1)
    return pl.pallas_call(
        partial(mlp_kernel, nf),
        out_shape=(
            shape((nf, tok, D)),
            shape((nf * tok, hidden)),
            shape((D, hidden)),
            shape((hidden, D)),
            shape((tok, D), F32),
        ),
        in_specs=[vmem()] * 4,
        out_specs=(hbm(), vmem(), vmem(), vmem(), vmem()),
        scratch_shapes=[
            pltpu.VMEM((nf, tok, D), BF),
            pltpu.VMEM((nf, tok, D), BF),
            pltpu.VMEM((D, hidden), BF),
            pltpu.VMEM((nf * tok, hidden), BF),
            pltpu.VMEM((nf, tok, D), BF),
            pltpu.VMEM((chips, tok, D), BF),
            pltpu.VMEM((chips - 1, tok, D), BF),
            pltpu.SemaphoreType.DMA((count,)),
            pltpu.SemaphoreType.DMA((count,)),
            pltpu.SemaphoreType.DMA((1,)),
        ],
        compiler_params=params(1),
        name="mlp",
    )(x_own, g_own, win, wout)


def run_attend(nf, ns, xs, ws, wo, planes, gg, lens):
    tok = xs[0].shape[0]
    wide = wo.shape[0]
    count = 6 * (nf - 1) + 8 * (ns - 1)
    flat = shape((nf * tok, wide))

    def kernel(*refs):
        attend_kernel(
            nf, ns, refs[0:3], refs[3:6], *refs[6:10], refs[10:13], *refs[13:]
        )

    return pl.pallas_call(
        kernel,
        out_shape=(shape((nf, tok, D)),) * 3 + (shape((3, D, wide)), flat, flat, flat, flat),
        in_specs=[vmem()] * 8 + [hbm(), pl.BlockSpec(memory_space=pltpu.SMEM)],
        out_specs=(hbm(),) * 3 + (vmem(),) * 5,
        scratch_shapes=[
            pltpu.VMEM((3, nf, tok, D), BF),
            pltpu.VMEM((nf, tok, D), BF),
            pltpu.VMEM((4, nf * tok, wide), BF),
            pltpu.VMEM((4, ns, nf // ns * tok, wide), BF),
            pltpu.VMEM((4, ns, nf // ns * tok, wide), BF),
            pltpu.VMEM((4, nf * tok, wide), BF),
            pltpu.VMEM((2, ns * tok, HEAD), F32),
            pltpu.SemaphoreType.DMA((count,)),
            pltpu.SemaphoreType.DMA((count,)),
            pltpu.SemaphoreType.DMA((4,)),
        ],
        compiler_params=params(2),
        name="attend",
    )(*xs, *ws, wo, planes, gg, lens)


def run_return(nf, att, ds, wfull, wo, wout, h, gg, xgs):
    tok = gg.shape[1]
    wide = wo.shape[0]
    chips = nf // 2
    count = 4 * CHUNKS * (nf - 1)
    parts = 2 if nf <= 8 else 1

    def kernel(*refs):
        return_kernel(nf, refs[0], refs[1:4], *refs[4:9], refs[9:12], *refs[12:])

    return pl.pallas_call(
        kernel,
        out_shape=(
            shape((tok, D), F32),
            shape((3, tok, D), F32),
            shape((3, D, wide)),
            shape((wide, D)),
        ),
        in_specs=[vmem()] * 8 + [hbm()] * 4,
        out_specs=(vmem(),) * 4,
        scratch_shapes=[
            pltpu.VMEM((nf, tok, D), BF),
            pltpu.VMEM((parts, nf, tok, D), BF),
            pltpu.VMEM((2, chips, tok, D), BF),
            pltpu.VMEM((4, chips - 1, tok, D), BF),
            pltpu.SemaphoreType.DMA((count,)),
            pltpu.SemaphoreType.DMA((count,)),
            pltpu.SemaphoreType.DMA,
            pltpu.SemaphoreType.REGULAR,
        ],
        compiler_params=params(3),
        name="give_back",
    )(att, *ds, wfull, wo, wout, h, gg, *xgs)


ROWS = 16
WIDTH = 512


def start_kernel(
    hist_ref,
    mix_in_ref,
    mix_out_ref,
    again_ref,
    mgain_ref,
    xgain_ref,
    low_ref,
    st_ref,
    coef_ref,
    inv_ref,
    pre_ref,
    act_ref,
    mixed_ref,
):
    tok = hist_ref.shape[1]

    def mix_step(i):
        rows = tile(i, ROWS)
        value = hist_ref[HIST - 1, rows, :].astype(F32)
        inv = lax.rsqrt(jnp.mean(value * value, axis=1, keepdims=True) + EPSILON)
        mixed_ref[rows, :] = (value * inv * xgain_ref[...]).astype(BF)
        inv_ref[STREAMS, rows, :] = inv

    loop(tok // ROWS, mix_step)
    pre = dot(mixed_ref[...], mix_in_ref[...].astype(BF))
    pre_ref[...] = pre
    act = (0.5 * pre * (1.0 + lax.erf(pre * (0.5**0.5)))).astype(BF)
    act_ref[...] = act
    coef_ref[...] = dot(act, mix_out_ref[...].astype(BF))

    def stream_step(i):
        rows = tile(i, ROWS)
        coef = coef_ref[rows, :]
        squares = [jnp.zeros((ROWS, 1), F32)] * STREAMS
        for begin in range(0, D, WIDTH):
            cols = slice(begin, begin + WIDTH)
            total = [jnp.zeros((ROWS, WIDTH), F32)] * STREAMS
            for j in range(HIST):
                entry = hist_ref[j, rows, cols].astype(F32)
                for c in range(STREAMS):
                    at = c * HIST + j
                    total[c] = total[c] + coef[:, at : at + 1] * entry
            for c in range(STREAMS):
                st_ref[c, rows, cols] = total[c]
                squares[c] = squares[c] + jnp.sum(total[c] * total[c], axis=1, keepdims=True)
        for c in range(STREAMS):
            inv = lax.rsqrt(squares[c] / D + EPSILON)
            inv_ref[c, rows, :] = inv
            gain = mgain_ref if c == STREAMS - 1 else again_ref
            low_ref[c, rows, :] = (st_ref[c, rows, :] * inv * gain[...]).astype(BF)

    loop(tok // ROWS, stream_step)


def run_start(hist, mix_in, mix_out, again, mgain, xgain):
    tok = hist.shape[1]
    hidden = mix_in.shape[1]
    return pl.pallas_call(
        start_kernel,
        out_shape=(
            shape((STREAMS, tok, D)),
            shape((STREAMS, tok, D), F32),
            shape((tok, STREAMS * HIST), F32),
            shape((STREAMS + 1, tok, 1), F32),
            shape((tok, hidden), F32),
            shape((tok, hidden)),
            shape((tok, D)),
        ),
        in_specs=[vmem()] * 6,
        out_specs=(vmem(),) * 7,
        compiler_params=pltpu.CompilerParams(vmem_limit_bytes=62 * MIB),
        name="streams",
    )(hist, mix_in, mix_out, again, mgain, xgain)


SMALL = 112


def end_kernel(
    hist_ref,
    st_ref,
    dx_ref,
    dxr_ref,
    g_ref,
    y_ref,
    coef_ref,
    inv_ref,
    pre_ref,
    act_ref,
    mixed_ref,
    mix_in_ref,
    mix_out_ref,
    again_ref,
    mgain_ref,
    xgain_ref,
    hg_ref,
    lo_ref,
    sm_ref,
    ds,
    last,
    dmixed,
    dcoef,
    gsum,
):
    tok = hist_ref.shape[1]
    gsum[...] = jnp.zeros_like(gsum)

    def back(value, inv, gain, grad):
        scaled = grad * gain
        mean = jnp.sum(value * scaled, axis=1, keepdims=True) / D
        return inv * scaled - value * (inv * inv * inv * mean)

    def row_step(i):
        rows = tile(i, ROWS)
        coef = coef_ref[rows, :]
        lane = lax.broadcasted_iota(jnp.int32, (ROWS, STREAMS * HIST), 1)
        for c in range(STREAMS):
            value, inv = st_ref[c, rows, :], inv_ref[c, rows, :]
            grad = dxr_ref[rows, :] if c == STREAMS - 1 else dx_ref[c, rows, :]
            gain = mgain_ref if c == STREAMS - 1 else again_ref
            gsum[c // 3] += grad * (value * inv)
            d_value = back(value, inv, gain[...], grad)
            if c == STREAMS - 1:
                d_value = d_value + g_ref[rows, :].astype(F32)
                lo_ref[rows, :] = (value + y_ref[rows, :]).astype(BF)
            ds[c] = d_value
        found = jnp.zeros((ROWS, STREAMS * HIST), F32)
        for j in range(HIST):
            sums = [jnp.zeros((ROWS, 128), F32)] * STREAMS
            for begin in range(0, D, WIDTH):
                cols = slice(begin, begin + WIDTH)
                entry = hist_ref[j, rows, cols].astype(F32)
                grad = jnp.zeros((ROWS, WIDTH), F32)
                for c in range(STREAMS):
                    at = c * HIST + j
                    value = ds[c, :, cols]
                    grad = grad + coef[:, at : at + 1] * value
                    product = value * entry
                    for k in range(0, WIDTH, 128):
                        sums[c] = sums[c] + product[:, k : k + 128]
                if j < HIST - 1:
                    hg_ref[j, rows, cols] = grad.astype(BF)
                else:
                    last[rows, cols] = grad
            for c in range(STREAMS):
                value = jnp.sum(sums[c], axis=1, keepdims=True)
                found = jnp.where(lane == c * HIST + j, value, found)
        dcoef[rows, :] = found.astype(BF)

    loop(tok // ROWS, row_step)
    mix_in, mix_out = mix_in_ref[...].astype(BF), mix_out_ref[...].astype(BF)
    pre, d_coef = pre_ref[...], dcoef[...]
    slope = 0.5 * (1.0 + lax.erf(pre * (0.5**0.5)))
    slope = slope + pre * jnp.exp(-0.5 * pre * pre) * 0.3989422804014327
    d_pre = (dot(d_coef, mix_out, 1, 1) * slope).astype(BF)
    hidden = pre.shape[1]
    sm_ref[0:hidden, :] = dot(d_pre, mixed_ref[...], 0, 0)
    dmixed[...] = dot(d_pre, mix_in, 1, 1)

    def last_step(i):
        rows = tile(i, ROWS)
        value, inv, grad = hist_ref[HIST - 1, rows, :].astype(F32), inv_ref[STREAMS, rows, :], dmixed[rows, :]
        gsum[2] += grad * (value * inv)
        total = last[rows, :] + back(value, inv, xgain_ref[...], grad)
        hg_ref[HIST - 1, rows, :] = total.astype(BF)

    loop(tok // ROWS, last_step)
    for k in range(3):
        sm_ref[hidden + k : hidden + k + 1, :] = jnp.sum(gsum[k], axis=0, keepdims=True)
    begin = hidden + 3
    sm_ref[begin:SMALL, :] = jnp.zeros((SMALL - begin, D), F32)
    turned = dot(d_coef, act_ref[...], 0, 0)
    for k in range(STREAMS * HIST):
        at = begin + k // STREAMS
        cols = slice(k % STREAMS * 128, k % STREAMS * 128 + hidden)
        sm_ref[at : at + 1, cols] = turned[k : k + 1, :]


def run_end(*args):
    tok = args[0].shape[1]
    return pl.pallas_call(
        end_kernel,
        out_shape=(shape((HIST, tok, D)), shape((tok, D)), shape((SMALL, D), F32)),
        in_specs=[vmem()] * 16,
        out_specs=(vmem(),) * 3,
        scratch_shapes=[
            pltpu.VMEM((STREAMS, ROWS, D), F32),
            pltpu.VMEM((tok, D), F32),
            pltpu.VMEM((tok, D), F32),
            pltpu.VMEM((tok, STREAMS * HIST), BF),
            pltpu.VMEM((3, ROWS, D), F32),
        ],
        compiler_params=pltpu.CompilerParams(vmem_limit_bytes=62 * MIB),
        name="streams_back",
    )(*args)


class Line:
    def __init__(self, plane, ns, part, inward, swap, res, sems, base, turned):
        self.plane, self.ns, self.turned = plane, ns, turned
        self.part, self.inward, self.swap, self.res = part, inward, swap, res
        self.sems, self.base = sems, base
        self.me = lax.axis_index("seq")
        self.side = self.me // (ns // 2)
        middle = ns // 2 - 1
        self.depth = (1 - self.side) * (middle - self.me) + self.side * (self.me - middle - 1)
        self.ends = middle
        self.in_to = self.me + 1 - 2 * self.side
        self.out_to = self.me - 1 + 2 * self.side
        self.other = ns - 1 - self.me
        self.count = part.shape[0]

    @staticmethod
    def slots(nf, turned):
        return 5 + (nf - 1 if turned else 0)

    def sem(self, chunk, kind):
        return self.base + chunk * self.slots(self.plane.nf, self.turned) + kind

    def half(self, ref, chunk, side):
        rows = ref.shape[-2] // 2
        rows = pl.ds(pl.multiple_of(side * rows, rows), rows)
        return ref.at[chunk, :, rows, :]

    def inner(self, chunk, src):
        return send(
            src.at[chunk], self.inward.at[chunk], self.sems, self.sem(chunk, 0), "seq", self.in_to
        )

    def cross(self, chunk):
        return send(
            self.half(self.inward, chunk, 1 - self.side),
            self.swap.at[chunk],
            self.sems,
            self.sem(chunk, 1),
            "seq",
            self.other,
        )

    def result(self):
        return self.res if self.turned else self.part

    def back_cross(self, chunk):
        return send(
            self.half(self.result(), chunk, self.side),
            self.half(self.res, chunk, self.side),
            self.sems,
            self.sem(chunk, 2),
            "seq",
            self.other,
        )

    def outer(self, chunk, side, src):
        return send(
            self.half(src, chunk, side),
            self.half(self.res, chunk, side),
            self.sems,
            self.sem(chunk, 3) + side,
            "seq",
            self.out_to,
        )

    def spread(self, chunk, step):
        rows = self.part.shape[-2] // 2
        rows = pl.ds(pl.multiple_of(self.side * rows, rows), rows)
        target = wrap(self.plane.me + step, self.plane.nf)
        return send(
            self.part.at[chunk, target, rows, :],
            self.res.at[chunk, self.plane.me, rows, :],
            self.sems,
            self.sem(chunk, 4) + step,
            "fsdp",
            target,
        )

    def keep(self, chunk, sem):
        if self.turned:
            rows = self.part.shape[-2] // 2
            rows = pl.ds(pl.multiple_of(self.side * rows, rows), rows)
            me = self.plane.me
            src, dst = self.part.at[chunk, me, rows, :], self.res.at[chunk, me, rows, :]
        else:
            src = self.half(self.part, chunk, self.side)
            dst = self.half(self.res, chunk, self.side)
        return pltpu.make_async_copy(src, dst, sem.at[chunk])

    def begin(self, chunk):
        if self.ends:

            @pl.when(self.depth == self.ends)
            def _():
                self.inner(chunk, self.part).start()

    def relay(self, chunk, hop):
        @pl.when(self.depth == self.ends - hop)
        def _():
            self.inner(chunk, self.part).wait_recv()
            total = self.inward[chunk].astype(F32) + self.part[chunk].astype(F32)
            self.inward[chunk] = total.astype(BF)
            self.inner(chunk, self.inward).start()

    def meet(self, chunk):
        @pl.when(self.depth == 0)
        def _():
            self.inner(chunk, self.part).wait_recv()
            theirs = self.half(self.inward, chunk, 1 - self.side)
            mine = self.half(self.part, chunk, 1 - self.side)

            def step(i):
                rows = tile(i, 16)
                total = theirs[:, rows, :].astype(F32) + mine[:, rows, :].astype(F32)
                theirs[:, rows, :] = total.astype(BF)

            loop(theirs.shape[1] // 16, step)
            self.cross(chunk).start()

    def settle(self, chunk, sem):
        @pl.when(self.depth == 0)
        def _():
            self.cross(chunk).wait_recv()
            theirs = self.half(self.inward, chunk, self.side)
            mine = self.half(self.part, chunk, self.side)

            def step(i):
                rows = tile(i, 16)
                total = theirs[:, rows, :].astype(F32) + mine[:, rows, :].astype(F32)
                total += self.swap[chunk, :, rows, :].astype(F32)
                mine[:, rows, :] = total.astype(BF)

            loop(theirs.shape[1] // 16, step)
            self.keep(chunk, sem).start()
            if self.turned:
                for k in range(1, self.plane.nf):
                    self.spread(chunk, k).start()
            else:
                self.hand_out(chunk)

    def hand_out(self, chunk):
        self.back_cross(chunk).start()
        if self.ends:
            self.outer(chunk, self.side, self.result()).start()

    def spread_end(self, chunk, sem):
        @pl.when(self.depth == 0)
        def _():
            for k in range(1, self.plane.nf):
                self.spread(chunk, k).wait_recv()
            self.keep(chunk, sem).wait()
            self.hand_out(chunk)

    def pass_on(self, chunk):
        @pl.when(self.depth == 0)
        def _():
            self.back_from(chunk).wait_recv()
            if self.ends:
                self.outer(chunk, 1 - self.side, self.res).start()

    def back_from(self, chunk):
        return send(
            self.half(self.result(), chunk, 1 - self.side),
            self.half(self.res, chunk, 1 - self.side),
            self.sems,
            self.sem(chunk, 2),
            "seq",
            self.other,
        )

    def outward_hop(self, chunk, hop):
        @pl.when(self.depth == hop)
        def _():
            for side in range(2):
                self.outer(chunk, side, self.res).wait_recv()
                if hop < self.ends:
                    self.outer(chunk, side, self.res).start()

    def phases(self, sem):
        listed = [self.begin]
        listed += [partial(self.relay, hop=hop) for hop in range(1, self.ends)]
        listed += [self.meet, partial(self.settle, sem=sem)]
        if self.turned:
            listed += [partial(self.spread_end, sem=sem)]
        listed += [self.pass_on]
        listed += [partial(self.outward_hop, hop=hop) for hop in range(1, self.ends + 1)]
        return listed

    def drain(self, chunk, sem):
        @pl.when(self.depth == 0)
        def _():
            self.cross(chunk).wait_send()
            self.back_cross(chunk).wait_send()
            if self.turned:
                for k in range(1, self.plane.nf):
                    self.spread(chunk, k).wait_send()
            else:
                self.keep(chunk, sem).wait()

        if self.ends:

            @pl.when(self.depth < self.ends)
            def _():
                for side in range(2):
                    self.outer(chunk, side, self.res).wait_send()

            @pl.when(self.depth > 0)
            def _():
                self.inner(chunk, self.part).wait_send()


class Ticks:
    def __init__(self, jobs):
        self.jobs = jobs
        self.now = 0

    def tick(self, upto=None):
        upto = len(self.jobs) if upto is None else upto
        late = [
            (i, self.now - i)
            for i in range(len(self.jobs))
            if 0 <= self.now - i < len(self.jobs[i][0].phases(self.jobs[i][2]))
        ]
        for i, phase in late:
            line, chunk, sem = self.jobs[i]
            line.phases(sem)[phase](chunk)
        self.now += 1
        return bool(late)

    def finish(self):
        while self.tick():
            pass
        for line, chunk, sem in self.jobs:
            line.drain(chunk, sem)


def sum_kernel(nf, ns, counts, turned, *refs):
    kinds = len(counts)
    ins, sm_ref, outs = refs[:kinds], refs[kinds], refs[kinds + 1 : 2 * kinds + 1]
    sm_out = refs[2 * kinds + 1]
    scratch = refs[2 * kinds + 2 :]
    inward, swap = scratch[:kinds], scratch[kinds : 2 * kinds]
    send_sem, recv_sem, copy_sem = scratch[2 * kinds : 2 * kinds + 3]
    sm_in, sm_z, sm_sem, sm_rsem = scratch[2 * kinds + 3 :]
    plane = Plane(nf)
    greet(nf, ns)
    jobs, base, copies = [], 0, 0
    for k in range(kinds):
        line = Line(
            plane, ns, ins[k], inward[k], swap[k], outs[k], (send_sem, recv_sem), base, turned[k]
        )
        base += counts[k] * Line.slots(nf, turned[k])
        for chunk in range(counts[k]):
            jobs.append((line, chunk, copy_sem.at[pl.ds(copies, counts[k])]))
        copies += counts[k]
    ticks = Ticks(jobs)
    small = Small(plane, ns, sm_ref, sm_in, sm_z, sm_out, (sm_sem, sm_rsem))
    ticks.tick()
    small.start()
    ticks.tick()
    ticks.tick()
    small.across()
    ticks.tick()
    ticks.tick()
    small.finish()
    ticks.finish()
    small.drain()


class Small:
    def __init__(self, plane, ns, src, mid, line, out, sems):
        self.plane, self.ns, self.src, self.mid, self.line, self.out = plane, ns, src, mid, line, out
        self.sems = sems
        self.me = lax.axis_index("seq")

    def scatter(self, step):
        target = wrap(self.plane.me + step, self.plane.nf)
        return send(
            self.src.at[target], self.mid.at[self.plane.me], self.sems, step - 1, "fsdp", target
        )

    def along(self, step):
        me = self.line.at[self.me]
        slot = self.plane.nf - 1 + step - 1
        return send(me, me, self.sems, slot, "seq", wrap(self.me + step, self.ns))

    def spread(self, step):
        me = self.out.at[self.plane.me]
        slot = self.plane.nf - 1 + self.ns - 1 + step - 1
        return send(me, me, self.sems, slot, "fsdp", wrap(self.plane.me + step, self.plane.nf))

    def start(self):
        self.mid[self.plane.me] = self.src[self.plane.me]
        for step in range(1, self.plane.nf):
            self.scatter(step).start()

    def across(self):
        for step in range(1, self.plane.nf):
            self.scatter(step).wait_recv()
        total = self.mid[0]
        for k in range(1, self.plane.nf):
            total += self.mid[k]
        self.line[self.me] = total
        for step in range(1, self.ns):
            self.along(step).start()

    def finish(self):
        for step in range(1, self.ns):
            self.along(step).wait_recv()
        total = self.line[0]
        for k in range(1, self.ns):
            total += self.line[k]
        self.out[self.plane.me] = total
        for step in range(1, self.plane.nf):
            self.spread(step).start()

    def drain(self):
        for step in range(1, self.plane.nf):
            self.spread(step).wait_recv()
        for step in range(1, self.plane.nf):
            self.scatter(step).wait_send()
            self.spread(step).wait_send()
        for step in range(1, self.ns):
            self.along(step).wait_send()


def run_sums(nf, ns, parts, turned, small):
    counts = [p.shape[0] for p in parts]
    total = sum(n * Line.slots(nf, t) for n, t in zip(counts, turned))
    kinds = len(parts)
    few = 2 * (nf - 1) + ns - 1
    halves = [(p.shape[0], p.shape[1], p.shape[2] // 2, p.shape[3]) for p in parts]
    cols = D // nf
    split = small.reshape(SMALL, nf, cols).transpose(1, 0, 2)
    outs = pl.pallas_call(
        partial(sum_kernel, nf, ns, counts, turned),
        out_shape=tuple(shape(p.shape) for p in parts) + (shape((nf, SMALL, cols), F32),),
        in_specs=[vmem()] * (kinds + 1),
        out_specs=(hbm(),) * kinds + (vmem(),),
        scratch_shapes=[pltpu.VMEM(p.shape, BF) for p in parts]
        + [pltpu.VMEM(h, BF) for h in halves]
        + [pltpu.SemaphoreType.DMA((total,))] * 2
        + [pltpu.SemaphoreType.DMA((sum(counts),))]
        + [
            pltpu.VMEM((nf, SMALL, cols), F32),
            pltpu.VMEM((ns, SMALL, cols), F32),
            pltpu.SemaphoreType.DMA((few,)),
            pltpu.SemaphoreType.DMA((few,)),
        ],
        compiler_params=params(4),
        name="sums",
    )(*parts, split)
    return outs[:-1], outs[-1].transpose(1, 0, 2).reshape(SMALL, D)


def natural_chunks(grad):
    return grad.reshape(grad.shape[0] // 128, 1, 128, grad.shape[1])


def turned_chunks(nf, grad):
    rows, cols = grad.shape
    return grad.reshape(nf, rows // nf, cols // 128, 128).transpose(2, 0, 1, 3)


def turned_rows(parts):
    chunks, nf, rows, cols = parts.shape
    return parts.transpose(2, 1, 0, 3).reshape(rows, nf * chunks * cols)


def local(
    nf,
    ns,
    history,
    cotangent,
    seq_lengths,
    wq,
    wk,
    wv,
    wo,
    w_in,
    w_out,
    mix_in,
    mix_out,
    attn_gain,
    mlp_gain,
    mix_gain,
):
    hist = history[:, 0]
    tok_rows = hist.shape[1]
    lens = lax.all_gather(seq_lengths, "fsdp", axis=0, tiled=True)
    slab_index = lax.axis_index("seq") * tok_rows + jnp.arange(tok_rows, dtype=jnp.int32)
    every_index = jnp.tile(slab_index, nf)
    _, place = token_marks(every_index, jnp.repeat(lens, tok_rows, axis=0))
    planes = rope_planes(place)
    gains = [g[None] for g in (attn_gain, mlp_gain, mix_gain)]
    low, stream, coef, inv, pre, act, mixed = run_start(hist, mix_in, mix_out, *gains)
    grad_out = cotangent[0]
    ws = [w.astype(BF) for w in (wq, wk, wv)]
    wo_low, win_low, wout_low = wo.astype(BF), w_in.astype(BF), w_out.astype(BF)

    gg, hidden, dwin, dwout, dx_r = run_mlp(nf, low[3], grad_out, win_low, wout_low)
    *xgs, wfull, att, dq, dk, dv = run_attend(
        nf, ns, [low[c] for c in range(3)], ws, wo_low, planes, gg, lens
    )
    y_sum, dx, dw, dwo = run_return(
        nf, att, (dq, dk, dv), wfull, wo_low, wout_low, hidden, gg, xgs
    )
    history_grad, layer_out, small = run_end(
        hist, stream, dx, dx_r, grad_out, y_sum, coef, inv, pre, act, mixed, mix_in, mix_out, *gains
    )
    parts = [natural_chunks(dwout), turned_chunks(nf, dwin)]
    parts += [turned_chunks(nf, dw[i]) for i in range(3)] + [natural_chunks(dwo)]
    sums, small = run_sums(nf, ns, parts, (False, True, True, True, True, False), small)
    dwout = sums[0].reshape(w_out.shape).astype(F32)
    dwo = sums[5].reshape(wo.shape).astype(F32)
    dw_in = turned_rows(sums[1]).astype(F32)
    dw_qkv = [turned_rows(sums[2 + i]).astype(F32) for i in range(3)]
    units = mix_in.shape[1]
    mix_out_rows = small[units + 3 :, : STREAMS * 128].reshape(HIST * STREAMS, 128)
    return (
        layer_out[None],
        history_grad[:, None],
        *dw_qkv,
        dwo,
        dw_in,
        dwout,
        small[:units].T,
        mix_out_rows[:, :units].T,
        small[units],
        small[units + 1],
        small[units + 2],
    )


def solution(mesh):
    rows, rep = P("fsdp", None), P()
    in_specs = (
        P(None, "fsdp", "seq", None),
        P("fsdp", "seq", None),
    ) + (rows,) * 7 + (rep,) * 5
    out_specs = (
        P("fsdp", "seq", None),
        P(None, "fsdp", "seq", None),
    ) + (rows,) * 6 + (rep,) * 5
    body = partial(local, mesh.shape["fsdp"], mesh.shape["seq"])
    return jax.shard_map(body, mesh=mesh, in_specs=in_specs, out_specs=out_specs, check_vma=False)
```

```python
from functools import partial

import jax
import jax.numpy as jnp
from jax import lax
from jax.experimental import pallas as pl
from jax.experimental.pallas import tpu as pltpu
from jax.sharding import PartitionSpec as P

D = 2048
HEADS = 16
HEAD = 128
ROT = 32
HIST = 9
STREAMS = 4
EPSILON = 1e-05
NEGATIVE = -1e30
MESH = pl.DeviceIdType.MESH
BF = jnp.bfloat16
F32 = jnp.float32
MIB = 2**20


CHUNKS = 4
LANES = 128
SLOTS = 4
EARLY = 3


def token_marks(tok_index, lengths):
    first_end = lengths[..., 0]
    second_end = first_end + lengths[..., 1]
    segment = (tok_index >= first_end).astype(jnp.int32) + (tok_index >= second_end).astype(
        jnp.int32
    )
    seq_begin = jnp.where(segment == 0, 0, jnp.where(segment == 1, first_end, second_end))
    return (segment, tok_index - seq_begin)


def rope_planes(tok_place):
    inverse = 10000.0 ** (-jnp.arange(0, ROT, 2, dtype=F32) / ROT)
    angles = tok_place.astype(F32)[:, None] * inverse[None, :]
    cosine, sine = jnp.cos(angles), jnp.sin(angles)
    rows = tok_place.shape[0]
    ones = jnp.ones((rows, HEAD - ROT), F32)
    none = jnp.zeros((rows, HEAD - ROT // 2), F32)
    gap = jnp.zeros((rows, ROT // 2), F32)
    return jnp.stack(
        [
            jnp.concatenate([cosine, cosine, ones], axis=1),
            jnp.concatenate([-sine, none], axis=1),
            jnp.concatenate([gap, sine, none[:, : HEAD - ROT]], axis=1),
        ]
    )


def dot(left_op, right_op, left_dim=1, right_dim=0):
    return lax.dot_general(
        left_op, right_op, (((left_dim,), (right_dim,)), ((), ())), preferred_element_type=F32
    )


def wrap(value, extent):
    return lax.rem(value + extent, extent)


def tile(index, extent):
    return pl.ds(pl.multiple_of(index * extent, extent), extent)


class Plane:
    def __init__(self, nf):
        self.nf = nf
        self.chips = nf // 2
        self.me = lax.axis_index("fsdp")
        self.chip = self.me // 2
        self.core = lax.rem(self.me, 2)

    def on(self, step, other=0):
        core = 1 - self.core if other else self.core
        return wrap(self.chip + step, self.chips) * 2 + core


def greet(nf, ns=1):
    barrier = pltpu.get_barrier_semaphore()
    for axis, extent in (("fsdp", nf), ("seq", ns)):
        for step in range(1, extent):
            pl.semaphore_signal(
                barrier,
                inc=1,
                device_id={axis: wrap(lax.axis_index(axis) + step, extent)},
                device_id_type=MESH,
            )
    pl.semaphore_wait(barrier, nf - 1 + ns - 1)


def send(src, dst, sems, slot, axis, target):
    return pltpu.make_async_remote_copy(
        src_ref=src,
        dst_ref=dst,
        send_sem=sems[0].at[slot],
        recv_sem=sems[1].at[slot],
        device_id={axis: target},
        device_id_type=MESH,
    )


class Gather:
    def __init__(self, plane, own, buf, sems, base):
        self.plane, self.own, self.buf, self.sems, self.base = plane, own, buf, sems, base

    def direct(self, step, slot=None):
        dst = self.buf.at[self.plane.me if slot is None else slot]
        src = self.own if slot is None else dst
        return send(src, dst, self.sems, self.base + step - 1, "fsdp", self.plane.on(step))

    def across(self, step, slot=None):
        slot = self.plane.on(-step) if slot is None else slot
        block = self.buf.at[slot]
        src = block if step else self.own
        base = self.base + self.plane.chips - 1
        return send(src, block, self.sems, base + step, "fsdp", self.plane.on(0, 1))

    def start(self):
        for step in range(1, self.plane.chips):
            self.direct(step).start()
        self.across(0).start()

    def keep(self, sem):
        return pltpu.make_async_copy(self.own, self.buf.at[self.plane.me], sem)

    def forward(self):
        for step in range(1, self.plane.chips):
            self.direct(step, self.plane.on(-step)).wait_recv()
            self.across(step).start()

    def finish(self):
        for step in range(self.plane.chips):
            self.across(step, self.plane.on(-step, 1)).wait_recv()

    def drain(self):
        for step in range(1, self.plane.chips):
            self.direct(step).wait_send()
        for step in range(self.plane.chips):
            self.across(step).wait_send()


class Turn:
    def __init__(self, plane, rows_ref, full_ref, sems, base, chunks):
        self.plane, self.sems, self.base, self.chunks = plane, sems, base, chunks
        self.rows_ref, self.full_ref = rows_ref, full_ref
        self.height = rows_ref.shape[0]
        self.width = full_ref.shape[1]
        self.part = self.width // chunks

    def copy(self, chunk, step, source=None):
        nf = self.plane.nf
        target = wrap(self.plane.me + step, nf)
        source = self.plane.me if source is None else source
        begin = pl.multiple_of(target * self.width + chunk * self.part, self.part)
        return send(
            self.rows_ref.at[:, pl.ds(begin, self.part)],
            self.full_ref.at[tile(source, self.height), tile(chunk, self.part)],
            self.sems,
            self.base + chunk * (nf - 1) + step - 1,
            "fsdp",
            target,
        )

    def start(self, chunk):
        for step in range(1, self.plane.nf):
            self.copy(chunk, step).start()

    def keep(self, sem):
        return pltpu.make_async_copy(
            self.rows_ref.at[:, tile(self.plane.me, self.width)],
            self.full_ref.at[tile(self.plane.me, self.height), :],
            sem,
        )

    def arrive(self, chunk):
        for step in range(1, self.plane.nf):
            self.copy(chunk, step, wrap(self.plane.me - step, self.plane.nf)).wait_recv()

    def drain(self, chunk):
        for step in range(1, self.plane.nf):
            self.copy(chunk, step).wait_send()


class Scatter:
    def __init__(self, plane, part, sib, rec, sems, base, chunks):
        self.plane, self.part, self.sib, self.rec = plane, part, sib, rec
        self.sems, self.base, self.chunks = sems, base, chunks
        self.width = part.shape[-1] // chunks

    def across(self, chunk, step):
        cols = tile(chunk, self.width)
        return send(
            self.part.at[self.plane.on(step, 1), :, cols],
            self.sib.at[wrap(self.plane.chip + step, self.plane.chips), :, cols],
            self.sems,
            self.base + chunk * (self.plane.nf - 1) + step,
            "fsdp",
            self.plane.on(0, 1),
        )

    def direct(self, chunk, step):
        cols = tile(chunk, self.width)
        return send(
            self.part.at[self.plane.on(step), :, cols],
            self.rec.at[step - 1, :, cols],
            self.sems,
            self.base + chunk * (self.plane.nf - 1) + self.plane.chips + step - 1,
            "fsdp",
            self.plane.on(step),
        )

    def start(self, chunk):
        for step in range(self.plane.chips):
            self.across(chunk, step).start()

    def combine(self, chunk):
        cols = tile(chunk, self.width)
        for step in range(1, self.plane.chips):
            chip = wrap(self.plane.chip + step, self.plane.chips)
            mine = self.plane.on(step)
            self.across(chunk, step).wait_recv()
            total = self.part[mine, :, cols].astype(F32) + self.sib[chip, :, cols].astype(F32)
            self.part[mine, :, cols] = total.astype(BF)
            self.direct(chunk, step).start()
        self.across(chunk, 0).wait_recv()

    def total(self, chunk):
        cols = tile(chunk, self.width)
        total = self.part[self.plane.me, :, cols].astype(F32)
        total += self.sib[self.plane.chip, :, cols].astype(F32)
        for step in range(1, self.plane.chips):
            self.direct(chunk, step).wait_recv()
            total += self.rec[step - 1, :, cols].astype(F32)
        return total

    def drain(self, chunk):
        for step in range(self.plane.chips):
            self.across(chunk, step).wait_send()
        for step in range(1, self.plane.chips):
            self.direct(chunk, step).wait_send()


def loop(extent, body):
    lax.fori_loop(0, extent, lambda i, c: (body(i), c)[1], 0)


def rows_of(ref3, begin, count):
    value = ref3[pl.ds(begin, count)]
    return value.reshape(count * value.shape[1], value.shape[2])


def vmem():
    return pl.BlockSpec(memory_space=pltpu.VMEM)


def hbm():
    return pl.BlockSpec(memory_space=pltpu.HBM)


def shape(dims, dtype=BF):
    return jax.ShapeDtypeStruct(tuple(dims), dtype)


def params(ident, limit=62):
    return pltpu.CompilerParams(
        collective_id=ident, has_side_effects=True, vmem_limit_bytes=limit * MIB
    )


ROWS = 16
WIDTH = 512


def start_kernel(
    hist_ref,
    mix_in_ref,
    mix_out_ref,
    again_ref,
    mgain_ref,
    xgain_ref,
    low_ref,
    st_ref,
    coef_ref,
    inv_ref,
    pre_ref,
    act_ref,
    mixed_ref,
):
    tok = hist_ref.shape[1]

    def mix_step(i):
        rows = tile(i, ROWS)
        value = hist_ref[HIST - 1, rows, :].astype(F32)
        inv = lax.rsqrt(jnp.mean(value * value, axis=1, keepdims=True) + EPSILON)
        mixed_ref[rows, :] = (value * inv * xgain_ref[...]).astype(BF)
        inv_ref[STREAMS, rows, :] = inv

    loop(tok // ROWS, mix_step)
    pre = dot(mixed_ref[...], mix_in_ref[...].astype(BF))
    pre_ref[...] = pre
    act = (0.5 * pre * (1.0 + lax.erf(pre * (0.5**0.5)))).astype(BF)
    act_ref[...] = act
    coef_ref[...] = dot(act, mix_out_ref[...].astype(BF))

    def stream_step(i):
        rows = tile(i, ROWS)
        coef = coef_ref[rows, :]
        squares = [jnp.zeros((ROWS, 1), F32)] * STREAMS
        for begin in range(0, D, WIDTH):
            cols = slice(begin, begin + WIDTH)
            total = [jnp.zeros((ROWS, WIDTH), F32)] * STREAMS
            for j in range(HIST):
                entry = hist_ref[j, rows, cols].astype(F32)
                for c in range(STREAMS):
                    at = c * HIST + j
                    total[c] = total[c] + coef[:, at : at + 1] * entry
            for c in range(STREAMS):
                st_ref[c, rows, cols] = total[c]
                squares[c] = squares[c] + jnp.sum(total[c] * total[c], axis=1, keepdims=True)
        for c in range(STREAMS):
            inv = lax.rsqrt(squares[c] / D + EPSILON)
            inv_ref[c, rows, :] = inv
            gain = mgain_ref if c == STREAMS - 1 else again_ref
            low_ref[c, rows, :] = (st_ref[c, rows, :] * inv * gain[...]).astype(BF)

    loop(tok // ROWS, stream_step)


def run_start(hist, mix_in, mix_out, again, mgain, xgain):
    tok = hist.shape[1]
    hidden = mix_in.shape[1]
    return pl.pallas_call(
        start_kernel,
        out_shape=(
            shape((STREAMS, tok, D)),
            shape((STREAMS, tok, D), F32),
            shape((tok, STREAMS * HIST), F32),
            shape((STREAMS + 1, tok, 1), F32),
            shape((tok, hidden), F32),
            shape((tok, hidden)),
            shape((tok, D)),
        ),
        in_specs=[vmem()] * 6,
        out_specs=(vmem(),) * 7,
        compiler_params=pltpu.CompilerParams(vmem_limit_bytes=62 * MIB),
        name="streams",
    )(hist, mix_in, mix_out, again, mgain, xgain)


def rotated(value, planes):
    return value * planes[0] + pltpu.roll(value, HEAD - ROT // 2, 1) * planes[1] + pltpu.roll(
        value, ROT // 2, 1
    ) * planes[2]


def rotated_back(value, planes):
    return value * planes[0] - pltpu.roll(value, HEAD - ROT // 2, 1) * planes[1] - pltpu.roll(
        value, ROT // 2, 1
    ) * planes[2]


class Exchange:
    def __init__(self, ns, sems, base):
        self.ns, self.sems, self.base = ns, sems, base
        self.me = lax.axis_index("seq")

    def copy(self, src, dst, lane, step):
        return send(
            src,
            dst,
            self.sems,
            self.base + lane * (self.ns - 1) + step - 1,
            "seq",
            wrap(self.me + step, self.ns),
        )


class Line:
    def __init__(self, plane, ns, part, inward, swap, res, sems, base, turned, copy_sem, credits):
        self.plane, self.ns, self.turned = plane, ns, turned
        self.part, self.inward, self.swap, self.res = part, inward, swap, res
        self.sems, self.base, self.copy_sem, self.credits = sems, base, copy_sem, credits
        self.me = lax.axis_index("seq")
        self.side = self.me // (ns // 2)
        middle = ns // 2 - 1
        self.depth = (1 - self.side) * (middle - self.me) + self.side * (self.me - middle - 1)
        self.ends = middle
        self.in_to = self.me + 1 - 2 * self.side
        self.out_to = self.me - 1 + 2 * self.side
        self.other = ns - 1 - self.me
        self.count = res.shape[0]
        self.slots = inward.shape[0]
        if self.ends != 1 and self.slots < self.count:
            raise ValueError("slots")

    @staticmethod
    def marks(nf, turned):
        return 5 + (nf - 1 if turned else 0)

    def sem(self, chunk, kind):
        return self.base + chunk * self.marks(self.plane.nf, self.turned) + kind

    def half(self, ref, chunk, side):
        rows = ref.shape[-2] // 2
        rows = pl.ds(pl.multiple_of(side * rows, rows), rows)
        return ref.at[chunk, :, rows, :]

    def inner(self, chunk, relayed=False):
        slot = chunk % self.slots
        src = self.inward.at[slot] if relayed else self.part.at[chunk]
        return send(src, self.inward.at[slot], self.sems, self.sem(chunk, 0), "seq", self.in_to)

    def cross(self, chunk):
        slot = chunk % self.slots
        return send(
            self.half(self.inward, slot, 1 - self.side),
            self.swap.at[slot],
            self.sems,
            self.sem(chunk, 1),
            "seq",
            self.other,
        )

    def result(self):
        return self.res if self.turned else self.part

    def back_cross(self, chunk, side=None):
        side = self.side if side is None else side
        return send(
            self.half(self.result(), chunk, side),
            self.half(self.res, chunk, side),
            self.sems,
            self.sem(chunk, 2),
            "seq",
            self.other,
        )

    def outer(self, chunk, side, src):
        return send(
            self.half(src, chunk, side),
            self.half(self.res, chunk, side),
            self.sems,
            self.sem(chunk, 3) + side,
            "seq",
            self.out_to,
        )

    def spread(self, chunk, step, source=None):
        rows = self.part.shape[-2] // 2
        rows = pl.ds(pl.multiple_of(self.side * rows, rows), rows)
        target = wrap(self.plane.me + step, self.plane.nf)
        source = self.plane.me if source is None else source
        return send(
            self.part.at[chunk, target, rows, :],
            self.res.at[chunk, source, rows, :],
            self.sems,
            self.sem(chunk, 4) + step,
            "fsdp",
            target,
        )

    def keep(self, chunk):
        if self.turned:
            rows = self.part.shape[-2] // 2
            rows = pl.ds(pl.multiple_of(self.side * rows, rows), rows)
            me = self.plane.me
            src, dst = self.part.at[chunk, me, rows, :], self.res.at[chunk, me, rows, :]
        else:
            src = self.half(self.part, chunk, self.side)
            dst = self.half(self.res, chunk, self.side)
        return pltpu.make_async_copy(src, dst, self.copy_sem.at[chunk])

    def begin(self, chunk):
        if self.ends:

            @pl.when(self.depth == self.ends)
            def _():
                if chunk >= self.slots:
                    pl.semaphore_wait(self.credits.at[0], 1)
                self.inner(chunk).start()

    def relay(self, chunk, hop):
        slot = chunk % self.slots

        @pl.when(self.depth == self.ends - hop)
        def _():
            self.inner(chunk).wait_recv()
            total = self.inward[slot].astype(F32) + self.part[chunk].astype(F32)
            self.inward[slot] = total.astype(BF)
            self.inner(chunk, True).start()

    def meet(self, chunk):
        slot = chunk % self.slots

        @pl.when(self.depth == 0)
        def _():
            self.inner(chunk).wait_recv()
            theirs = self.half(self.inward, slot, 1 - self.side)
            mine = self.half(self.part, chunk, 1 - self.side)

            def step(i):
                rows = tile(i, 16)
                total = theirs[:, rows, :].astype(F32) + mine[:, rows, :].astype(F32)
                theirs[:, rows, :] = total.astype(BF)

            loop(theirs.shape[1] // 16, step)
            if chunk >= self.slots:
                pl.semaphore_wait(self.credits.at[1], 1)
            self.cross(chunk).start()

    def settle(self, chunk):
        slot = chunk % self.slots

        @pl.when(self.depth == 0)
        def _():
            self.cross(chunk).wait_recv()
            theirs = self.half(self.inward, slot, self.side)
            mine = self.half(self.part, chunk, self.side)

            def step(i):
                rows = tile(i, 16)
                total = theirs[:, rows, :].astype(F32) + mine[:, rows, :].astype(F32)
                total += self.swap[slot, :, rows, :].astype(F32)
                mine[:, rows, :] = total.astype(BF)

            loop(theirs.shape[1] // 16, step)
            self.keep(chunk).start()
            if self.turned:
                for k in range(1, self.plane.nf):
                    self.spread(chunk, k).start()
            else:
                self.hand_out(chunk)
            self.cross(chunk).wait_send()
            if chunk + self.slots < self.count:
                pl.semaphore_signal(
                    self.credits.at[0], inc=1, device_id={"seq": self.out_to}, device_id_type=MESH
                )
                pl.semaphore_signal(
                    self.credits.at[1], inc=1, device_id={"seq": self.other}, device_id_type=MESH
                )

    def hand_out(self, chunk):
        self.back_cross(chunk).start()
        if self.ends:
            self.outer(chunk, self.side, self.result()).start()

    def spread_end(self, chunk):
        @pl.when(self.depth == 0)
        def _():
            for k in range(1, self.plane.nf):
                self.spread(chunk, k, wrap(self.plane.me - k, self.plane.nf)).wait_recv()
            self.keep(chunk).wait()
            self.hand_out(chunk)

    def pass_on(self, chunk):
        @pl.when(self.depth == 0)
        def _():
            self.back_cross(chunk, 1 - self.side).wait_recv()
            if self.ends:
                self.outer(chunk, 1 - self.side, self.res).start()

    def outward_hop(self, chunk, hop):
        @pl.when(self.depth == hop)
        def _():
            for side in range(2):
                self.outer(chunk, side, self.res).wait_recv()
                self.outer(chunk, side, self.res).start()

    def pause(self, chunk):
        pass

    def phases(self):
        listed = [self.begin, self.pause]
        listed += [partial(self.relay, hop=hop) for hop in range(1, self.ends)]
        listed += [self.meet, self.settle]
        if self.turned:
            listed += [self.spread_end]
        listed += [self.pass_on]
        listed += [partial(self.outward_hop, hop=hop) for hop in range(1, self.ends)]
        return listed

    def drain(self, chunk):
        @pl.when(self.depth == 0)
        def _():
            self.back_cross(chunk).wait_send()
            if self.turned:
                for k in range(1, self.plane.nf):
                    self.spread(chunk, k).wait_send()
            else:
                self.keep(chunk).wait()

        if self.ends:

            @pl.when(self.depth == self.ends)
            def _():
                for side in range(2):
                    self.outer(chunk, side, self.res).wait_recv()

            @pl.when(self.depth < self.ends)
            def _():
                for side in range(2):
                    self.outer(chunk, side, self.res).wait_send()

            @pl.when(self.depth > 0)
            def _():
                self.inner(chunk).wait_send()


class Ticks:
    def __init__(self, jobs):
        self.jobs = jobs
        self.now = 0

    def tick(self, times=1):
        for _ in range(times):
            if self.now < len(self.jobs):
                line, chunk = self.jobs[self.now]
                line.begin(chunk)
            for i, (line, chunk) in enumerate(self.jobs):
                phase = self.now - i
                if 0 < phase < len(line.phases()):
                    line.phases()[phase](chunk)
            self.now += 1

    def finish(self):
        depth = max(len(line.phases()) for line, _ in self.jobs)
        while self.now < len(self.jobs) + depth:
            self.tick()
        for line, chunk in self.jobs:
            line.drain(chunk)


class Lines:
    def __init__(self, nf, kinds):
        self.nf, self.kinds = nf, kinds

    def scratch(self):
        listed = []
        for (blocks, rows, cols), count, _ in self.kinds:
            slots = min(count, SLOTS)
            listed.append(pltpu.VMEM((slots, blocks, rows, cols), BF))
            listed.append(pltpu.VMEM((slots, blocks, rows // 2, cols), BF))
            listed.append(pltpu.SemaphoreType.DMA((count,)))
            listed.append(pltpu.SemaphoreType.REGULAR((2,)))
        marks = sum(count * Line.marks(self.nf, turned) for _, count, turned in self.kinds)
        return listed + [pltpu.SemaphoreType.DMA((marks,))] * 2

    def count(self):
        return 4 * len(self.kinds) + 2

    def outs(self):
        return [shape((count,) + dims) for dims, count, _ in self.kinds]

    def build(self, plane, ns, parts, results, scratch):
        lines, base = [], 0
        sems = tuple(scratch[-2:])
        for k, (_, count, turned) in enumerate(self.kinds):
            inward, swap, copy_sem, credits = scratch[4 * k : 4 * k + 4]
            lines.append(
                Line(
                    plane,
                    ns,
                    parts[k],
                    inward,
                    swap,
                    results[k],
                    sems,
                    base,
                    turned,
                    copy_sem,
                    credits,
                )
            )
            base += count * Line.marks(self.nf, turned)
        return lines


def forward_lines(nf, wide, hidden):
    count = EARLY * (hidden // CHUNKS // LANES)
    return Lines(nf, [((1, LANES, D), count, False), ((nf, D // nf, LANES), count, True)])


def forward_kernel(nf, ns, lines, *refs):
    (low, g_ref, win_ref, wout_ref, wq_ref, wk_ref, wv_ref, wo_ref, planes_ref, lens_ref) = refs[:10]
    refs = refs[10:]
    (xq_out, xk_out, xv_out, gg_out, win_out, h_out, dup_out, w_out, rest_out, rest_in) = refs[:10]
    refs = refs[10:]
    sum_out, sum_in, att_ref, dq_ref, dk_ref, dv_ref = refs[:6]
    refs = refs[6:]
    (xr, gg, wfull, hid, dup, p_out, p_in, stage, wqkv, qkva, zin, zout, zback, dkv) = refs[:14]
    send_sem, recv_sem, copy_sem = refs[14:17]
    line_refs = refs[17:]
    plane = Plane(nf)
    sems = (send_sem, recv_sem)
    tok = g_ref.shape[0]
    wide = wo_ref.shape[0]
    heads = wide // HEAD
    per = nf // ns
    slab = per * tok
    group_tok = ns * tok
    sq = lax.axis_index("seq")
    width = wfull.shape[1] // CHUNKS
    blocks = min(4, nf)
    pieces = width // LANES
    step_sems = nf - 1
    greet(nf, ns)
    l_out, l_in = lines.build(plane, ns, (p_out, p_in), (sum_out, sum_in), line_refs)
    jobs = []
    for n in range(EARLY):
        jobs += [(l_out, n * pieces + k) for k in range(pieces)]
        jobs += [(l_in, n * pieces + k) for k in range(pieces)]
    ticks = Ticks(jobs)
    ag_r = Gather(plane, low.at[3], xr, sems, 0)
    ag_g = Gather(plane, g_ref, gg, sems, step_sems)
    ag_x = [
        Gather(plane, low.at[i], out, sems, (2 + i) * step_sems)
        for i, out in enumerate((xq_out, xk_out, xv_out))
    ]
    turn = Turn(plane, win_ref, wfull, sems, 5 * step_sems, CHUNKS)
    turns = [
        Turn(plane, w, wqkv.at[i], sems, (5 + CHUNKS + i) * step_sems, 1)
        for i, w in enumerate((wq_ref, wk_ref, wv_ref))
    ]
    base = (8 + CHUNKS) * step_sems
    there = Exchange(ns, sems, base)
    home = Exchange(ns, sems, base + 4 * (ns - 1))
    ag_r.start()
    turn.start(0)
    ag_g.start()
    for chunk in range(1, CHUNKS):
        turn.start(chunk)
    for i in range(3):
        ag_x[i].start()
        turns[i].start(0)
    keeps = [ag_r.keep(copy_sem.at[0]), ag_g.keep(copy_sem.at[1]), turn.keep(copy_sem.at[2])]
    keeps += [ag_x[i].keep(copy_sem.at[3 + i]) for i in range(3)]
    keeps += [turns[i].keep(copy_sem.at[6 + i]) for i in range(3)]
    for keep in keeps:
        keep.start()
    ag_r.forward()
    ag_g.forward()
    ag_r.finish()
    ag_g.finish()
    for keep in keeps:
        keep.wait()
    saves = []

    def save(src, dst):
        saves.append(pltpu.make_async_copy(src, dst, copy_sem.at[9 + len(saves)]))
        saves[-1].start()

    save(gg, gg_out)

    for chunk in range(CHUNKS):
        turn.arrive(chunk)
        cols = slice(chunk * width, chunk * width + width)

        def rows_step(i, cols=cols):
            rows = tile(i, blocks * tok)
            up = dot(rows_of(xr, i * blocks, blocks), wfull[:, cols])
            dh = dot(rows_of(gg, i * blocks, blocks), wout_ref[cols, :], 1, 1)
            cdf = 0.5 * (1.0 + lax.erf(up * (0.5**0.5)))
            slope = cdf + up * jnp.exp(-0.5 * up * up) * 0.3989422804014327
            hid[rows, cols] = (up * cdf).astype(BF)
            dup[rows, cols] = (dh * slope).astype(BF)

        loop(nf // blocks, rows_step)

        def grad_step(i, cols=cols, chunk=chunk):
            feats = tile(i, WIDTH)
            every = gg[:, :, feats].reshape(nf * tok, WIDTH)
            grad = dot(hid[:, cols], every, 0, 0).astype(BF)
            for k in range(pieces):
                p_out[chunk * pieces + k, 0, :, feats] = grad[k * LANES : k * LANES + LANES]
            every = xr[:, :, feats].reshape(nf * tok, WIDTH)
            grad = dot(every, dup[:, cols], 0, 0).astype(BF)
            count = WIDTH * nf // D
            for k in range(pieces):
                piece = grad[:, k * LANES : k * LANES + LANES].reshape(count, D // nf, LANES)
                p_in[chunk * pieces + k, pl.ds(i * count, count)] = piece

        loop(D // WIDTH, grad_step)
        ticks.tick()

    early = EARLY * pieces
    save(wfull, win_out)
    save(hid, h_out)
    save(dup, dup_out)
    save(p_out.at[pl.ds(early, CHUNKS * pieces - early)], rest_out)
    save(p_in.at[pl.ds(early, CHUNKS * pieces - early)], rest_in)

    def ship(i):
        for step in range(1, ns):
            target = wrap(sq + step, ns)
            there.copy(qkva.at[i, tile(target, slab), :], zin.at[i, sq], i, step).start()
        zin[i, sq] = qkva[i, tile(sq, slab), :]

    def da_step(i):
        rows = tile(i, blocks * tok)
        qkva[3, rows, :] = dot(rows_of(gg, i * blocks, blocks), wo_ref[...], 1, 1).astype(BF)

    loop(nf // blocks, da_step)
    ship(3)
    ticks.tick()
    for i in range(3):
        ag_x[i].forward()
        turns[i].arrive(0)
        ag_x[i].finish()
        load = pltpu.make_async_copy(ag_x[i].buf, stage, copy_sem.at[15])
        load.start()
        load.wait()

        def lin_step(r, i=i):
            rows = tile(r, blocks * tok)
            lin = dot(rows_of(stage, r * blocks, blocks), wqkv[i])
            for head in range(heads):
                cols = slice(head * HEAD, head * HEAD + HEAD)
                piece = lin[:, cols]
                if i < 2:
                    piece = rotated(piece, [planes_ref[k, rows, :] for k in range(3)])
                qkva[i, rows, cols] = piece.astype(BF)

        loop(nf // blocks, lin_step)
        ship(i)
        ticks.tick(2 if i < 2 else 1)
    save(wqkv, w_out)
    for i in range(4):
        for step in range(1, ns):
            there.copy(zin.at[i, 0], zin.at[i, wrap(sq - step, ns)], i, step).wait_recv()

    scale = HEAD ** (-0.5)
    queries = min(256, group_tok)
    q_slabs = queries // tok

    def pair_step(pair):
        grp = pair // heads
        head = lax.rem(pair, heads)
        cols = tile(head, HEAD)
        toks = tile(grp, tok)
        first_end = lens_ref[sq * per + grp, 0]
        second_end = first_end + lens_ref[sq * per + grp, 1]

        def part_of(i, begin, count):
            return zin[i, pl.ds(begin, count), toks, cols].reshape(count * tok, HEAD)

        keys, values = part_of(1, 0, ns), part_of(2, 0, ns)
        dkv[...] = jnp.zeros_like(dkv)

        def query_step(j):
            begin = j * q_slabs
            query, d_att = part_of(0, begin, q_slabs), part_of(3, begin, q_slabs)
            qi = j * queries + lax.broadcasted_iota(jnp.int32, (queries, group_tok), 0)
            ki = lax.broadcasted_iota(jnp.int32, (queries, group_tok), 1)
            seg_q = (qi >= first_end).astype(jnp.int32) + (qi >= second_end).astype(jnp.int32)
            seg_k = (ki >= first_end).astype(jnp.int32) + (ki >= second_end).astype(jnp.int32)
            allowed = (seg_q == seg_k) & (qi >= ki)
            scores = jnp.where(allowed, dot(query, keys, 1, 1) * scale, NEGATIVE)
            top = jnp.max(scores, axis=1, keepdims=True)
            expo = jnp.where(allowed, jnp.exp(scores - top), 0.0)
            prob = expo / jnp.sum(expo, axis=1, keepdims=True)
            prob_low = prob.astype(BF)
            attended = dot(prob_low, values)
            delta = jnp.sum(d_att.astype(F32) * attended, axis=1, keepdims=True)
            d_score = (prob * (dot(d_att, values, 1, 1) - delta)).astype(BF)
            d_query = dot(d_score, keys) * scale
            dkv[0] += dot(d_score, query, 0, 0)
            dkv[1] += dot(prob_low, d_att, 0, 0)
            where = pl.ds(begin, q_slabs)
            zout[0, where, toks, cols] = attended.astype(BF).reshape(q_slabs, tok, HEAD)
            zout[1, where, toks, cols] = d_query.astype(BF).reshape(q_slabs, tok, HEAD)

        loop(group_tok // queries, query_step)
        zout[2, :, toks, cols] = (dkv[0] * scale).astype(BF).reshape(ns, tok, HEAD)
        zout[3, :, toks, cols] = dkv[1].astype(BF).reshape(ns, tok, HEAD)

    loop(per * heads, pair_step)

    for i in (1, 2, 3, 0):
        for step in range(1, ns):
            target = wrap(sq + step, ns)
            home.copy(zout.at[i, target], zback.at[i, tile(sq, slab), :], i, step).start()
        zback[i, tile(sq, slab), :] = zout[i, sq]
    ticks.tick()
    outs = (att_ref, dq_ref, dk_ref, dv_ref)
    for i in (1, 2, 3, 0):
        for step in range(1, ns):
            source = wrap(sq - step, ns)
            home.copy(zout.at[i, 0], zback.at[i, tile(source, slab), :], i, step).wait_recv()
        if i in (0, 3):
            outs[i][...] = zback[i]
        else:

            def back_step(r, i=i):
                rows = tile(r, tok)
                for head in range(heads):
                    cols = slice(head * HEAD, head * HEAD + HEAD)
                    piece = zback[i, rows, cols].astype(F32)
                    piece = rotated_back(piece, [planes_ref[k, rows, :] for k in range(3)])
                    outs[i][rows, cols] = piece.astype(BF)

            loop(nf, back_step)
        ticks.tick()
    ticks.finish()
    for gather in (ag_r, ag_g, *ag_x):
        gather.drain()
    for chunk in range(CHUNKS):
        turn.drain(chunk)
    for i in range(3):
        turns[i].drain(0)
    for copy in saves:
        copy.wait()
    for i in range(4):
        for step in range(1, ns):
            there.copy(zin.at[i, 0], zin.at[i, 0], i, step).wait_send()
            home.copy(zout.at[i, 0], zout.at[i, 0], i, step).wait_send()


def run_forward(nf, ns, low, g_own, win, wout, ws, wo, planes, lens):
    tok = g_own.shape[0]
    hidden = wout.shape[0]
    wide = wo.shape[0]
    lines = forward_lines(nf, wide, hidden)
    count = (8 + CHUNKS) * (nf - 1) + 8 * (ns - 1)
    flat = shape((nf * tok, wide))
    block = shape((nf, tok, D))
    total = CHUNKS * (hidden // CHUNKS // LANES)
    rest = total - lines.kinds[0][1]
    outs = [block] * 4 + [shape((D, hidden))] + [shape((nf * tok, hidden))] * 2
    outs += [shape((3, D, wide)), shape((rest, 1, LANES, D)), shape((rest, nf, D // nf, LANES))]
    outs += lines.outs() + [flat] * 4
    exchange = pltpu.VMEM((4, ns, nf // ns * tok, wide), BF)
    return pl.pallas_call(
        partial(forward_kernel, nf, ns, lines),
        out_shape=tuple(outs),
        in_specs=[hbm()] * 3
        + [vmem()]
        + [hbm()] * 3
        + [vmem()] * 2
        + [pl.BlockSpec(memory_space=pltpu.SMEM)],
        out_specs=(hbm(),) * 12 + (vmem(),) * 4,
        scratch_shapes=[
            pltpu.VMEM((nf, tok, D), BF),
            pltpu.VMEM((nf, tok, D), BF),
            pltpu.VMEM((D, hidden), BF),
            pltpu.VMEM((nf * tok, hidden), BF),
            pltpu.VMEM((nf * tok, hidden), BF),
            pltpu.VMEM((total, 1, LANES, D), BF),
            pltpu.VMEM((total, nf, D // nf, LANES), BF),
            pltpu.VMEM((nf, tok, D), BF),
            pltpu.VMEM((3, D, wide), BF),
            pltpu.VMEM((4, nf * tok, wide), BF),
            exchange,
            exchange,
            pltpu.VMEM((4, nf * tok, wide), BF),
            pltpu.VMEM((2, ns * tok, HEAD), F32),
            pltpu.SemaphoreType.DMA((count,)),
            pltpu.SemaphoreType.DMA((count,)),
            pltpu.SemaphoreType.DMA((16,)),
        ]
        + lines.scratch(),
        compiler_params=params(1),
        name="forward",
    )(low, g_own, win, wout, *ws, wo, planes, lens)


TENSORS = 5


def return_lines(nf, wide, rest):
    count = wide // LANES
    kinds = [((1, LANES, D), rest, False), ((nf, D // nf, LANES), rest, True)]
    return Lines(nf, kinds + [((nf, D // nf, LANES), count, True)] * 2)


def return_kernel(nf, ns, lines, *refs):
    att_ref, dq_ref, dk_ref, dv_ref, dup_ref, wqkv, win_ref, wo_ref, wout_ref, h_ref = refs[:10]
    p_out, p_in = refs[10:12]
    sources = refs[12:16]
    refs = refs[16:]
    y_ref, dx_ref, dwv_ref, dwo_ref = refs[:4]
    results = refs[4:8]
    refs = refs[8:]
    stage, part, sib, rec, p_q, p_k, send_sem, recv_sem, copy_sem, credit = refs[:10]
    line_refs = refs[10:]
    plane = Plane(nf)
    sems = (send_sem, recv_sem)
    tok = y_ref.shape[0]
    wide = wo_ref.shape[0]
    parts, sibs = part.shape[0], sib.shape[0]
    greet(nf, ns)
    built = lines.build(plane, ns, (p_out, p_in, p_q, p_k), results, line_refs)
    jobs = []
    for line in built:
        jobs += [(line, chunk) for chunk in range(line.count)]
    ticks = Ticks(jobs)
    load = pltpu.make_async_copy(sources[0], stage, copy_sem)
    load.start()
    scats = [
        Scatter(
            plane,
            part.at[t % parts],
            sib.at[t % sibs],
            rec.at[t % sibs],
            sems,
            t * CHUNKS * (nf - 1),
            CHUNKS,
        )
        for t in range(TENSORS)
    ]
    firsts = (dq_ref, dk_ref, dv_ref, dup_ref)

    def total(t):
        def total_step(chunk):
            feats = tile(chunk, D // CHUNKS)
            if t < 4:
                dx_ref[t, :, feats] = scats[t].total(chunk)
            else:
                y_ref[:, feats] = scats[t].total(chunk)

        loop(CHUNKS, total_step)
        if t + sibs < TENSORS:
            for target in [plane.on(0, 1)] + [plane.on(k) for k in range(1, plane.chips)]:
                pl.semaphore_signal(
                    credit.at[t], inc=1, device_id={"fsdp": target}, device_id_type=MESH
                )

    ticks.tick()
    for t in range(TENSORS):
        if t >= sibs:
            pl.semaphore_wait(credit.at[t - sibs], plane.chips)
        for chunk in range(CHUNKS):
            feats = slice(chunk * (D // CHUNKS), (chunk + 1) * (D // CHUNKS))
            if t >= parts:
                scats[t - parts].drain(chunk)
            if t < 3:
                value = dot(firsts[t][...], wqkv[t, feats, :], 1, 1)
            elif t == 3:
                value = dot(dup_ref[...], win_ref[feats, :], 1, 1)
            else:
                value = dot(att_ref[...], wo_ref[:, feats]) + dot(h_ref[...], wout_ref[:, feats])
            scats[t].part[:, :, feats] = value.astype(BF).reshape(nf, tok, D // CHUNKS)
            scats[t].start(chunk)
            if chunk > 0:
                scats[t].combine(chunk - 1)
            if chunk % 2:
                ticks.tick()
        scats[t].combine(CHUNKS - 1)
        if t < 4:
            pltpu.make_async_copy(sources[t], stage, copy_sem).wait()

            def grad_step(i, t=t):
                feats = tile(i, WIDTH)
                every = stage[:, :, feats].reshape(nf * tok, WIDTH)
                if t < 3:
                    grad = dot(every, firsts[t][...], 0, 0).astype(BF)
                    count = WIDTH * nf // D
                    for k in range(wide // LANES):
                        piece = grad[:, k * LANES : k * LANES + LANES]
                        piece = piece.reshape(count, D // nf, LANES)
                        (p_q, p_k, dwv_ref)[t][k, pl.ds(i * count, count)] = piece
                else:
                    grad = dot(att_ref[...], every, 0, 0).astype(BF)
                    for k in range(wide // LANES):
                        dwo_ref[k, 0, :, feats] = grad[k * LANES : k * LANES + LANES]

            loop(D // WIDTH, grad_step)
            if t < 3:
                pltpu.make_async_copy(sources[t + 1], stage, copy_sem).start()
        if t:
            total(t - 1)
    total(TENSORS - 1)
    ticks.finish()
    for t in range(TENSORS - parts, TENSORS):
        loop(CHUNKS, scats[t].drain)


def run_return(nf, ns, att, ds, dup, wqkv, win, wo, wout, h, p_out, p_in, gg, xgs):
    tok = gg.shape[1]
    wide = wo.shape[0]
    chips = nf // 2
    count = TENSORS * CHUNKS * (nf - 1)
    parts = 2 if nf <= 8 else 1
    lines = return_lines(nf, wide, p_out.shape[0])
    turned = (wide // LANES, nf, D // nf, LANES)
    outs = [shape((tok, D), F32), shape((4, tok, D), F32), shape(turned)]
    outs += [shape((wide // LANES, 1, LANES, D))] + lines.outs()
    return pl.pallas_call(
        partial(return_kernel, nf, ns, lines),
        out_shape=tuple(outs),
        in_specs=[vmem()] * 12 + [hbm()] * 4,
        out_specs=(vmem(),) * 4 + (hbm(),) * 4,
        scratch_shapes=[
            pltpu.VMEM((nf, tok, D), BF),
            pltpu.VMEM((parts, nf, tok, D), BF),
            pltpu.VMEM((2, chips, tok, D), BF),
            pltpu.VMEM((2, chips - 1, tok, D), BF),
            pltpu.VMEM(turned, BF),
            pltpu.VMEM(turned, BF),
            pltpu.SemaphoreType.DMA((count,)),
            pltpu.SemaphoreType.DMA((count,)),
            pltpu.SemaphoreType.DMA,
            pltpu.SemaphoreType.REGULAR((TENSORS - 2,)),
        ]
        + lines.scratch(),
        compiler_params=params(2),
        name="give_back",
    )(att, *ds, dup, wqkv, win, wo, wout, h, p_out, p_in, *xgs, gg)


SMALL = 112


def end_lines(nf, wide):
    count = wide // LANES
    return Lines(nf, [((nf, D // nf, LANES), count, True), ((1, LANES, D), count, False)])


def end_kernel(
    nf,
    ns,
    lines,
    p_v,
    p_o,
    hist_ref,
    st_ref,
    dx_ref,
    g_ref,
    y_ref,
    coef_ref,
    inv_ref,
    pre_ref,
    act_ref,
    mixed_ref,
    mix_in_ref,
    mix_out_ref,
    again_ref,
    mgain_ref,
    xgain_ref,
    hg_ref,
    lo_ref,
    sm_out,
    sum_v,
    sum_o,
    ds,
    last,
    dmixed,
    dcoef,
    gsum,
    sm_ref,
    sm_src,
    sm_in,
    sm_z,
    sm_sem,
    sm_rsem,
    *line_refs,
):
    tok = hist_ref.shape[1]
    plane = Plane(nf)
    greet(nf, ns)
    built = lines.build(plane, ns, (p_v, p_o), (sum_v, sum_o), line_refs)
    jobs = []
    for line in built:
        jobs += [(line, chunk) for chunk in range(line.count)]
    ticks = Ticks(jobs)
    small = Small(plane, ns, sm_src, sm_in, sm_z, sm_out, (sm_sem, sm_rsem))
    ticks.tick(2)
    gsum[...] = jnp.zeros_like(gsum)

    def back(value, inv, gain, grad):
        scaled = grad * gain
        mean = jnp.sum(value * scaled, axis=1, keepdims=True) / D
        return inv * scaled - value * (inv * inv * inv * mean)

    def row_step(i):
        rows = tile(i, ROWS)
        coef = coef_ref[rows, :]
        lane = lax.broadcasted_iota(jnp.int32, (ROWS, STREAMS * HIST), 1)
        for c in range(STREAMS):
            value, inv = st_ref[c, rows, :], inv_ref[c, rows, :]
            grad = dx_ref[c, rows, :]
            gain = mgain_ref if c == STREAMS - 1 else again_ref
            gsum[c // 3] += grad * (value * inv)
            d_value = back(value, inv, gain[...], grad)
            if c == STREAMS - 1:
                d_value = d_value + g_ref[rows, :].astype(F32)
                lo_ref[rows, :] = (value + y_ref[rows, :]).astype(BF)
            ds[c] = d_value
        found = jnp.zeros((ROWS, STREAMS * HIST), F32)
        for j in range(HIST):
            sums = [jnp.zeros((ROWS, 128), F32)] * STREAMS
            for begin in range(0, D, WIDTH):
                cols = slice(begin, begin + WIDTH)
                entry = hist_ref[j, rows, cols].astype(F32)
                grad = jnp.zeros((ROWS, WIDTH), F32)
                for c in range(STREAMS):
                    at = c * HIST + j
                    value = ds[c, :, cols]
                    grad = grad + coef[:, at : at + 1] * value
                    product = value * entry
                    for k in range(0, WIDTH, 128):
                        sums[c] = sums[c] + product[:, k : k + 128]
                if j < HIST - 1:
                    hg_ref[j, rows, cols] = grad.astype(BF)
                else:
                    last[rows, cols] = grad
            for c in range(STREAMS):
                value = jnp.sum(sums[c], axis=1, keepdims=True)
                found = jnp.where(lane == c * HIST + j, value, found)
        dcoef[rows, :] = found.astype(BF)

    loop(tok // ROWS // 2, row_step)
    ticks.tick()
    loop(tok // ROWS // 2, lambda i: row_step(i + tok // ROWS // 2))
    ticks.tick()
    mix_in, mix_out = mix_in_ref[...].astype(BF), mix_out_ref[...].astype(BF)
    pre, d_coef = pre_ref[...], dcoef[...]
    slope = 0.5 * (1.0 + lax.erf(pre * (0.5**0.5)))
    slope = slope + pre * jnp.exp(-0.5 * pre * pre) * 0.3989422804014327
    d_pre = (dot(d_coef, mix_out, 1, 1) * slope).astype(BF)
    hidden = pre.shape[1]
    sm_ref[0:hidden, :] = dot(d_pre, mixed_ref[...], 0, 0)
    dmixed[...] = dot(d_pre, mix_in, 1, 1)

    def last_step(i):
        rows = tile(i, ROWS)
        value, inv, grad = hist_ref[HIST - 1, rows, :].astype(F32), inv_ref[STREAMS, rows, :], dmixed[rows, :]
        gsum[2] += grad * (value * inv)
        total = last[rows, :] + back(value, inv, xgain_ref[...], grad)
        hg_ref[HIST - 1, rows, :] = total.astype(BF)

    loop(tok // ROWS, last_step)
    for k in range(3):
        sm_ref[hidden + k : hidden + k + 1, :] = jnp.sum(gsum[k], axis=0, keepdims=True)
    begin = hidden + 3
    sm_ref[begin:SMALL, :] = jnp.zeros((SMALL - begin, D), F32)
    turned = dot(d_coef, act_ref[...], 0, 0)
    for k in range(STREAMS * HIST):
        at = begin + k // STREAMS
        cols = slice(k % STREAMS * 128, k % STREAMS * 128 + hidden)
        sm_ref[at : at + 1, cols] = turned[k : k + 1, :]
    for k in range(nf):
        sm_src[k] = sm_ref[:, k * (D // nf) : (k + 1) * (D // nf)]
    small.start()
    ticks.tick(2)
    small.across()
    ticks.tick(2)
    small.finish()
    ticks.finish()
    small.drain()


def run_end(nf, ns, p_v, p_o, *args):
    tok = args[0].shape[1]
    wide = p_v.shape[0] * LANES
    lines = end_lines(nf, wide)
    cols = D // nf
    few = 2 * (nf - 1) + ns - 1
    outs = [shape((HIST, tok, D)), shape((tok, D)), shape((nf, SMALL, cols), F32)]
    return pl.pallas_call(
        partial(end_kernel, nf, ns, lines),
        out_shape=tuple(outs + lines.outs()),
        in_specs=[vmem()] * 17,
        out_specs=(vmem(),) * 3 + (hbm(),) * 2,
        scratch_shapes=[
            pltpu.VMEM((STREAMS, ROWS, D), F32),
            pltpu.VMEM((tok, D), F32),
            pltpu.VMEM((tok, D), F32),
            pltpu.VMEM((tok, STREAMS * HIST), BF),
            pltpu.VMEM((3, ROWS, D), F32),
            pltpu.VMEM((SMALL, D), F32),
            pltpu.VMEM((nf, SMALL, cols), F32),
            pltpu.VMEM((nf, SMALL, cols), F32),
            pltpu.VMEM((ns, SMALL, cols), F32),
            pltpu.SemaphoreType.DMA((few,)),
            pltpu.SemaphoreType.DMA((few,)),
        ]
        + lines.scratch(),
        compiler_params=params(3),
        name="streams_back",
    )(p_v, p_o, *args)


class Small:
    def __init__(self, plane, ns, src, mid, line, out, sems):
        self.plane, self.ns, self.src, self.mid, self.line, self.out = plane, ns, src, mid, line, out
        self.sems = sems
        self.me = lax.axis_index("seq")

    def scatter(self, step):
        target = wrap(self.plane.me + step, self.plane.nf)
        return send(
            self.src.at[target], self.mid.at[self.plane.me], self.sems, step - 1, "fsdp", target
        )

    def along(self, step):
        me = self.line.at[self.me]
        slot = self.plane.nf - 1 + step - 1
        return send(me, me, self.sems, slot, "seq", wrap(self.me + step, self.ns))

    def spread(self, step):
        me = self.out.at[self.plane.me]
        slot = self.plane.nf - 1 + self.ns - 1 + step - 1
        return send(me, me, self.sems, slot, "fsdp", wrap(self.plane.me + step, self.plane.nf))

    def start(self):
        self.mid[self.plane.me] = self.src[self.plane.me]
        for step in range(1, self.plane.nf):
            self.scatter(step).start()

    def across(self):
        for step in range(1, self.plane.nf):
            self.scatter(step).wait_recv()
        total = self.mid[0]
        for k in range(1, self.plane.nf):
            total += self.mid[k]
        self.line[self.me] = total
        for step in range(1, self.ns):
            self.along(step).start()

    def finish(self):
        for step in range(1, self.ns):
            self.along(step).wait_recv()
        total = self.line[0]
        for k in range(1, self.ns):
            total += self.line[k]
        self.out[self.plane.me] = total
        for step in range(1, self.plane.nf):
            self.spread(step).start()

    def drain(self):
        for step in range(1, self.plane.nf):
            self.spread(step).wait_recv()
        for step in range(1, self.plane.nf):
            self.scatter(step).wait_send()
            self.spread(step).wait_send()
        for step in range(1, self.ns):
            self.along(step).wait_send()


def turned_kernel(*refs):
    out_ref, at = refs[-1], 0
    for ref in refs[:-1]:
        for k in range(ref.shape[0]):
            out_ref[:, at : at + LANES] = ref[k, 0].astype(F32)
            at += LANES


def turned_rows(*parts):
    _, nf, rows, _ = parts[0].shape
    wide = sum(p.shape[0] for p in parts) * LANES
    return pl.pallas_call(
        turned_kernel,
        grid=(nf,),
        out_shape=shape((rows, nf * wide), F32),
        in_specs=[pl.BlockSpec((p.shape[0], 1, rows, LANES), lambda i: (0, i, 0, 0)) for p in parts],
        out_specs=pl.BlockSpec((rows, wide), lambda i: (0, i)),
        name="turned_rows",
    )(*parts)


def local(
    nf,
    ns,
    history,
    cotangent,
    seq_lengths,
    wq,
    wk,
    wv,
    wo,
    w_in,
    w_out,
    mix_in,
    mix_out,
    attn_gain,
    mlp_gain,
    mix_gain,
):
    hist = history[:, 0]
    tok_rows = hist.shape[1]
    lens = lax.all_gather(seq_lengths, "fsdp", axis=0, tiled=True)
    slab_index = lax.axis_index("seq") * tok_rows + jnp.arange(tok_rows, dtype=jnp.int32)
    every_index = jnp.tile(slab_index, nf)
    _, place = token_marks(every_index, jnp.repeat(lens, tok_rows, axis=0))
    planes = rope_planes(place)
    gains = [g[None] for g in (attn_gain, mlp_gain, mix_gain)]
    low, stream, coef, inv, pre, act, mixed = run_start(hist, mix_in, mix_out, *gains)
    grad_out = cotangent[0]
    ws = [w.astype(BF) for w in (wq, wk, wv)]
    wo_low, win_low, wout_low = wo.astype(BF), w_in.astype(BF), w_out.astype(BF)
    *xgs, gg, win_full, hidden, dup, wqkv, rest_out, rest_in, out_a, in_a, att, dq, dk, dv = run_forward(
        nf, ns, low, grad_out, win_low, wout_low, ws, wo_low, planes, lens
    )
    y_sum, dx, dwv, dwo, out_b, in_b, sum_q, sum_k = run_return(
        nf,
        ns,
        att,
        (dq, dk, dv),
        dup,
        wqkv,
        win_full,
        wo_low,
        wout_low,
        hidden,
        rest_out,
        rest_in,
        gg,
        xgs,
    )
    history_grad, layer_out, small, sum_v, sum_o = run_end(
        nf, ns, dwv, dwo, hist, stream, dx, grad_out, y_sum, coef, inv, pre, act, mixed, mix_in, mix_out, *gains
    )
    dwout = jnp.concatenate([out_a, out_b], axis=0).reshape(w_out.shape).astype(F32)
    dwo = sum_o.reshape(wo.shape).astype(F32)
    dw_in = turned_rows(in_a, in_b)
    dw_qkv = [turned_rows(s) for s in (sum_q, sum_k, sum_v)]
    small = small.transpose(1, 0, 2).reshape(SMALL, D)
    units = mix_in.shape[1]
    mix_out_rows = small[units + 3 :, : STREAMS * 128].reshape(HIST * STREAMS, 128)
    return (
        layer_out[None],
        history_grad[:, None],
        *dw_qkv,
        dwo,
        dw_in,
        dwout,
        small[:units].T,
        mix_out_rows[:, :units].T,
        small[units],
        small[units + 1],
        small[units + 2],
    )


def solution(mesh):
    rows, rep = P("fsdp", None), P()
    in_specs = (
        P(None, "fsdp", "seq", None),
        P("fsdp", "seq", None),
    ) + (rows,) * 7 + (rep,) * 5
    out_specs = (
        P("fsdp", "seq", None),
        P(None, "fsdp", "seq", None),
    ) + (rows,) * 6 + (rep,) * 5
    body = partial(local, mesh.shape["fsdp"], mesh.shape["seq"])
    return jax.shard_map(body, mesh=mesh, in_specs=in_specs, out_specs=out_specs, check_vma=False)
```

```python
from functools import partial

import jax
import jax.numpy as jnp
from jax import lax
from jax.experimental import pallas as pl
from jax.experimental.pallas import tpu as pltpu
from jax.sharding import PartitionSpec as P

D = 2048
HEADS = 16
HEAD = 128
ROT = 32
HIST = 9
STREAMS = 4
EPSILON = 1e-05
NEGATIVE = -1e30
MESH = pl.DeviceIdType.MESH
BF = jnp.bfloat16
F32 = jnp.float32
MIB = 2**20


CHUNKS = 4
LANES = 128
SLOTS = 6


def token_marks(tok_index, lengths):
    first_end = lengths[..., 0]
    second_end = first_end + lengths[..., 1]
    segment = (tok_index >= first_end).astype(jnp.int32) + (tok_index >= second_end).astype(
        jnp.int32
    )
    seq_begin = jnp.where(segment == 0, 0, jnp.where(segment == 1, first_end, second_end))
    return (segment, tok_index - seq_begin)


def rope_planes(tok_place):
    inverse = 10000.0 ** (-jnp.arange(0, ROT, 2, dtype=F32) / ROT)
    angles = tok_place.astype(F32)[:, None] * inverse[None, :]
    cosine, sine = jnp.cos(angles), jnp.sin(angles)
    rows = tok_place.shape[0]
    ones = jnp.ones((rows, HEAD - ROT), F32)
    none = jnp.zeros((rows, HEAD - ROT // 2), F32)
    gap = jnp.zeros((rows, ROT // 2), F32)
    return jnp.stack(
        [
            jnp.concatenate([cosine, cosine, ones], axis=1),
            jnp.concatenate([-sine, none], axis=1),
            jnp.concatenate([gap, sine, none[:, : HEAD - ROT]], axis=1),
        ]
    )


def dot(left_op, right_op, left_dim=1, right_dim=0):
    return lax.dot_general(
        left_op, right_op, (((left_dim,), (right_dim,)), ((), ())), preferred_element_type=F32
    )


def wrap(value, extent):
    return lax.rem(value + extent, extent)


def tile(index, extent):
    return pl.ds(pl.multiple_of(index * extent, extent), extent)


class Plane:
    def __init__(self, nf):
        self.nf = nf
        self.chips = nf // 2
        self.me = lax.axis_index("fsdp")
        self.chip = self.me // 2
        self.core = lax.rem(self.me, 2)

    def on(self, step, other=0):
        core = 1 - self.core if other else self.core
        return wrap(self.chip + step, self.chips) * 2 + core


def greet(nf, ns=1):
    barrier = pltpu.get_barrier_semaphore()
    for axis, extent in (("fsdp", nf), ("seq", ns)):
        for step in range(1, extent):
            pl.semaphore_signal(
                barrier,
                inc=1,
                device_id={axis: wrap(lax.axis_index(axis) + step, extent)},
                device_id_type=MESH,
            )
    pl.semaphore_wait(barrier, nf - 1 + ns - 1)


def send(src, dst, sems, slot, axis, target):
    return pltpu.make_async_remote_copy(
        src_ref=src,
        dst_ref=dst,
        send_sem=sems[0].at[slot],
        recv_sem=sems[1].at[slot],
        device_id={axis: target},
        device_id_type=MESH,
    )


class Gather:
    def __init__(self, plane, own, buf, sems, base):
        self.plane, self.own, self.buf, self.sems, self.base = plane, own, buf, sems, base

    def direct(self, step, slot=None):
        dst = self.buf.at[self.plane.me if slot is None else slot]
        src = self.own if slot is None else dst
        return send(src, dst, self.sems, self.base + step - 1, "fsdp", self.plane.on(step))

    def across(self, step, slot=None):
        slot = self.plane.on(-step) if slot is None else slot
        block = self.buf.at[slot]
        src = block if step else self.own
        base = self.base + self.plane.chips - 1
        return send(src, block, self.sems, base + step, "fsdp", self.plane.on(0, 1))

    def start(self):
        for step in range(1, self.plane.chips):
            self.direct(step).start()
        self.across(0).start()

    def keep(self, sem):
        return pltpu.make_async_copy(self.own, self.buf.at[self.plane.me], sem)

    def forward(self):
        for step in range(1, self.plane.chips):
            self.direct(step, self.plane.on(-step)).wait_recv()
            self.across(step).start()

    def finish(self):
        for step in range(self.plane.chips):
            self.across(step, self.plane.on(-step, 1)).wait_recv()

    def drain(self):
        for step in range(1, self.plane.chips):
            self.direct(step).wait_send()
        for step in range(self.plane.chips):
            self.across(step).wait_send()


class Turn:
    def __init__(self, plane, rows_ref, full_ref, sems, base, chunks):
        self.plane, self.sems, self.base, self.chunks = plane, sems, base, chunks
        self.rows_ref, self.full_ref = rows_ref, full_ref
        self.height = rows_ref.shape[0]
        self.width = full_ref.shape[1]
        self.part = self.width // chunks

    def copy(self, chunk, step, source=None):
        nf = self.plane.nf
        target = wrap(self.plane.me + step, nf)
        source = self.plane.me if source is None else source
        begin = pl.multiple_of(target * self.width + chunk * self.part, self.part)
        return send(
            self.rows_ref.at[:, pl.ds(begin, self.part)],
            self.full_ref.at[tile(source, self.height), tile(chunk, self.part)],
            self.sems,
            self.base + chunk * (nf - 1) + step - 1,
            "fsdp",
            target,
        )

    def start(self, chunk):
        for step in range(1, self.plane.nf):
            self.copy(chunk, step).start()

    def keep(self, sem):
        return pltpu.make_async_copy(
            self.rows_ref.at[:, tile(self.plane.me, self.width)],
            self.full_ref.at[tile(self.plane.me, self.height), :],
            sem,
        )

    def arrive(self, chunk):
        for step in range(1, self.plane.nf):
            self.copy(chunk, step, wrap(self.plane.me - step, self.plane.nf)).wait_recv()

    def drain(self, chunk):
        for step in range(1, self.plane.nf):
            self.copy(chunk, step).wait_send()


class Scatter:
    def __init__(self, plane, part, sib, rec, sems, base, chunks):
        self.plane, self.part, self.sib, self.rec = plane, part, sib, rec
        self.sems, self.base, self.chunks = sems, base, chunks
        self.width = part.shape[-1] // chunks

    def across(self, chunk, step):
        cols = tile(chunk, self.width)
        return send(
            self.part.at[self.plane.on(step, 1), :, cols],
            self.sib.at[wrap(self.plane.chip + step, self.plane.chips), :, cols],
            self.sems,
            self.base + chunk * (self.plane.nf - 1) + step,
            "fsdp",
            self.plane.on(0, 1),
        )

    def direct(self, chunk, step):
        cols = tile(chunk, self.width)
        return send(
            self.part.at[self.plane.on(step), :, cols],
            self.rec.at[step - 1, :, cols],
            self.sems,
            self.base + chunk * (self.plane.nf - 1) + self.plane.chips + step - 1,
            "fsdp",
            self.plane.on(step),
        )

    def start(self, chunk):
        for step in range(self.plane.chips):
            self.across(chunk, step).start()

    def combine(self, chunk):
        cols = tile(chunk, self.width)
        for step in range(1, self.plane.chips):
            chip = wrap(self.plane.chip + step, self.plane.chips)
            mine = self.plane.on(step)
            self.across(chunk, step).wait_recv()
            total = self.part[mine, :, cols].astype(F32) + self.sib[chip, :, cols].astype(F32)
            self.part[mine, :, cols] = total.astype(BF)
            self.direct(chunk, step).start()
        self.across(chunk, 0).wait_recv()

    def total(self, chunk):
        cols = tile(chunk, self.width)
        total = self.part[self.plane.me, :, cols].astype(F32)
        total += self.sib[self.plane.chip, :, cols].astype(F32)
        for step in range(1, self.plane.chips):
            self.direct(chunk, step).wait_recv()
            total += self.rec[step - 1, :, cols].astype(F32)
        return total

    def drain(self, chunk):
        for step in range(self.plane.chips):
            self.across(chunk, step).wait_send()
        for step in range(1, self.plane.chips):
            self.direct(chunk, step).wait_send()


def loop(extent, body):
    lax.fori_loop(0, extent, lambda i, c: (body(i), c)[1], 0)


def rows_of(ref3, begin, count):
    value = ref3[pl.ds(begin, count)]
    return value.reshape(count * value.shape[1], value.shape[2])


def vmem():
    return pl.BlockSpec(memory_space=pltpu.VMEM)


def hbm():
    return pl.BlockSpec(memory_space=pltpu.HBM)


def shape(dims, dtype=BF):
    return jax.ShapeDtypeStruct(tuple(dims), dtype)


def params(ident, limit=62):
    return pltpu.CompilerParams(
        collective_id=ident, has_side_effects=True, vmem_limit_bytes=limit * MIB
    )


ROWS = 16
WIDTH = 512


def start_kernel(
    hist_ref,
    mix_in_ref,
    mix_out_ref,
    again_ref,
    mgain_ref,
    xgain_ref,
    low_ref,
    st_ref,
    coef_ref,
    inv_ref,
    pre_ref,
    act_ref,
    mixed_ref,
):
    tok = hist_ref.shape[1]

    def mix_step(i):
        rows = tile(i, ROWS)
        value = hist_ref[HIST - 1, rows, :].astype(F32)
        inv = lax.rsqrt(jnp.mean(value * value, axis=1, keepdims=True) + EPSILON)
        mixed_ref[rows, :] = (value * inv * xgain_ref[...]).astype(BF)
        inv_ref[STREAMS, rows, :] = inv

    loop(tok // ROWS, mix_step)
    pre = dot(mixed_ref[...], mix_in_ref[...].astype(BF))
    pre_ref[...] = pre
    act = (0.5 * pre * (1.0 + lax.erf(pre * (0.5**0.5)))).astype(BF)
    act_ref[...] = act
    coef_ref[...] = dot(act, mix_out_ref[...].astype(BF))

    def stream_step(i):
        rows = tile(i, ROWS)
        coef = coef_ref[rows, :]
        squares = [jnp.zeros((ROWS, 1), F32)] * STREAMS
        for begin in range(0, D, WIDTH):
            cols = slice(begin, begin + WIDTH)
            total = [jnp.zeros((ROWS, WIDTH), F32)] * STREAMS
            for j in range(HIST):
                entry = hist_ref[j, rows, cols].astype(F32)
                for c in range(STREAMS):
                    at = c * HIST + j
                    total[c] = total[c] + coef[:, at : at + 1] * entry
            for c in range(STREAMS):
                st_ref[c, rows, cols] = total[c]
                squares[c] = squares[c] + jnp.sum(total[c] * total[c], axis=1, keepdims=True)
        for c in range(STREAMS):
            inv = lax.rsqrt(squares[c] / D + EPSILON)
            inv_ref[c, rows, :] = inv
            gain = mgain_ref if c == STREAMS - 1 else again_ref
            low_ref[c, rows, :] = (st_ref[c, rows, :] * inv * gain[...]).astype(BF)

    loop(tok // ROWS, stream_step)


def run_start(hist, mix_in, mix_out, again, mgain, xgain):
    tok = hist.shape[1]
    hidden = mix_in.shape[1]
    return pl.pallas_call(
        start_kernel,
        out_shape=(
            shape((STREAMS, tok, D)),
            shape((STREAMS, tok, D), F32),
            shape((tok, STREAMS * HIST), F32),
            shape((STREAMS + 1, tok, 1), F32),
            shape((tok, hidden), F32),
            shape((tok, hidden)),
            shape((tok, D)),
        ),
        in_specs=[vmem()] * 6,
        out_specs=(vmem(),) * 7,
        compiler_params=pltpu.CompilerParams(vmem_limit_bytes=62 * MIB),
        name="streams",
    )(hist, mix_in, mix_out, again, mgain, xgain)


def rotated(value, planes):
    return value * planes[0] + pltpu.roll(value, HEAD - ROT // 2, 1) * planes[1] + pltpu.roll(
        value, ROT // 2, 1
    ) * planes[2]


def rotated_back(value, planes):
    return value * planes[0] - pltpu.roll(value, HEAD - ROT // 2, 1) * planes[1] - pltpu.roll(
        value, ROT // 2, 1
    ) * planes[2]


class Exchange:
    def __init__(self, ns, sems, base):
        self.ns, self.sems, self.base = ns, sems, base
        self.me = lax.axis_index("seq")

    def copy(self, src, dst, lane, step):
        return send(
            src,
            dst,
            self.sems,
            self.base + lane * (self.ns - 1) + step - 1,
            "seq",
            wrap(self.me + step, self.ns),
        )


class Line:
    def __init__(self, plane, ns, part, inward, swap, res, sems, base, turned, copy_sem, credits):
        self.plane, self.ns, self.turned = plane, ns, turned
        self.part, self.inward, self.swap, self.res = part, inward, swap, res
        self.sems, self.base, self.copy_sem, self.credits = sems, base, copy_sem, credits
        self.me = lax.axis_index("seq")
        self.side = self.me // (ns // 2)
        middle = ns // 2 - 1
        self.depth = (1 - self.side) * (middle - self.me) + self.side * (self.me - middle - 1)
        self.ends = middle
        self.in_to = self.me + 1 - 2 * self.side
        self.out_to = self.me - 1 + 2 * self.side
        self.other = ns - 1 - self.me
        self.count = res.shape[0]
        self.slots = inward.shape[0]
        if self.ends != 1 and self.slots < self.count:
            raise ValueError("slots")

    @staticmethod
    def marks(nf, turned):
        return 5 + (nf - 1 if turned else 0)

    def sem(self, chunk, kind):
        return self.base + chunk * self.marks(self.plane.nf, self.turned) + kind

    def half(self, ref, chunk, side):
        rows = ref.shape[-2] // 2
        rows = pl.ds(pl.multiple_of(side * rows, rows), rows)
        return ref.at[chunk, :, rows, :]

    def inner(self, chunk, relayed=False):
        slot = chunk % self.slots
        src = self.inward.at[slot] if relayed else self.part.at[chunk]
        return send(src, self.inward.at[slot], self.sems, self.sem(chunk, 0), "seq", self.in_to)

    def cross(self, chunk):
        slot = chunk % self.slots
        return send(
            self.half(self.inward, slot, 1 - self.side),
            self.swap.at[slot],
            self.sems,
            self.sem(chunk, 1),
            "seq",
            self.other,
        )

    def result(self):
        return self.res if self.turned else self.part

    def back_cross(self, chunk, side=None):
        side = self.side if side is None else side
        return send(
            self.half(self.result(), chunk, side),
            self.half(self.res, chunk, side),
            self.sems,
            self.sem(chunk, 2),
            "seq",
            self.other,
        )

    def outer(self, chunk, side, src):
        return send(
            self.half(src, chunk, side),
            self.half(self.res, chunk, side),
            self.sems,
            self.sem(chunk, 3) + side,
            "seq",
            self.out_to,
        )

    def spread(self, chunk, step, source=None):
        rows = self.part.shape[-2] // 2
        rows = pl.ds(pl.multiple_of(self.side * rows, rows), rows)
        target = wrap(self.plane.me + step, self.plane.nf)
        source = self.plane.me if source is None else source
        return send(
            self.part.at[chunk, target, rows, :],
            self.res.at[chunk, source, rows, :],
            self.sems,
            self.sem(chunk, 4) + step,
            "fsdp",
            target,
        )

    def keep(self, chunk):
        if self.turned:
            rows = self.part.shape[-2] // 2
            rows = pl.ds(pl.multiple_of(self.side * rows, rows), rows)
            me = self.plane.me
            src, dst = self.part.at[chunk, me, rows, :], self.res.at[chunk, me, rows, :]
        else:
            src = self.half(self.part, chunk, self.side)
            dst = self.half(self.res, chunk, self.side)
        return pltpu.make_async_copy(src, dst, self.copy_sem.at[chunk])

    def begin(self, chunk):
        if self.ends:

            @pl.when(self.depth == self.ends)
            def _():
                if chunk >= self.slots:
                    pl.semaphore_wait(self.credits.at[0], 1)
                self.inner(chunk).start()

    def relay(self, chunk, hop):
        slot = chunk % self.slots

        @pl.when(self.depth == self.ends - hop)
        def _():
            self.inner(chunk).wait_recv()
            total = self.inward[slot].astype(F32) + self.part[chunk].astype(F32)
            self.inward[slot] = total.astype(BF)
            self.inner(chunk, True).start()

    def meet(self, chunk):
        slot = chunk % self.slots

        @pl.when(self.depth == 0)
        def _():
            self.inner(chunk).wait_recv()
            theirs = self.half(self.inward, slot, 1 - self.side)
            mine = self.half(self.part, chunk, 1 - self.side)

            def step(i):
                rows = tile(i, 16)
                total = theirs[:, rows, :].astype(F32) + mine[:, rows, :].astype(F32)
                theirs[:, rows, :] = total.astype(BF)

            loop(theirs.shape[1] // 16, step)
            if chunk >= self.slots:
                pl.semaphore_wait(self.credits.at[1], 1)
            self.cross(chunk).start()

    def settle(self, chunk):
        slot = chunk % self.slots

        @pl.when(self.depth == 0)
        def _():
            self.cross(chunk).wait_recv()
            theirs = self.half(self.inward, slot, self.side)
            mine = self.half(self.part, chunk, self.side)

            def step(i):
                rows = tile(i, 16)
                total = theirs[:, rows, :].astype(F32) + mine[:, rows, :].astype(F32)
                total += self.swap[slot, :, rows, :].astype(F32)
                mine[:, rows, :] = total.astype(BF)

            loop(theirs.shape[1] // 16, step)
            self.keep(chunk).start()
            if self.turned:
                for k in range(1, self.plane.nf):
                    self.spread(chunk, k).start()
            else:
                self.hand_out(chunk)
            self.cross(chunk).wait_send()
            if chunk + self.slots < self.count:
                pl.semaphore_signal(
                    self.credits.at[0], inc=1, device_id={"seq": self.out_to}, device_id_type=MESH
                )
                pl.semaphore_signal(
                    self.credits.at[1], inc=1, device_id={"seq": self.other}, device_id_type=MESH
                )

    def hand_out(self, chunk):
        self.back_cross(chunk).start()
        if self.ends:
            self.outer(chunk, self.side, self.result()).start()

    def spread_end(self, chunk):
        @pl.when(self.depth == 0)
        def _():
            for k in range(1, self.plane.nf):
                self.spread(chunk, k, wrap(self.plane.me - k, self.plane.nf)).wait_recv()
            self.keep(chunk).wait()
            self.hand_out(chunk)

    def pass_on(self, chunk):
        @pl.when(self.depth == 0)
        def _():
            self.back_cross(chunk, 1 - self.side).wait_recv()
            if self.ends:
                self.outer(chunk, 1 - self.side, self.res).start()

    def outward_hop(self, chunk, hop):
        @pl.when(self.depth == hop)
        def _():
            for side in range(2):
                self.outer(chunk, side, self.res).wait_recv()
                self.outer(chunk, side, self.res).start()

    def pause(self, chunk):
        pass

    def phases(self):
        listed = [partial(self.relay, hop=hop) for hop in range(1, self.ends)]
        listed += [self.meet, self.settle]
        if self.turned:
            listed += [self.pause, self.spread_end]
        listed += [self.pass_on]
        listed += [partial(self.outward_hop, hop=hop) for hop in range(1, self.ends)]
        return listed

    def drain(self, chunk):
        @pl.when(self.depth == 0)
        def _():
            self.back_cross(chunk).wait_send()
            if self.turned:
                for k in range(1, self.plane.nf):
                    self.spread(chunk, k).wait_send()
            else:
                self.keep(chunk).wait()

        if self.ends:

            @pl.when(self.depth == self.ends)
            def _():
                for side in range(2):
                    self.outer(chunk, side, self.res).wait_recv()

            @pl.when(self.depth < self.ends)
            def _():
                for side in range(2):
                    self.outer(chunk, side, self.res).wait_send()

            @pl.when(self.depth > 0)
            def _():
                self.inner(chunk).wait_send()


class Ticks:
    def __init__(self, jobs, lead):
        self.jobs, self.lead = jobs, lead
        self.now, self.begun = 0, 0

    def tick(self, times=1):
        for _ in range(times):
            while self.begun < min(len(self.jobs), self.now + self.lead + 1):
                line, chunk = self.jobs[self.begun]
                line.begin(chunk)
                self.begun += 1
            for i, (line, chunk) in enumerate(self.jobs):
                phase = self.now - i - 1
                if 0 <= phase < len(line.phases()):
                    line.phases()[phase](chunk)
            self.now += 1

    def finish(self):
        depth = max(len(line.phases()) for line, _ in self.jobs)
        while self.now < len(self.jobs) + depth:
            self.tick()
        for line, chunk in self.jobs:
            line.drain(chunk)


class Lines:
    def __init__(self, nf, kinds):
        self.nf, self.kinds = nf, kinds

    def scratch(self):
        listed = []
        for (blocks, rows, cols), count, _ in self.kinds:
            slots = min(count, SLOTS)
            listed.append(pltpu.VMEM((slots, blocks, rows, cols), BF))
            listed.append(pltpu.VMEM((slots, blocks, rows // 2, cols), BF))
            listed.append(pltpu.SemaphoreType.DMA((count,)))
            listed.append(pltpu.SemaphoreType.REGULAR((2,)))
        marks = sum(count * Line.marks(self.nf, turned) for _, count, turned in self.kinds)
        return listed + [pltpu.SemaphoreType.DMA((marks,))] * 2

    def count(self):
        return 4 * len(self.kinds) + 2

    def outs(self):
        return [shape((count,) + dims) for dims, count, _ in self.kinds]

    def build(self, plane, ns, parts, results, scratch):
        lines, base = [], 0
        sems = tuple(scratch[-2:])
        for k, (_, count, turned) in enumerate(self.kinds):
            inward, swap, copy_sem, credits = scratch[4 * k : 4 * k + 4]
            lines.append(
                Line(
                    plane,
                    ns,
                    parts[k],
                    inward,
                    swap,
                    results[k],
                    sems,
                    base,
                    turned,
                    copy_sem,
                    credits,
                )
            )
            base += count * Line.marks(self.nf, turned)
        return lines


def forward_lines(nf, wide, hidden):
    return Lines(nf, [((1, LANES, D), hidden // LANES, False)])


def forward_kernel(nf, ns, lines, *refs):
    (low, g_ref, win_ref, wout_ref, wq_ref, wk_ref, wv_ref, wo_ref, planes_ref, lens_ref) = refs[:10]
    refs = refs[10:]
    (xq_out, xk_out, xv_out, gg_out, pr_out, py_out, w_out, rest_in) = refs[:8]
    refs = refs[8:]
    sum_out, att_ref, dq_ref, dk_ref, dv_ref = refs[:5]
    refs = refs[5:]
    (xr, gg, wfull, hid, dup, p_out, p_in, stage, wqkv, qkva, zin, zout, zback, dkv) = refs[:14]
    send_sem, recv_sem, copy_sem = refs[14:17]
    line_refs = refs[17:]
    plane = Plane(nf)
    sems = (send_sem, recv_sem)
    tok = g_ref.shape[0]
    wide = wo_ref.shape[0]
    heads = wide // HEAD
    per = nf // ns
    slab = per * tok
    group_tok = ns * tok
    sq = lax.axis_index("seq")
    width = wfull.shape[1] // CHUNKS
    blocks = min(4, nf)
    pieces = width // LANES
    step_sems = nf - 1
    greet(nf, ns)
    (l_out,) = lines.build(plane, ns, (p_out,), (sum_out,), line_refs)
    ticks = Ticks([(l_out, chunk) for chunk in range(l_out.count)], 1)
    ag_r = Gather(plane, low.at[3], xr, sems, 0)
    ag_g = Gather(plane, g_ref, gg, sems, step_sems)
    ag_x = [
        Gather(plane, low.at[i], out, sems, (2 + i) * step_sems)
        for i, out in enumerate((xq_out, xk_out, xv_out))
    ]
    turn = Turn(plane, win_ref, wfull, sems, 5 * step_sems, CHUNKS)
    turns = [
        Turn(plane, w, wqkv.at[i], sems, (5 + CHUNKS + i) * step_sems, 1)
        for i, w in enumerate((wq_ref, wk_ref, wv_ref))
    ]
    base = (8 + CHUNKS) * step_sems
    there = Exchange(ns, sems, base)
    home = Exchange(ns, sems, base + 4 * (ns - 1))
    ag_r.start()
    turn.start(0)
    ag_g.start()
    for chunk in range(1, CHUNKS):
        turn.start(chunk)
    for i in range(3):
        ag_x[i].start()
        turns[i].start(0)
    keeps = [ag_r.keep(copy_sem.at[0]), ag_g.keep(copy_sem.at[1]), turn.keep(copy_sem.at[2])]
    keeps += [ag_x[i].keep(copy_sem.at[3 + i]) for i in range(3)]
    keeps += [turns[i].keep(copy_sem.at[6 + i]) for i in range(3)]
    for keep in keeps:
        keep.start()
    ag_r.forward()
    ag_g.forward()
    ag_r.finish()
    ag_g.finish()
    for keep in keeps:
        keep.wait()
    saves, started = [], []

    def save(src, dst):
        started.append(dst)
        saves.append(pltpu.make_async_copy(src, dst, copy_sem.at[8 + len(started)]))
        saves[-1].start()

    save(gg, gg_out)

    for chunk in range(CHUNKS):
        turn.arrive(chunk)
        cols = slice(chunk * width, chunk * width + width)

        def rows_step(i, cols=cols):
            rows = tile(i, blocks * tok)
            up = dot(rows_of(xr, i * blocks, blocks), wfull[:, cols])
            dh = dot(rows_of(gg, i * blocks, blocks), wout_ref[cols, :], 1, 1)
            cdf = 0.5 * (1.0 + lax.erf(up * (0.5**0.5)))
            slope = cdf + up * jnp.exp(-0.5 * up * up) * 0.3989422804014327
            hid[rows, cols] = (up * cdf).astype(BF)
            dup[rows, cols] = (dh * slope).astype(BF)

        loop(nf // blocks, rows_step)

        def grad_step(i, cols=cols, chunk=chunk):
            feats = tile(i, WIDTH)
            every = gg[:, :, feats].reshape(nf * tok, WIDTH)
            grad = dot(hid[:, cols], every, 0, 0).astype(BF)
            for k in range(pieces):
                p_out[chunk * pieces + k, 0, :, feats] = grad[k * LANES : k * LANES + LANES]
            every = xr[:, :, feats].reshape(nf * tok, WIDTH)
            grad = dot(every, dup[:, cols], 0, 0).astype(BF)
            count = WIDTH * nf // D
            for k in range(pieces):
                piece = grad[:, k * LANES : k * LANES + LANES].reshape(count, D // nf, LANES)
                p_in[chunk * pieces + k, pl.ds(i * count, count)] = piece

        loop(D // WIDTH, grad_step)
        ticks.tick()

    save(p_in, rest_in)

    def partial_sums(left, right, right_dim, out):
        def step(i):
            feats = tile(i, WIDTH)
            block = right[feats, :] if right_dim else right[:, feats]
            value = dot(left[...], block, 1, right_dim).astype(BF)
            stage[:, :, feats] = value.reshape(nf, tok, WIDTH)

        loop(D // WIDTH, step)
        save(stage, out)

    partial_sums(dup, wfull, 1, pr_out)

    def ship(i):
        for step in range(1, ns):
            target = wrap(sq + step, ns)
            there.copy(qkva.at[i, tile(target, slab), :], zin.at[i, sq], i, step).start()
        zin[i, sq] = qkva[i, tile(sq, slab), :]

    def da_step(i):
        rows = tile(i, blocks * tok)
        qkva[3, rows, :] = dot(rows_of(gg, i * blocks, blocks), wo_ref[...], 1, 1).astype(BF)

    loop(nf // blocks, da_step)
    ship(3)
    ticks.tick()
    for i in range(3):
        ag_x[i].forward()
        turns[i].arrive(0)
        ag_x[i].finish()
        if i == 0:
            saves[-1].wait()
            saves.pop()
        load = pltpu.make_async_copy(ag_x[i].buf, stage, copy_sem.at[15])
        load.start()
        load.wait()

        def lin_step(r, i=i):
            rows = tile(r, blocks * tok)
            lin = dot(rows_of(stage, r * blocks, blocks), wqkv[i])
            for head in range(heads):
                cols = slice(head * HEAD, head * HEAD + HEAD)
                piece = lin[:, cols]
                if i < 2:
                    piece = rotated(piece, [planes_ref[k, rows, :] for k in range(3)])
                qkva[i, rows, cols] = piece.astype(BF)

        loop(nf // blocks, lin_step)
        ship(i)
        ticks.tick(2 if i < 2 else 1)
    save(wqkv, w_out)
    partial_sums(hid, wout_ref, 0, py_out)
    for i in range(4):
        for step in range(1, ns):
            there.copy(zin.at[i, 0], zin.at[i, wrap(sq - step, ns)], i, step).wait_recv()

    scale = HEAD ** (-0.5)
    queries = min(256, group_tok)
    q_slabs = queries // tok

    def pair_step(pair):
        grp = pair // heads
        head = lax.rem(pair, heads)
        cols = tile(head, HEAD)
        toks = tile(grp, tok)
        first_end = lens_ref[sq * per + grp, 0]
        second_end = first_end + lens_ref[sq * per + grp, 1]

        def part_of(i, begin, count):
            return zin[i, pl.ds(begin, count), toks, cols].reshape(count * tok, HEAD)

        keys, values = part_of(1, 0, ns), part_of(2, 0, ns)
        dkv[...] = jnp.zeros_like(dkv)

        def query_step(j):
            begin = j * q_slabs
            query, d_att = part_of(0, begin, q_slabs), part_of(3, begin, q_slabs)
            qi = j * queries + lax.broadcasted_iota(jnp.int32, (queries, group_tok), 0)
            ki = lax.broadcasted_iota(jnp.int32, (queries, group_tok), 1)
            seg_q = (qi >= first_end).astype(jnp.int32) + (qi >= second_end).astype(jnp.int32)
            seg_k = (ki >= first_end).astype(jnp.int32) + (ki >= second_end).astype(jnp.int32)
            allowed = (seg_q == seg_k) & (qi >= ki)
            scores = jnp.where(allowed, dot(query, keys, 1, 1) * scale, NEGATIVE)
            top = jnp.max(scores, axis=1, keepdims=True)
            expo = jnp.where(allowed, jnp.exp(scores - top), 0.0)
            prob = expo / jnp.sum(expo, axis=1, keepdims=True)
            prob_low = prob.astype(BF)
            attended = dot(prob_low, values)
            delta = jnp.sum(d_att.astype(F32) * attended, axis=1, keepdims=True)
            d_score = (prob * (dot(d_att, values, 1, 1) - delta)).astype(BF)
            d_query = dot(d_score, keys) * scale
            dkv[0] += dot(d_score, query, 0, 0)
            dkv[1] += dot(prob_low, d_att, 0, 0)
            where = pl.ds(begin, q_slabs)
            zout[0, where, toks, cols] = attended.astype(BF).reshape(q_slabs, tok, HEAD)
            zout[1, where, toks, cols] = d_query.astype(BF).reshape(q_slabs, tok, HEAD)

        loop(group_tok // queries, query_step)
        zout[2, :, toks, cols] = (dkv[0] * scale).astype(BF).reshape(ns, tok, HEAD)
        zout[3, :, toks, cols] = dkv[1].astype(BF).reshape(ns, tok, HEAD)

    loop(per * heads, pair_step)

    for i in (1, 2, 3, 0):
        for step in range(1, ns):
            target = wrap(sq + step, ns)
            home.copy(zout.at[i, target], zback.at[i, tile(sq, slab), :], i, step).start()
        zback[i, tile(sq, slab), :] = zout[i, sq]
    ticks.tick()
    outs = (att_ref, dq_ref, dk_ref, dv_ref)
    for i in (1, 2, 3, 0):
        for step in range(1, ns):
            source = wrap(sq - step, ns)
            home.copy(zout.at[i, 0], zback.at[i, tile(source, slab), :], i, step).wait_recv()
        if i in (0, 3):
            outs[i][...] = zback[i]
        else:

            def back_step(r, i=i):
                rows = tile(r, tok)
                for head in range(heads):
                    cols = slice(head * HEAD, head * HEAD + HEAD)
                    piece = zback[i, rows, cols].astype(F32)
                    piece = rotated_back(piece, [planes_ref[k, rows, :] for k in range(3)])
                    outs[i][rows, cols] = piece.astype(BF)

            loop(nf, back_step)
        ticks.tick()
    ticks.finish()
    for gather in (ag_r, ag_g, *ag_x):
        gather.drain()
    for chunk in range(CHUNKS):
        turn.drain(chunk)
    for i in range(3):
        turns[i].drain(0)
    for copy in saves:
        copy.wait()
    for i in range(4):
        for step in range(1, ns):
            there.copy(zin.at[i, 0], zin.at[i, 0], i, step).wait_send()
            home.copy(zout.at[i, 0], zout.at[i, 0], i, step).wait_send()


def run_forward(nf, ns, low, g_own, win, wout, ws, wo, planes, lens):
    tok = g_own.shape[0]
    hidden = wout.shape[0]
    wide = wo.shape[0]
    lines = forward_lines(nf, wide, hidden)
    count = (8 + CHUNKS) * (nf - 1) + 8 * (ns - 1)
    flat = shape((nf * tok, wide))
    block = shape((nf, tok, D))
    total = CHUNKS * (hidden // CHUNKS // LANES)
    outs = [block] * 6 + [shape((3, D, wide)), shape((total, nf, D // nf, LANES))]
    outs += lines.outs() + [flat] * 4
    exchange = pltpu.VMEM((4, ns, nf // ns * tok, wide), BF)
    return pl.pallas_call(
        partial(forward_kernel, nf, ns, lines),
        out_shape=tuple(outs),
        in_specs=[hbm()] * 3
        + [vmem()]
        + [hbm()] * 3
        + [vmem()] * 2
        + [pl.BlockSpec(memory_space=pltpu.SMEM)],
        out_specs=(hbm(),) * 9 + (vmem(),) * 4,
        scratch_shapes=[
            pltpu.VMEM((nf, tok, D), BF),
            pltpu.VMEM((nf, tok, D), BF),
            pltpu.VMEM((D, hidden), BF),
            pltpu.VMEM((nf * tok, hidden), BF),
            pltpu.VMEM((nf * tok, hidden), BF),
            pltpu.VMEM((total, 1, LANES, D), BF),
            pltpu.VMEM((total, nf, D // nf, LANES), BF),
            pltpu.VMEM((nf, tok, D), BF),
            pltpu.VMEM((3, D, wide), BF),
            pltpu.VMEM((4, nf * tok, wide), BF),
            exchange,
            exchange,
            pltpu.VMEM((4, nf * tok, wide), BF),
            pltpu.VMEM((2, ns * tok, HEAD), F32),
            pltpu.SemaphoreType.DMA((count,)),
            pltpu.SemaphoreType.DMA((count,)),
            pltpu.SemaphoreType.DMA((16,)),
        ]
        + lines.scratch(),
        compiler_params=params(1),
        name="forward",
    )(low, g_own, win, wout, *ws, wo, planes, lens)


TENSORS = 5
SMALL = 112


def back_lines(nf, wide, rest):
    counts = [rest] + [wide // LANES] * 3
    kinds = [((nf, D // nf, LANES), count, True) for count in counts]
    return Lines(nf, kinds + [((1, LANES, D), wide // LANES, False)])


def back_kernel(nf, ns, lines, *refs):
    att_ref, dq_ref, dk_ref, dv_ref, wqkv, wo_ref, p_in, g_ref = refs[:8]
    coef_ref, inv_ref, pre_ref, act_ref, mixed_ref, mix_in_ref, mix_out_ref = refs[8:15]
    again_ref, mgain_ref, xgain_ref = refs[15:18]
    sources, (pr_ref, py_ref, hist_ref, st_ref) = refs[18:22], refs[22:26]
    lo_ref, sm_out, hg_ref = refs[26:29]
    results, refs = refs[29:34], refs[34:]
    stage, part, sib, rec, grads, p_o, dx_ref, y_ref = refs[:8]
    hists, sts, hgs, h8, ds, dcoef, gsum = refs[8:15]
    sm_ref, sm_src, sm_in, sm_z, sm_sem, sm_rsem = refs[15:21]
    send_sem, recv_sem, copy_sem, tile_sem, credit = refs[21:26]
    line_refs = refs[26:]
    dmixed, last = dx_ref.at[0], dx_ref.at[1]
    plane = Plane(nf)
    sems = (send_sem, recv_sem)
    tok = lo_ref.shape[0]
    wide = wo_ref.shape[0]
    parts, sibs = part.shape[0], sib.shape[0]
    greet(nf, ns)
    built = lines.build(plane, ns, (p_in, *[grads.at[t] for t in range(3)], p_o), results, line_refs)
    jobs = []
    for line in built:
        jobs += [(line, chunk) for chunk in range(line.count)]
    ticks = Ticks(jobs, 1)
    small = Small(plane, ns, sm_src, sm_in, sm_z, sm_out, (sm_sem, sm_rsem))
    ticks.tick()
    load = pltpu.make_async_copy(sources[0], stage, copy_sem.at[0])
    load.start()
    pltpu.make_async_copy(hist_ref.at[HIST - 1], h8, copy_sem.at[1]).start()
    scats = [
        Scatter(
            plane,
            part.at[t % parts],
            sib.at[t % sibs],
            rec.at[t % sibs],
            sems,
            t * CHUNKS * (nf - 1),
            CHUNKS,
        )
        for t in range(TENSORS)
    ]
    firsts = (dq_ref, dk_ref, dv_ref)

    def total(t):
        def total_step(chunk):
            feats = tile(chunk, D // CHUNKS)
            if t < 4:
                dx_ref[t, :, feats] = scats[t].total(chunk)
            else:
                lo_ref[:, feats] = (y_ref[:, feats] + scats[t].total(chunk)).astype(BF)

        loop(CHUNKS, total_step)
        if t + sibs < TENSORS:
            for target in [plane.on(0, 1)] + [plane.on(k) for k in range(1, plane.chips)]:
                pl.semaphore_signal(
                    credit.at[t], inc=1, device_id={"fsdp": target}, device_id_type=MESH
                )

    def fetch(t, chunk):
        feats = slice(chunk * (D // CHUNKS), (chunk + 1) * (D // CHUNKS))
        src = (pr_ref, py_ref)[t - 3].at[:, :, feats]
        return pltpu.make_async_copy(src, scats[t].part.at[:, :, feats], copy_sem.at[2 + chunk])

    for t in range(TENSORS):
        if t >= sibs:
            pl.semaphore_wait(credit.at[t - sibs], plane.chips)
        if t >= 3:
            for chunk in range(CHUNKS):
                scats[t - parts].drain(chunk)
                fetch(t, chunk).start()
        for chunk in range(CHUNKS):
            feats = slice(chunk * (D // CHUNKS), (chunk + 1) * (D // CHUNKS))
            if t < 3:
                if t >= parts:
                    scats[t - parts].drain(chunk)
                value = dot(firsts[t][...], wqkv[t, feats, :], 1, 1)
                scats[t].part[:, :, feats] = value.astype(BF).reshape(nf, tok, D // CHUNKS)
            else:
                fetch(t, chunk).wait()
            if t == 4:
                value = dot(att_ref[...], wo_ref[:, feats]).reshape(nf, tok, D // CHUNKS)
                value = value + scats[t].part[:, :, feats].astype(F32)
                scats[t].part[:, :, feats] = value.astype(BF)
            scats[t].start(chunk)
            if chunk > 0:
                scats[t].combine(chunk - 1)
            if chunk % 2:
                ticks.tick()
        scats[t].combine(CHUNKS - 1)
        if t < 4:
            pltpu.make_async_copy(sources[t], stage, copy_sem.at[0]).wait()

            def grad_step(i, t=t):
                feats = tile(i, WIDTH)
                every = stage[:, :, feats].reshape(nf * tok, WIDTH)
                if t < 3:
                    grad = dot(every, firsts[t][...], 0, 0).astype(BF)
                    count = WIDTH * nf // D
                    for k in range(wide // LANES):
                        piece = grad[:, k * LANES : k * LANES + LANES]
                        piece = piece.reshape(count, D // nf, LANES)
                        grads[t, k, pl.ds(i * count, count)] = piece
                else:
                    grad = dot(att_ref[...], every, 0, 0).astype(BF)
                    for k in range(wide // LANES):
                        p_o[k, 0, :, feats] = grad[k * LANES : k * LANES + LANES]

            loop(D // WIDTH, grad_step)
            if t < 3:
                pltpu.make_async_copy(sources[t + 1], stage, copy_sem.at[0]).start()
        if t:
            total(t - 1)

    gsum[...] = jnp.zeros_like(gsum)
    steps = tok // ROWS

    def tiles_in(i, slot):
        rows = pl.ds(i * ROWS, ROWS)
        first = pltpu.make_async_copy(hist_ref.at[:, rows, :], hists.at[slot], tile_sem.at[slot])
        second = pltpu.make_async_copy(st_ref.at[:, rows, :], sts.at[slot], tile_sem.at[2 + slot])
        return first, second

    def tiles_out(i, slot):
        rows = pl.ds(i * ROWS, ROWS)
        dst = hg_ref.at[pl.ds(0, HIST - 1), rows, :]
        return pltpu.make_async_copy(hgs.at[slot], dst, tile_sem.at[4 + slot])

    def back(value, inv, gain, grad):
        scaled = grad * gain
        mean = jnp.sum(value * scaled, axis=1, keepdims=True) / D
        return inv * scaled - value * (inv * inv * inv * mean)

    def row_step(i, slot):
        rows = pl.ds(i * ROWS, ROWS)
        for copy in tiles_in(i, slot):
            copy.wait()
        if i + 1 < steps:
            for copy in tiles_in(i + 1, 1 - slot):
                copy.start()
        if i > 1:
            tiles_out(i - 2, slot).wait()
        coef = coef_ref[rows, :]
        lane = lax.broadcasted_iota(jnp.int32, (ROWS, STREAMS * HIST), 1)
        for c in range(STREAMS):
            value, inv = sts[slot, c], inv_ref[c, rows, :]
            grad = dx_ref[c, rows, :]
            gain = mgain_ref if c == STREAMS - 1 else again_ref
            gsum[c // 3] += grad * (value * inv)
            d_value = back(value, inv, gain[...], grad)
            if c == STREAMS - 1:
                d_value = d_value + g_ref[rows, :].astype(F32)
                y_ref[rows, :] = value
            ds[c] = d_value
        found = jnp.zeros((ROWS, STREAMS * HIST), F32)
        for j in range(HIST):
            sums = [jnp.zeros((ROWS, 128), F32)] * STREAMS
            for begin in range(0, D, WIDTH):
                cols = slice(begin, begin + WIDTH)
                entry = hists[slot, j, :, cols].astype(F32)
                grad = jnp.zeros((ROWS, WIDTH), F32)
                for c in range(STREAMS):
                    at = c * HIST + j
                    value = ds[c, :, cols]
                    grad = grad + coef[:, at : at + 1] * value
                    product = value * entry
                    for k in range(0, WIDTH, 128):
                        sums[c] = sums[c] + product[:, k : k + 128]
                if j < HIST - 1:
                    hgs[slot, j, :, cols] = grad.astype(BF)
                else:
                    last[rows, cols] = grad
            for c in range(STREAMS):
                value = jnp.sum(sums[c], axis=1, keepdims=True)
                found = jnp.where(lane == c * HIST + j, value, found)
        dcoef[rows, :] = found.astype(BF)
        tiles_out(i, slot).start()

    for copy in tiles_in(0, 0):
        copy.start()
    for i in range(steps):
        row_step(i, i % 2)
        if i % 2:
            ticks.tick()
    total(TENSORS - 1)
    mix_in, mix_out = mix_in_ref[...].astype(BF), mix_out_ref[...].astype(BF)
    pre, d_coef = pre_ref[...], dcoef[...]
    slope = 0.5 * (1.0 + lax.erf(pre * (0.5**0.5)))
    slope = slope + pre * jnp.exp(-0.5 * pre * pre) * 0.3989422804014327
    d_pre = (dot(d_coef, mix_out, 1, 1) * slope).astype(BF)
    hidden = pre.shape[1]
    sm_ref[0:hidden, :] = dot(d_pre, mixed_ref[...], 0, 0)
    dmixed[...] = dot(d_pre, mix_in, 1, 1)
    pltpu.make_async_copy(hist_ref.at[HIST - 1], h8, copy_sem.at[1]).wait()

    def last_step(i):
        rows = tile(i, ROWS)
        value, inv, grad = h8[rows, :].astype(F32), inv_ref[STREAMS, rows, :], dmixed[rows, :]
        gsum[2] += grad * (value * inv)
        h8[rows, :] = (last[rows, :] + back(value, inv, xgain_ref[...], grad)).astype(BF)

    loop(steps, last_step)
    end = pltpu.make_async_copy(h8, hg_ref.at[HIST - 1], copy_sem.at[1])
    end.start()
    for k in range(3):
        sm_ref[hidden + k : hidden + k + 1, :] = jnp.sum(gsum[k], axis=0, keepdims=True)
    begin = hidden + 3
    sm_ref[begin:SMALL, :] = jnp.zeros((SMALL - begin, D), F32)
    turned = dot(d_coef, act_ref[...], 0, 0)
    for k in range(STREAMS * HIST):
        at = begin + k // STREAMS
        cols = slice(k % STREAMS * (D // nf), k % STREAMS * (D // nf) + hidden)
        sm_ref[at : at + 1, cols] = turned[k : k + 1, :]
    for k in range(nf):
        sm_src[k] = sm_ref[:, k * (D // nf) : (k + 1) * (D // nf)]
    small.start()
    ticks.tick(2)
    small.across()
    ticks.tick(2)
    small.finish()
    ticks.finish()
    small.drain()
    for t in range(TENSORS - parts, TENSORS):
        loop(CHUNKS, scats[t].drain)
    end.wait()
    for i in (steps - 2, steps - 1):
        tiles_out(i, i % 2).wait()


def run_back(nf, ns, near, far):
    wo = near[5]
    tok = near[7].shape[0]
    wide = wo.shape[0]
    chips = nf // 2
    cols = D // nf
    count = TENSORS * CHUNKS * (nf - 1)
    few = 2 * (nf - 1) + ns - 1
    parts = 2 if nf <= 8 else 1
    lines = back_lines(nf, wide, near[6].shape[0])
    outs = [shape((tok, D)), shape((nf, SMALL, cols), F32), shape((HIST, tok, D))]
    return pl.pallas_call(
        partial(back_kernel, nf, ns, lines),
        out_shape=tuple(outs + lines.outs()),
        in_specs=[vmem()] * len(near) + [hbm()] * len(far),
        out_specs=(vmem(),) * 2 + (hbm(),) * 6,
        scratch_shapes=[
            pltpu.VMEM((nf, tok, D), BF),
            pltpu.VMEM((parts, nf, tok, D), BF),
            pltpu.VMEM((2, chips, tok, D), BF),
            pltpu.VMEM((2, chips - 1, tok, D), BF),
            pltpu.VMEM((3, wide // LANES, nf, D // nf, LANES), BF),
            pltpu.VMEM((wide // LANES, 1, LANES, D), BF),
            pltpu.VMEM((4, tok, D), F32),
            pltpu.VMEM((tok, D), F32),
            pltpu.VMEM((2, HIST, ROWS, D), BF),
            pltpu.VMEM((2, STREAMS, ROWS, D), F32),
            pltpu.VMEM((2, HIST - 1, ROWS, D), BF),
            pltpu.VMEM((tok, D), BF),
            pltpu.VMEM((STREAMS, ROWS, D), F32),
            pltpu.VMEM((tok, STREAMS * HIST), BF),
            pltpu.VMEM((3, ROWS, D), F32),
            pltpu.VMEM((SMALL, D), F32),
            pltpu.VMEM((nf, SMALL, cols), F32),
            pltpu.VMEM((nf, SMALL, cols), F32),
            pltpu.VMEM((ns, SMALL, cols), F32),
            pltpu.SemaphoreType.DMA((few,)),
            pltpu.SemaphoreType.DMA((few,)),
            pltpu.SemaphoreType.DMA((count,)),
            pltpu.SemaphoreType.DMA((count,)),
            pltpu.SemaphoreType.DMA((2 + CHUNKS,)),
            pltpu.SemaphoreType.DMA((6,)),
            pltpu.SemaphoreType.REGULAR((TENSORS - 2,)),
        ]
        + lines.scratch(),
        compiler_params=params(2, 63),
        name="back",
    )(*near, *far)


class Small:
    def __init__(self, plane, ns, src, mid, line, out, sems):
        self.plane, self.ns, self.src, self.mid, self.line, self.out = plane, ns, src, mid, line, out
        self.sems = sems
        self.me = lax.axis_index("seq")

    def scatter(self, step):
        target = wrap(self.plane.me + step, self.plane.nf)
        return send(
            self.src.at[target], self.mid.at[self.plane.me], self.sems, step - 1, "fsdp", target
        )

    def along(self, step):
        me = self.line.at[self.me]
        slot = self.plane.nf - 1 + step - 1
        return send(me, me, self.sems, slot, "seq", wrap(self.me + step, self.ns))

    def spread(self, step):
        me = self.out.at[self.plane.me]
        slot = self.plane.nf - 1 + self.ns - 1 + step - 1
        return send(me, me, self.sems, slot, "fsdp", wrap(self.plane.me + step, self.plane.nf))

    def start(self):
        self.mid[self.plane.me] = self.src[self.plane.me]
        for step in range(1, self.plane.nf):
            self.scatter(step).start()

    def across(self):
        for step in range(1, self.plane.nf):
            self.scatter(step).wait_recv()
        total = self.mid[0]
        for k in range(1, self.plane.nf):
            total += self.mid[k]
        self.line[self.me] = total
        for step in range(1, self.ns):
            self.along(step).start()

    def finish(self):
        for step in range(1, self.ns):
            self.along(step).wait_recv()
        total = self.line[0]
        for k in range(1, self.ns):
            total += self.line[k]
        self.out[self.plane.me] = total
        for step in range(1, self.plane.nf):
            self.spread(step).start()

    def drain(self):
        for step in range(1, self.plane.nf):
            self.spread(step).wait_recv()
        for step in range(1, self.plane.nf):
            self.scatter(step).wait_send()
            self.spread(step).wait_send()
        for step in range(1, self.ns):
            self.along(step).wait_send()


def finish_kernel(units, *refs):
    sum_in, sum_q, sum_k, sum_v, out_ref, sm_ref = refs[:6]
    w_in, wq, wk, wv, w_out, mix_in, mix_out, again, mgain, xgain = refs[6:]
    for dst, ref in ((w_in, sum_in), (wq, sum_q), (wk, sum_k), (wv, sum_v)):
        for k in range(ref.shape[0]):
            dst[:, k * LANES : (k + 1) * LANES] = ref[k, 0].astype(F32)
    w_out[...] = out_ref[...].astype(F32)
    mix_in[...] = sm_ref[0, 0:units, :]
    for k, dst in enumerate((again, mgain, xgain)):
        dst[...] = sm_ref[0, units + k : units + k + 1, :]

    @pl.when(pl.program_id(0) < STREAMS)
    def _():
        mix_out[0] = sm_ref[0, units + 3 : units + 3 + HIST, 0:LANES]


def run_finish(nf, units, turned, out, small):
    cols = D // nf
    hidden = out.shape[0]
    wide = turned[1].shape[0] * LANES
    rows = turned[0].shape[2]

    def chunks(part):
        return pl.BlockSpec((part.shape[0], 1, rows, LANES), lambda i: (0, i, 0, 0))

    def block(height, width):
        return pl.BlockSpec((height, width), lambda i: (0, i))

    return pl.pallas_call(
        partial(finish_kernel, units),
        grid=(nf,),
        out_shape=(
            shape((rows, nf * hidden), F32),
            *[shape((rows, D), F32)] * 3,
            shape((hidden, D), F32),
            shape((units, D), F32),
            shape((STREAMS, HIST, LANES), F32),
            *[shape((1, D), F32)] * 3,
        ),
        in_specs=[
            *[chunks(part) for part in turned],
            pl.BlockSpec((hidden // nf, D), lambda i: (i, 0)),
            pl.BlockSpec((1, SMALL, cols), lambda i: (i, 0, 0)),
        ],
        out_specs=(
            block(rows, hidden),
            *[block(rows, wide)] * 3,
            pl.BlockSpec((hidden // nf, D), lambda i: (i, 0)),
            block(units, cols),
            pl.BlockSpec((1, HIST, LANES), lambda i: (jnp.minimum(i, STREAMS - 1), 0, 0)),
            *[block(1, cols)] * 3,
        ),
        compiler_params=pltpu.CompilerParams(vmem_limit_bytes=40 * MIB),
        name="finish",
    )(*turned, out, small)


def local(
    nf,
    ns,
    history,
    cotangent,
    seq_lengths,
    wq,
    wk,
    wv,
    wo,
    w_in,
    w_out,
    mix_in,
    mix_out,
    attn_gain,
    mlp_gain,
    mix_gain,
):
    hist = history[:, 0]
    tok_rows = hist.shape[1]
    lens = lax.all_gather(seq_lengths, "fsdp", axis=0, tiled=True)
    slab_index = lax.axis_index("seq") * tok_rows + jnp.arange(tok_rows, dtype=jnp.int32)
    every_index = jnp.tile(slab_index, nf)
    _, place = token_marks(every_index, jnp.repeat(lens, tok_rows, axis=0))
    planes = rope_planes(place)
    gains = [g[None] for g in (attn_gain, mlp_gain, mix_gain)]
    low, stream, coef, inv, pre, act, mixed = run_start(hist, mix_in, mix_out, *gains)
    grad_out = cotangent[0]
    ws = [w.astype(BF) for w in (wq, wk, wv)]
    wo_low, win_low, wout_low = wo.astype(BF), w_in.astype(BF), w_out.astype(BF)
    *xgs, gg, pr, py, wqkv, p_in, sum_out, att, dq, dk, dv = run_forward(
        nf, ns, low, grad_out, win_low, wout_low, ws, wo_low, planes, lens
    )
    near = (att, dq, dk, dv, wqkv, wo_low, p_in, grad_out)
    near += (coef, inv, pre, act, mixed, mix_in, mix_out, *gains)
    far = (*xgs, gg, pr, py, hist, stream)
    layer_out, small, history_grad, sum_in, *sums, sum_o = run_back(nf, ns, near, far)
    dwo = sum_o.reshape(wo.shape).astype(F32)
    units = mix_in.shape[1]
    dw_in, dwq, dwk, dwv, dwout, dmix_in, dmix_out, *dgains = run_finish(
        nf, units, (sum_in, *sums), sum_out.reshape(w_out.shape), small
    )
    dmix_out = dmix_out.transpose(2, 1, 0).reshape(LANES, STREAMS * HIST)[:units]
    return (
        layer_out[None],
        history_grad[:, None],
        dwq,
        dwk,
        dwv,
        dwo,
        dw_in,
        dwout,
        dmix_in.T,
        dmix_out,
        *[grad[0] for grad in dgains],
    )


def solution(mesh):
    rows, rep = P("fsdp", None), P()
    in_specs = (
        P(None, "fsdp", "seq", None),
        P("fsdp", "seq", None),
    ) + (rows,) * 7 + (rep,) * 5
    out_specs = (
        P("fsdp", "seq", None),
        P(None, "fsdp", "seq", None),
    ) + (rows,) * 6 + (rep,) * 5
    body = partial(local, mesh.shape["fsdp"], mesh.shape["seq"])
    return jax.shard_map(body, mesh=mesh, in_specs=in_specs, out_specs=out_specs, check_vma=False)
```

```python
from functools import partial

import jax
import jax.numpy as jnp
from jax import lax
from jax.experimental import pallas as pl
from jax.experimental.pallas import tpu as pltpu
from jax.sharding import PartitionSpec as P

D = 2048
HEADS = 16
HEAD = 128
ROT = 32
HIST = 9
STREAMS = 4
EPSILON = 1e-05
NEGATIVE = -1e30
MESH = pl.DeviceIdType.MESH
BF = jnp.bfloat16
F32 = jnp.float32
MIB = 2**20


CHUNKS = 4
LANES = 128
SLOTS = 4


def token_marks(tok_index, lengths):
    first_end = lengths[..., 0]
    second_end = first_end + lengths[..., 1]
    segment = (tok_index >= first_end).astype(jnp.int32) + (tok_index >= second_end).astype(
        jnp.int32
    )
    seq_begin = jnp.where(segment == 0, 0, jnp.where(segment == 1, first_end, second_end))
    return (segment, tok_index - seq_begin)


def token_table(tok_index, lengths):
    _, place = token_marks(tok_index, lengths)
    inverse = 10000.0 ** (-jnp.arange(0, ROT, 2, dtype=F32) / ROT)
    angles = place.astype(F32)[:, None] * inverse[None, :]
    rows = place.shape[0]
    ends = jnp.stack([lengths[0], lengths[0] + lengths[1]]).astype(F32)
    ends = jnp.broadcast_to(ends[None], (rows, 2))
    rest = jnp.zeros((rows, LANES - ROT - 2), F32)
    return jnp.concatenate([jnp.cos(angles), jnp.sin(angles), ends, rest], axis=1)


def rope_planes(packed):
    lane = lax.broadcasted_iota(jnp.int32, packed.shape, 1)
    half = ROT // 2
    cosine = jnp.where(lane < ROT, pltpu.roll(packed, half, 1), 1.0)
    cosine = jnp.where(lane < half, packed, cosine)
    low = jnp.where(lane < half, -pltpu.roll(packed, HEAD - half, 1), 0.0)
    high = jnp.where((lane >= half) & (lane < ROT), packed, 0.0)
    return cosine, low, high


def dot(left_op, right_op, left_dim=1, right_dim=0):
    return lax.dot_general(
        left_op, right_op, (((left_dim,), (right_dim,)), ((), ())), preferred_element_type=F32
    )


def wrap(value, extent):
    return lax.rem(value + extent, extent)


def tile(index, extent):
    return pl.ds(pl.multiple_of(index * extent, extent), extent)


class Plane:
    def __init__(self, nf):
        self.nf = nf
        self.chips = nf // 2
        self.me = lax.axis_index("fsdp")
        self.chip = self.me // 2
        self.core = lax.rem(self.me, 2)

    def on(self, step, other=0):
        core = 1 - self.core if other else self.core
        return wrap(self.chip + step, self.chips) * 2 + core


def greet(nf, ns=1):
    barrier = pltpu.get_barrier_semaphore()
    for axis, extent in (("fsdp", nf), ("seq", ns)):
        for step in range(1, extent):
            pl.semaphore_signal(
                barrier,
                inc=1,
                device_id={axis: wrap(lax.axis_index(axis) + step, extent)},
                device_id_type=MESH,
            )
    pl.semaphore_wait(barrier, nf - 1 + ns - 1)


def send(src, dst, sems, slot, axis, target):
    return pltpu.make_async_remote_copy(
        src_ref=src,
        dst_ref=dst,
        send_sem=sems[0].at[slot],
        recv_sem=sems[1].at[slot],
        device_id={axis: target},
        device_id_type=MESH,
    )


class Gather:
    def __init__(self, plane, own, buf, sems, base):
        self.plane, self.own, self.buf, self.sems, self.base = plane, own, buf, sems, base

    def direct(self, step, slot=None):
        dst = self.buf.at[self.plane.me if slot is None else slot]
        src = self.own if slot is None else dst
        return send(src, dst, self.sems, self.base + step - 1, "fsdp", self.plane.on(step))

    def across(self, step, slot=None):
        slot = self.plane.on(-step) if slot is None else slot
        block = self.buf.at[slot]
        src = block if step else self.own
        base = self.base + self.plane.chips - 1
        return send(src, block, self.sems, base + step, "fsdp", self.plane.on(0, 1))

    def start(self):
        for step in range(1, self.plane.chips):
            self.direct(step).start()
        self.across(0).start()

    def keep(self, sem):
        return pltpu.make_async_copy(self.own, self.buf.at[self.plane.me], sem)

    def forward(self):
        for step in range(1, self.plane.chips):
            self.direct(step, self.plane.on(-step)).wait_recv()
            self.across(step).start()

    def finish(self):
        for step in range(self.plane.chips):
            self.across(step, self.plane.on(-step, 1)).wait_recv()

    def drain(self):
        for step in range(1, self.plane.chips):
            self.direct(step).wait_send()
        for step in range(self.plane.chips):
            self.across(step).wait_send()


class Turn:
    def __init__(self, plane, rows_ref, full_ref, sems, base, chunks):
        self.plane, self.sems, self.base, self.chunks = plane, sems, base, chunks
        self.rows_ref, self.full_ref = rows_ref, full_ref
        self.height = rows_ref.shape[0]
        self.width = full_ref.shape[1]
        self.part = self.width // chunks

    def copy(self, chunk, step, source=None):
        nf = self.plane.nf
        target = wrap(self.plane.me + step, nf)
        source = self.plane.me if source is None else source
        begin = pl.multiple_of(target * self.width + chunk * self.part, self.part)
        return send(
            self.rows_ref.at[:, pl.ds(begin, self.part)],
            self.full_ref.at[tile(source, self.height), tile(chunk, self.part)],
            self.sems,
            self.base + chunk * (nf - 1) + step - 1,
            "fsdp",
            target,
        )

    def start(self, chunk):
        for step in range(1, self.plane.nf):
            self.copy(chunk, step).start()

    def keep(self, sem):
        return pltpu.make_async_copy(
            self.rows_ref.at[:, tile(self.plane.me, self.width)],
            self.full_ref.at[tile(self.plane.me, self.height), :],
            sem,
        )

    def arrive(self, chunk):
        for step in range(1, self.plane.nf):
            self.copy(chunk, step, wrap(self.plane.me - step, self.plane.nf)).wait_recv()

    def drain(self, chunk):
        for step in range(1, self.plane.nf):
            self.copy(chunk, step).wait_send()


class Scatter:
    def __init__(self, plane, part, sib, rec, sems, base, chunks):
        self.plane, self.part, self.sib, self.rec = plane, part, sib, rec
        self.sems, self.base, self.chunks = sems, base, chunks
        self.width = part.shape[-1] // chunks

    def across(self, chunk, step):
        cols = tile(chunk, self.width)
        return send(
            self.part.at[self.plane.on(step, 1), :, cols],
            self.sib.at[wrap(self.plane.chip + step, self.plane.chips), :, cols],
            self.sems,
            self.base + chunk * (self.plane.nf - 1) + step,
            "fsdp",
            self.plane.on(0, 1),
        )

    def direct(self, chunk, step):
        cols = tile(chunk, self.width)
        return send(
            self.part.at[self.plane.on(step), :, cols],
            self.rec.at[step - 1, :, cols],
            self.sems,
            self.base + chunk * (self.plane.nf - 1) + self.plane.chips + step - 1,
            "fsdp",
            self.plane.on(step),
        )

    def start(self, chunk):
        for step in range(self.plane.chips):
            self.across(chunk, step).start()

    def combine(self, chunk):
        cols = tile(chunk, self.width)
        for step in range(1, self.plane.chips):
            chip = wrap(self.plane.chip + step, self.plane.chips)
            mine = self.plane.on(step)
            self.across(chunk, step).wait_recv()
            total = self.part[mine, :, cols].astype(F32) + self.sib[chip, :, cols].astype(F32)
            self.part[mine, :, cols] = total.astype(BF)
            self.direct(chunk, step).start()
        self.across(chunk, 0).wait_recv()

    def total(self, chunk):
        cols = tile(chunk, self.width)
        total = self.part[self.plane.me, :, cols].astype(F32)
        total += self.sib[self.plane.chip, :, cols].astype(F32)
        for step in range(1, self.plane.chips):
            self.direct(chunk, step).wait_recv()
            total += self.rec[step - 1, :, cols].astype(F32)
        return total

    def drain(self, chunk):
        for step in range(self.plane.chips):
            self.across(chunk, step).wait_send()
        for step in range(1, self.plane.chips):
            self.direct(chunk, step).wait_send()


def loop(extent, body):
    lax.fori_loop(0, extent, lambda i, c: (body(i), c)[1], 0)


def rows_of(ref3, begin, count):
    value = ref3[pl.ds(begin, count)]
    return value.reshape(count * value.shape[1], value.shape[2])


def vmem():
    return pl.BlockSpec(memory_space=pltpu.VMEM)


def hbm():
    return pl.BlockSpec(memory_space=pltpu.HBM)


def shape(dims, dtype=BF):
    return jax.ShapeDtypeStruct(tuple(dims), dtype)


def params(ident, limit=62):
    return pltpu.CompilerParams(
        collective_id=ident, has_side_effects=True, vmem_limit_bytes=limit * MIB
    )


ROWS = 16
WIDTH = 512


def rotated(value, planes):
    return value * planes[0] + pltpu.roll(value, HEAD - ROT // 2, 1) * planes[1] + pltpu.roll(
        value, ROT // 2, 1
    ) * planes[2]


def rotated_back(value, planes):
    return value * planes[0] - pltpu.roll(value, HEAD - ROT // 2, 1) * planes[1] - pltpu.roll(
        value, ROT // 2, 1
    ) * planes[2]


class Exchange:
    def __init__(self, ns, sems, base):
        self.ns, self.sems, self.base = ns, sems, base
        self.me = lax.axis_index("seq")

    def copy(self, src, dst, lane, step):
        return send(
            src,
            dst,
            self.sems,
            self.base + lane * (self.ns - 1) + step - 1,
            "seq",
            wrap(self.me + step, self.ns),
        )


class Line:
    def __init__(self, plane, ns, part, inward, swap, res, sems, base, turned, copy_sem, credits):
        self.plane, self.ns, self.turned = plane, ns, turned
        self.part, self.inward, self.swap, self.res = part, inward, swap, res
        self.sems, self.base, self.copy_sem, self.credits = sems, base, copy_sem, credits
        self.me = lax.axis_index("seq")
        self.side = self.me // (ns // 2)
        middle = ns // 2 - 1
        self.depth = (1 - self.side) * (middle - self.me) + self.side * (self.me - middle - 1)
        self.ends = middle
        self.in_to = self.me + 1 - 2 * self.side
        self.out_to = self.me - 1 + 2 * self.side
        self.other = ns - 1 - self.me
        self.count = res.shape[0]
        self.slots = inward.shape[0]
        if self.ends != 1 and self.slots < self.count:
            raise ValueError("slots")

    @staticmethod
    def marks(nf, turned):
        return 5 + (nf - 1 if turned else 0)

    def sem(self, chunk, kind):
        return self.base + chunk * self.marks(self.plane.nf, self.turned) + kind

    def half(self, ref, chunk, side):
        rows = ref.shape[-2] // 2
        rows = pl.ds(pl.multiple_of(side * rows, rows), rows)
        return ref.at[chunk, :, rows, :]

    def inner(self, chunk, relayed=False):
        slot = chunk % self.slots
        src = self.inward.at[slot] if relayed else self.part.at[chunk]
        return send(src, self.inward.at[slot], self.sems, self.sem(chunk, 0), "seq", self.in_to)

    def cross(self, chunk):
        slot = chunk % self.slots
        return send(
            self.half(self.inward, slot, 1 - self.side),
            self.swap.at[slot],
            self.sems,
            self.sem(chunk, 1),
            "seq",
            self.other,
        )

    def result(self):
        return self.res if self.turned else self.part

    def back_cross(self, chunk, side=None):
        side = self.side if side is None else side
        return send(
            self.half(self.result(), chunk, side),
            self.half(self.res, chunk, side),
            self.sems,
            self.sem(chunk, 2),
            "seq",
            self.other,
        )

    def outer(self, chunk, side, src):
        return send(
            self.half(src, chunk, side),
            self.half(self.res, chunk, side),
            self.sems,
            self.sem(chunk, 3) + side,
            "seq",
            self.out_to,
        )

    def spread(self, chunk, step, source=None):
        rows = self.part.shape[-2] // 2
        rows = pl.ds(pl.multiple_of(self.side * rows, rows), rows)
        target = wrap(self.plane.me + step, self.plane.nf)
        source = self.plane.me if source is None else source
        return send(
            self.part.at[chunk, target, rows, :],
            self.res.at[chunk, source, rows, :],
            self.sems,
            self.sem(chunk, 4) + step,
            "fsdp",
            target,
        )

    def keep(self, chunk):
        if self.turned:
            rows = self.part.shape[-2] // 2
            rows = pl.ds(pl.multiple_of(self.side * rows, rows), rows)
            me = self.plane.me
            src, dst = self.part.at[chunk, me, rows, :], self.res.at[chunk, me, rows, :]
        else:
            src = self.half(self.part, chunk, self.side)
            dst = self.half(self.res, chunk, self.side)
        return pltpu.make_async_copy(src, dst, self.copy_sem.at[chunk])

    def begin(self, chunk):
        if self.ends:

            @pl.when(self.depth == self.ends)
            def _():
                if chunk >= self.slots:
                    pl.semaphore_wait(self.credits.at[0], 1)
                self.inner(chunk).start()

    def relay(self, chunk, hop):
        slot = chunk % self.slots

        @pl.when(self.depth == self.ends - hop)
        def _():
            self.inner(chunk).wait_recv()
            total = self.inward[slot].astype(F32) + self.part[chunk].astype(F32)
            self.inward[slot] = total.astype(BF)
            self.inner(chunk, True).start()

    def meet(self, chunk):
        slot = chunk % self.slots

        @pl.when(self.depth == 0)
        def _():
            self.inner(chunk).wait_recv()
            theirs = self.half(self.inward, slot, 1 - self.side)
            mine = self.half(self.part, chunk, 1 - self.side)

            def step(i):
                rows = tile(i, 16)
                total = theirs[:, rows, :].astype(F32) + mine[:, rows, :].astype(F32)
                theirs[:, rows, :] = total.astype(BF)

            loop(theirs.shape[1] // 16, step)
            if chunk >= self.slots:
                pl.semaphore_wait(self.credits.at[1], 1)
            self.cross(chunk).start()

    def settle(self, chunk):
        slot = chunk % self.slots

        @pl.when(self.depth == 0)
        def _():
            self.cross(chunk).wait_recv()
            theirs = self.half(self.inward, slot, self.side)
            mine = self.half(self.part, chunk, self.side)

            def step(i):
                rows = tile(i, 16)
                total = theirs[:, rows, :].astype(F32) + mine[:, rows, :].astype(F32)
                total += self.swap[slot, :, rows, :].astype(F32)
                mine[:, rows, :] = total.astype(BF)

            loop(theirs.shape[1] // 16, step)
            self.keep(chunk).start()
            if self.turned:
                for k in range(1, self.plane.nf):
                    self.spread(chunk, k).start()
            else:
                self.hand_out(chunk)
            self.cross(chunk).wait_send()
            if chunk + self.slots < self.count:
                pl.semaphore_signal(
                    self.credits.at[0], inc=1, device_id={"seq": self.out_to}, device_id_type=MESH
                )
                pl.semaphore_signal(
                    self.credits.at[1], inc=1, device_id={"seq": self.other}, device_id_type=MESH
                )

    def hand_out(self, chunk):
        self.back_cross(chunk).start()
        if self.ends:
            self.outer(chunk, self.side, self.result()).start()

    def spread_end(self, chunk):
        @pl.when(self.depth == 0)
        def _():
            for k in range(1, self.plane.nf):
                self.spread(chunk, k, wrap(self.plane.me - k, self.plane.nf)).wait_recv()
            self.keep(chunk).wait()
            self.hand_out(chunk)

    def pass_on(self, chunk):
        @pl.when(self.depth == 0)
        def _():
            self.back_cross(chunk, 1 - self.side).wait_recv()
            if self.ends:
                self.outer(chunk, 1 - self.side, self.res).start()

    def outward_hop(self, chunk, hop):
        @pl.when(self.depth == hop)
        def _():
            for side in range(2):
                self.outer(chunk, side, self.res).wait_recv()
                self.outer(chunk, side, self.res).start()

    def pause(self, chunk):
        pass

    def phases(self):
        listed = [partial(self.relay, hop=hop) for hop in range(1, self.ends)]
        listed += [self.meet, self.settle]
        if self.turned:
            listed += [self.pause, self.spread_end]
        listed += [self.pass_on]
        listed += [partial(self.outward_hop, hop=hop) for hop in range(1, self.ends)]
        return listed

    def drain(self, chunk):
        @pl.when(self.depth == 0)
        def _():
            self.back_cross(chunk).wait_send()
            if self.turned:
                for k in range(1, self.plane.nf):
                    self.spread(chunk, k).wait_send()
            else:
                self.keep(chunk).wait()

        if self.ends:

            @pl.when(self.depth == self.ends)
            def _():
                for side in range(2):
                    self.outer(chunk, side, self.res).wait_recv()

            @pl.when(self.depth < self.ends)
            def _():
                for side in range(2):
                    self.outer(chunk, side, self.res).wait_send()

            @pl.when(self.depth > 0)
            def _():
                self.inner(chunk).wait_send()


class Ticks:
    def __init__(self, jobs, lead):
        self.jobs, self.lead = jobs, lead
        self.now, self.begun = 0, 0

    def open(self):
        line, chunk = self.jobs[self.begun]
        line.begin(chunk)
        self.begun += 1

    def tick(self, times=1):
        for _ in range(times):
            while self.begun < min(len(self.jobs), self.now + self.lead + 1):
                line, chunk = self.jobs[self.begun]
                line.begin(chunk)
                self.begun += 1
            for i, (line, chunk) in enumerate(self.jobs):
                phase = self.now - i - 1
                if 0 <= phase < len(line.phases()):
                    line.phases()[phase](chunk)
            self.now += 1

    def finish(self):
        depth = max(len(line.phases()) for line, _ in self.jobs)
        while self.now < len(self.jobs) + depth:
            self.tick()
        for line, chunk in self.jobs:
            line.drain(chunk)


class Lines:
    def __init__(self, nf, kinds):
        self.nf, self.kinds = nf, kinds

    def scratch(self):
        listed = []
        for (blocks, rows, cols), count, _ in self.kinds:
            slots = min(count, SLOTS)
            listed.append(pltpu.VMEM((slots, blocks, rows, cols), BF))
            listed.append(pltpu.VMEM((slots, blocks, rows // 2, cols), BF))
            listed.append(pltpu.SemaphoreType.DMA((count,)))
            listed.append(pltpu.SemaphoreType.REGULAR((2,)))
        marks = sum(count * Line.marks(self.nf, turned) for _, count, turned in self.kinds)
        return listed + [pltpu.SemaphoreType.DMA((marks,))] * 2

    def count(self):
        return 4 * len(self.kinds) + 2

    def outs(self):
        return [shape((count,) + dims) for dims, count, _ in self.kinds]

    def build(self, plane, ns, parts, results, scratch):
        lines, base = [], 0
        sems = tuple(scratch[-2:])
        for k, (_, count, turned) in enumerate(self.kinds):
            inward, swap, copy_sem, credits = scratch[4 * k : 4 * k + 4]
            lines.append(
                Line(
                    plane,
                    ns,
                    parts[k],
                    inward,
                    swap,
                    results[k],
                    sems,
                    base,
                    turned,
                    copy_sem,
                    credits,
                )
            )
            base += count * Line.marks(self.nf, turned)
        return lines


def forward_lines(nf, wide, hidden):
    width = hidden // CHUNKS
    return Lines(nf, [((1, width, D * LANES // width), hidden // LANES, False)])


def forward_kernel(nf, ns, lines, *refs):
    hist_ref, g_ref, win_ref, wq_ref, wk_ref, wv_ref, wo_f32, wout_f32 = refs[:8]
    tab_ref, mix_in_ref, mix_out_ref, again_ref, mgain_ref, xgain_ref = refs[8:14]
    refs = refs[14:]
    (xq_out, xk_out, xv_out, gg_out, py_out, w_out, rest_in) = refs[:7]
    wo_out, wrow_out, win_out, st_out, sum_out = refs[7:12]
    att_ref, dq_ref, dk_ref, dv_ref, dxr_ref = refs[12:17]
    coef_ref, inv_ref, pre_ref, act_ref, mixed_ref = refs[17:22]
    refs = refs[22:]
    (xr, gg, wfull, hid, dup, p_out, p_in, stage, wqkv, zin, zback, dkv) = refs[:12]
    wout_ref, wo_ref, wtile, sts, lows, h8, tab, sib, rec = refs[12:21]
    send_sem, recv_sem, copy_sem = refs[21:24]
    line_refs = refs[24:]
    plane = Plane(nf)
    sems = (send_sem, recv_sem)
    tok = g_ref.shape[0]
    wide = wo_ref.shape[0]
    heads = wide // HEAD
    per = nf // ns
    slab = per * tok
    group_tok = ns * tok
    sq = lax.axis_index("seq")
    width = wfull.shape[1] // CHUNKS
    blocks = min(4, nf)
    pieces = width // LANES
    step_sems = nf - 1
    greet(nf, ns)
    (l_out,) = lines.build(plane, ns, (p_out,), (sum_out,), line_refs)
    ticks = Ticks([(l_out, chunk) for chunk in range(l_out.count)], 1)
    ag_r = Gather(plane, xr.at[plane.me], xr, sems, 0)
    ag_x = [
        Gather(plane, out.at[plane.me], out, sems, (2 + i) * step_sems)
        for i, out in enumerate((xq_out, xk_out, xv_out))
    ]
    turn = Turn(plane, win_out, wfull, sems, 5 * step_sems, CHUNKS)
    turns = [
        Turn(plane, wrow_out.at[i], wqkv.at[i], sems, (5 + CHUNKS + i) * step_sems, 1)
        for i in range(3)
    ]
    ag_t = Gather(plane, tab_ref, tab, sems, (8 + CHUNKS) * step_sems)
    scat = Scatter(plane, xr, sib, rec, sems, (9 + CHUNKS) * step_sems, CHUNKS)
    base = (9 + 2 * CHUNKS) * step_sems
    part_cols = D // pieces
    ag_gs = []
    for p in range(pieces):
        cols = slice(p * part_cols, (p + 1) * part_cols)
        at = base + (p - 1) * step_sems if p else step_sems
        ag_gs.append(Gather(plane, g_ref.at[:, cols], gg.at[:, :, cols], sems, at))
    base += (pieces - 1) * step_sems
    there = Exchange(ns, sems, base)
    home = Exchange(ns, sems, base + 4 * (ns - 1))
    late = HIST - 1
    entries = pltpu.make_async_copy(hist_ref.at[pl.ds(0, late)], stage.at[pl.ds(0, late)], copy_sem.at[5])
    newest = pltpu.make_async_copy(hist_ref.at[late], h8, copy_sem.at[6])
    newest.start()
    entries.start()
    ag_gs[0].start()
    keeps = [ag_gs[p].keep(copy_sem.at[8 + p]) for p in range(pieces)]
    keeps.append(ag_t.keep(copy_sem.at[7]))
    for keep in keeps:
        keep.start()
    high, broad = width, part_cols

    def tiles_of(src, dst, store):
        for r in range(0, src.shape[0], high):
            for c in range(0, src.shape[1], broad):
                where = (pl.ds(r, high), pl.ds(c, broad))
                casts.append((src.at[where], dst.at[where], store))

    def fetch(n):
        return pltpu.make_async_copy(casts[n][0], wtile.at[n % 2], copy_sem.at[16 + n % 2])

    def cast_all():
        stores = []
        fetch(0).start()
        fetch(1).start()
        for n, (_, dst, store) in enumerate(casts):
            fetch(n).wait()
            low = p_out.at[len(stores), 0] if store else dst

            def cast_step(i, n=n, low=low):
                rows = tile(i, ROWS)
                low[rows, :] = wtile[n % 2, rows, :].astype(BF)

            loop(high // ROWS, cast_step)
            if n + 2 < len(casts):
                fetch(n + 2).start()
            if store:
                stores.append(pltpu.make_async_copy(low, dst, copy_sem.at[18 + len(stores)]))
                stores[-1].start()
        for copy in stores:
            copy.wait()

    casts = []
    tiles_of(win_ref, win_out, True)
    cast_all()
    turn.start(0)
    keeps.append(turn.keep(copy_sem.at[1]))
    keeps[-1].start()
    newest.wait()

    def mix_step(i):
        rows = tile(i, ROWS)
        value = h8[rows, :].astype(F32)
        inv = lax.rsqrt(jnp.mean(value * value, axis=1, keepdims=True) + EPSILON)
        mixed_ref[rows, :] = (value * inv * xgain_ref[...]).astype(BF)
        inv_ref[STREAMS, rows, :] = inv

    loop(tok // ROWS, mix_step)
    pre = dot(mixed_ref[...], mix_in_ref[...].astype(BF), 1, 1)
    pre_ref[...] = pre
    act = (0.5 * pre * (1.0 + lax.erf(pre * (0.5**0.5)))).astype(BF)
    act_ref[...] = act
    coef_ref[...] = dot(act, mix_out_ref[...].astype(BF), 1, 1)
    entries.wait()

    def tiles_out(i, slot):
        rows = tile(i, ROWS)
        listed = [pltpu.make_async_copy(sts.at[slot], st_out.at[:, rows, :], copy_sem.at[26 + slot])]
        for c, out in enumerate((xq_out, xk_out, xv_out)):
            dst = out.at[plane.me, rows, :]
            sem = copy_sem.at[28 + c * 2 + slot]
            listed.append(pltpu.make_async_copy(lows.at[slot, c], dst, sem))
        return listed

    def stream_step(i):
        slot = lax.rem(i, 2)
        rows = tile(i, ROWS)

        @pl.when(i > 1)
        def _():
            for copy in tiles_out(i - 2, slot):
                copy.wait()

        coef = coef_ref[rows, :]
        squares = [jnp.zeros((ROWS, 1), F32)] * STREAMS
        for begin in range(0, D, WIDTH):
            cols = slice(begin, begin + WIDTH)
            total = [jnp.zeros((ROWS, WIDTH), F32)] * STREAMS
            for j in range(HIST):
                entry = (stage[j, rows, cols] if j < late else h8[rows, cols]).astype(F32)
                for c in range(STREAMS):
                    at = c * HIST + j
                    total[c] = total[c] + coef[:, at : at + 1] * entry
            for c in range(STREAMS):
                sts[slot, c, :, cols] = total[c]
                squares[c] = squares[c] + jnp.sum(total[c] * total[c], axis=1, keepdims=True)
        for c in range(STREAMS):
            inv = lax.rsqrt(squares[c] / D + EPSILON)
            inv_ref[c, rows, :] = inv
            gain = mgain_ref if c == STREAMS - 1 else again_ref
            normed = (sts[slot, c] * inv * gain[...]).astype(BF)
            if c < STREAMS - 1:
                lows[slot, c] = normed
            else:
                xr[plane.me, rows, :] = normed
        for copy in tiles_out(i, slot):
            copy.start()

    steps = tok // ROWS
    loop(steps, stream_step)
    ag_r.start()
    for p in range(1, pieces):
        ag_gs[p].start()
    for chunk in range(1, CHUNKS):
        turn.start(chunk)
    ag_t.start()
    for i in (steps - 2, steps - 1):
        for copy in tiles_out(i, i % 2):
            copy.wait()
    ag_x[0].start()
    casts = []
    tiles_of(wout_f32, wout_ref, False)
    tiles_of(wo_f32, wo_ref, False)
    for i, w in enumerate((wq_ref, wk_ref, wv_ref)):
        tiles_of(w, wrow_out.at[i], True)
    cast_all()
    for i in range(3):
        if i:
            ag_x[i].start()
        turns[i].start(0)
        keeps.append(turns[i].keep(copy_sem.at[2 + i]))
        keeps[-1].start()
    ag_gs[0].forward()
    ag_r.forward()
    ag_gs[0].finish()
    ag_r.finish()
    for keep in keeps:
        keep.wait()
    saves, started = [], []

    def save(src, dst):
        started.append(dst)
        saves.append(pltpu.make_async_copy(src, dst, copy_sem.at[36 + len(started)]))
        saves[-1].start()

    save(wo_ref, wo_out)

    def act(up):
        return 0.5 * (1.0 + lax.erf(up * (0.5**0.5)))

    def out_grad(chunk, p):
        cols = slice(chunk * width, chunk * width + width)

        def step(i):
            feats = pl.ds(pl.multiple_of(p * part_cols + i * WIDTH, WIDTH), WIDTH)
            every = gg[:, :, feats].reshape(nf * tok, WIDTH)
            grad = dot(hid[:, cols], every, 0, 0).astype(BF)
            p_out[chunk * pieces + p, 0, :, tile(i, WIDTH)] = grad

        loop(part_cols // WIDTH, step)

    def first_step(i):
        rows = tile(i, blocks * tok)
        up = dot(rows_of(xr, i * blocks, blocks), wfull[:, 0:width])
        hid[rows, 0:width] = (up * act(up)).astype(BF)

    turn.arrive(0)
    loop(nf // blocks, first_step)
    out_grad(0, 0)
    ticks.open()
    for p in range(1, pieces):
        ag_gs[p].forward()
        ag_gs[p].finish()
    save(gg, gg_out)

    for chunk in range(CHUNKS):
        if chunk:
            turn.arrive(chunk)
        cols = slice(chunk * width, chunk * width + width)

        def rows_step(i, cols=cols):
            rows = tile(i, blocks * tok)
            up = dot(rows_of(xr, i * blocks, blocks), wfull[:, cols])
            dh = dot(rows_of(gg, i * blocks, blocks), wout_ref[cols, :], 1, 1)
            cdf = act(up)
            slope = cdf + up * jnp.exp(-0.5 * up * up) * 0.3989422804014327
            hid[rows, cols] = (up * cdf).astype(BF)
            dup[rows, cols] = (dh * slope).astype(BF)

        loop(nf // blocks, rows_step)

        for p in range(1 if chunk == 0 else 0, pieces):
            out_grad(chunk, p)
        ticks.tick()

        def grad_step(i, cols=cols, chunk=chunk):
            feats = tile(i, WIDTH)
            every = xr[:, :, feats].reshape(nf * tok, WIDTH)
            grad = dot(every, dup[:, cols], 0, 0).astype(BF)
            count = WIDTH * nf // D
            for k in range(pieces):
                piece = grad[:, k * LANES : k * LANES + LANES].reshape(count, D // nf, LANES)
                p_in[chunk * pieces + k, pl.ds(i * count, count)] = piece

        loop(D // WIDTH, grad_step)

    save(p_in, rest_in)

    def scatter_step(chunk):
        feats = tile(chunk, D // CHUNKS)
        value = dot(dup[...], wfull[feats, :], 1, 1).astype(BF)
        xr[:, :, feats] = value.reshape(nf, tok, D // CHUNKS)
        scat.start(chunk)

    ag_r.drain()
    loop(CHUNKS, scatter_step)

    def lane(i):
        return slice(i * wide, (i + 1) * wide)

    def ship(i):
        for step in range(1, ns):
            target = wrap(sq + step, ns)
            there.copy(dup.at[tile(target, slab), lane(i)], zin.at[i, sq], i, step).start()
        zin[i, sq] = dup[tile(sq, slab), lane(i)]

    def da_step(i):
        rows = tile(i, blocks * tok)
        dup[rows, lane(3)] = dot(rows_of(gg, i * blocks, blocks), wo_ref[...], 1, 1).astype(BF)

    loop(nf // blocks, da_step)
    ship(3)
    loop(CHUNKS, scat.combine)
    ticks.tick()
    ag_t.forward()
    ag_t.finish()
    for i in range(3):
        ag_x[i].forward()
        turns[i].arrive(0)
        ag_x[i].finish()
        load = pltpu.make_async_copy(ag_x[i].buf, stage, copy_sem.at[15])
        load.start()
        load.wait()

        def lin_step(r, i=i):
            rows = tile(r, blocks * tok)
            lin = dot(rows_of(stage, r * blocks, blocks), wqkv[i])
            if i < 2:
                planes = rope_planes(rows_of(tab, r * blocks, blocks))
            for head in range(heads):
                piece = lin[:, head * HEAD : head * HEAD + HEAD]
                if i < 2:
                    piece = rotated(piece, planes)
                at = i * wide + head * HEAD
                dup[rows, at : at + HEAD] = piece.astype(BF)

        loop(nf // blocks, lin_step)
        ship(i)
        ticks.tick(2 if i < 2 else 1)
    save(wqkv, w_out)

    def out_step(i):
        feats = tile(i, WIDTH)
        value = dot(hid[...], wout_ref[:, feats]).astype(BF)
        stage[:, :, feats] = value.reshape(nf, tok, WIDTH)

    loop(D // WIDTH, out_step)
    save(stage, py_out)
    for i in range(4):
        for step in range(1, ns):
            there.copy(zin.at[i, 0], zin.at[i, wrap(sq - step, ns)], i, step).wait_recv()

    scale = HEAD ** (-0.5)
    queries = min(256, group_tok)
    q_slabs = queries // tok

    def pair_step(pair):
        grp = pair // heads
        head = lax.rem(pair, heads)
        cols = tile(head, HEAD)
        toks = tile(grp, tok)
        marks = tab[sq * per + grp, 0:1, :]
        first_end, second_end = marks[:, ROT : ROT + 1], marks[:, ROT + 1 : ROT + 2]

        def part_of(i, begin, count):
            return zin[i, pl.ds(begin, count), toks, cols].reshape(count * tok, HEAD)

        def keep_rows(i, begin, count, value):
            at = pl.ds(pl.multiple_of(i * wide + head * HEAD, HEAD), HEAD)
            for k in range(count):
                rows = pl.ds(pl.multiple_of((begin + k) * slab + grp * tok, tok), tok)
                hid[rows, at] = value[k * tok : (k + 1) * tok].astype(BF)

        keys, values = part_of(1, 0, ns), part_of(2, 0, ns)
        dkv[...] = jnp.zeros_like(dkv)

        def query_step(j):
            begin = j * q_slabs
            query, d_att = part_of(0, begin, q_slabs), part_of(3, begin, q_slabs)
            qi = j * queries + lax.broadcasted_iota(jnp.int32, (queries, group_tok), 0)
            ki = lax.broadcasted_iota(jnp.int32, (queries, group_tok), 1)
            qf, kf = qi.astype(F32), ki.astype(F32)
            seg_q = (qf >= first_end).astype(jnp.int32) + (qf >= second_end).astype(jnp.int32)
            seg_k = (kf >= first_end).astype(jnp.int32) + (kf >= second_end).astype(jnp.int32)
            allowed = (seg_q == seg_k) & (qi >= ki)
            scores = jnp.where(allowed, dot(query, keys, 1, 1) * scale, NEGATIVE)
            top = jnp.max(scores, axis=1, keepdims=True)
            expo = jnp.where(allowed, jnp.exp(scores - top), 0.0)
            prob = expo / jnp.sum(expo, axis=1, keepdims=True)
            prob_low = prob.astype(BF)
            attended = dot(prob_low, values)
            delta = jnp.sum(d_att.astype(F32) * attended, axis=1, keepdims=True)
            d_score = (prob * (dot(d_att, values, 1, 1) - delta)).astype(BF)
            d_query = dot(d_score, keys) * scale
            dkv[0] += dot(d_score, query, 0, 0)
            dkv[1] += dot(prob_low, d_att, 0, 0)
            keep_rows(0, begin, q_slabs, attended)
            keep_rows(1, begin, q_slabs, d_query)

        loop(group_tok // queries, query_step)
        keep_rows(2, 0, ns, dkv[0] * scale)
        keep_rows(3, 0, ns, dkv[1])

    loop(per * heads, pair_step)

    for i in (1, 2, 3, 0):
        for step in range(1, ns):
            target = wrap(sq + step, ns)
            src = hid.at[tile(target, slab), lane(i)]
            home.copy(src, zback.at[i, tile(sq, slab), :], i, step).start()
        zback[i, tile(sq, slab), :] = hid[tile(sq, slab), lane(i)]
    ticks.tick()
    outs = (att_ref, dq_ref, dk_ref, dv_ref)
    for i in (1, 2, 3, 0):
        for step in range(1, ns):
            source = wrap(sq - step, ns)
            dst = zback.at[i, tile(source, slab), :]
            home.copy(dst, dst, i, step).wait_recv()
        if i in (1, 2):

            def back_step(r, i=i):
                rows = tile(r, tok)
                planes = rope_planes(tab[r])
                for head in range(heads):
                    cols = slice(head * HEAD, head * HEAD + HEAD)
                    piece = zback[i, rows, cols].astype(F32)
                    piece = rotated_back(piece, planes)
                    zback[i, rows, cols] = piece.astype(BF)

            loop(nf, back_step)
        save(zback.at[i], outs[i])
        ticks.tick()

    def total_step(chunk):
        value = scat.total(chunk)
        sts[:, :, :, tile(chunk, D // CHUNKS)] = value.reshape(*sts.shape[:3], D // CHUNKS)
        scat.drain(chunk)

    loop(CHUNKS, total_step)
    save(sts, dxr_ref)
    ticks.finish()
    for gather in (*ag_gs, ag_t, *ag_x):
        gather.drain()
    for chunk in range(CHUNKS):
        turn.drain(chunk)
    for i in range(3):
        turns[i].drain(0)
    for copy in saves:
        copy.wait()
    for i in range(4):
        for step in range(1, ns):
            there.copy(zin.at[i, 0], zin.at[i, 0], i, step).wait_send()
            home.copy(zin.at[i, 0], zin.at[i, 0], i, step).wait_send()


def run_forward(nf, ns, hist, g_own, win, ws, wo, wout, table, mixing):
    tok = g_own.shape[0]
    hidden = wout.shape[0]
    wide = wo.shape[0]
    units = mixing[0].shape[0]
    lines = forward_lines(nf, wide, hidden)
    count = (8 + 2 * CHUNKS + hidden // CHUNKS // LANES) * (nf - 1) + 8 * (ns - 1)
    flat = shape((nf * tok, wide))
    block = shape((nf, tok, D))
    total = CHUNKS * (hidden // CHUNKS // LANES)
    outs = [block] * 5 + [shape((3, D, wide)), shape((total, nf, D // nf, LANES))]
    outs += [shape((wide, D)), shape((3, wide, D)), shape(win.shape)]
    outs += [shape((STREAMS, tok, D), F32)]
    slots = tok // STREAMS // ROWS
    outs += lines.outs() + [flat] * 4 + [shape((slots, STREAMS, ROWS, D), F32)]
    outs += [shape((tok, STREAMS * HIST), F32), shape((STREAMS + 1, tok, 1), F32)]
    outs += [shape((tok, units), F32), shape((tok, units)), shape((tok, D))]
    exchange = pltpu.VMEM((4, ns, nf // ns * tok, wide), BF)
    return pl.pallas_call(
        partial(forward_kernel, nf, ns, lines),
        out_shape=tuple(outs),
        in_specs=[hbm()] * 8 + [vmem()] * 6,
        out_specs=(hbm(),) * 17 + (vmem(),) * 5,
        scratch_shapes=[
            pltpu.VMEM((nf, tok, D), BF),
            pltpu.VMEM((nf, tok, D), BF),
            pltpu.VMEM((D, hidden), BF),
            pltpu.VMEM((nf * tok, hidden), BF),
            pltpu.VMEM((nf * tok, hidden), BF),
            pltpu.VMEM(lines.outs()[0].shape, BF),
            pltpu.VMEM((total, nf, D // nf, LANES), BF),
            pltpu.VMEM((nf, tok, D), BF),
            pltpu.VMEM((3, D, wide), BF),
            exchange,
            pltpu.VMEM((4, nf * tok, wide), BF),
            pltpu.VMEM((2, ns * tok, HEAD), F32),
            pltpu.VMEM((hidden, D), BF),
            pltpu.VMEM((wide, D), BF),
            pltpu.VMEM((2,) + lines.kinds[0][0][1:], F32),
            pltpu.VMEM((slots, STREAMS, ROWS, D), F32),
            pltpu.VMEM((2, STREAMS - 1, ROWS, D), BF),
            pltpu.VMEM((tok, D), BF),
            pltpu.VMEM((nf, tok, LANES), F32),
            pltpu.VMEM((nf // 2, tok, D), BF),
            pltpu.VMEM((nf // 2 - 1, tok, D), BF),
            pltpu.SemaphoreType.DMA((count,)),
            pltpu.SemaphoreType.DMA((count,)),
            pltpu.SemaphoreType.DMA((48,)),
        ]
        + lines.scratch(),
        compiler_params=params(1, 63),
        name="forward",
    )(hist, g_own, win, *ws, wo, wout, table, *mixing)


TENSORS = 4
SMALL = 112


def back_lines(nf, wide, rest):
    counts = [rest] + [wide // LANES] * 3
    kinds = [((nf, D // nf, LANES), count, True) for count in counts]
    return Lines(nf, kinds + [((1, LANES, D), wide // LANES, False)])


def back_kernel(nf, ns, lines, *refs):
    att_ref, dq_ref, dk_ref, dv_ref, wqkv, wo_ref, p_in, g_ref = refs[:8]
    coef_ref, inv_ref, pre_ref, act_ref, mixed_ref, mix_in_ref, mix_out_ref = refs[8:15]
    again_ref, mgain_ref, xgain_ref = refs[15:18]
    sources, (dxr_ref, py_ref, hist_ref, st_ref) = refs[18:22], refs[22:26]
    lo_ref, sm_out, hg_ref = refs[26:29]
    results, refs = refs[29:34], refs[34:]
    stage, part, sib, rec, grads, p_o, dx_ref, y_ref = refs[:8]
    hists, sts, hgs, h8, ds, dcoef, gsum = refs[8:15]
    sm_ref, sm_src, sm_in, sm_z, sm_sem, sm_rsem = refs[15:21]
    send_sem, recv_sem, copy_sem, tile_sem, credit = refs[21:26]
    line_refs = refs[26:]
    dmixed, last = dx_ref.at[0], dx_ref.at[1]
    plane = Plane(nf)
    sems = (send_sem, recv_sem)
    tok = lo_ref.shape[0]
    wide = wo_ref.shape[0]
    parts, sibs = part.shape[0], sib.shape[0]
    greet(nf, ns)
    built = lines.build(plane, ns, (p_in, *[grads.at[t] for t in range(3)], p_o), results, line_refs)
    jobs = []
    for line in built:
        jobs += [(line, chunk) for chunk in range(line.count)]
    ticks = Ticks(jobs, 1)
    small = Small(plane, ns, sm_src, sm_in, sm_z, sm_out, (sm_sem, sm_rsem))
    ticks.tick()
    load = pltpu.make_async_copy(sources[0], stage, copy_sem.at[0])
    load.start()
    pltpu.make_async_copy(hist_ref.at[HIST - 1], h8, copy_sem.at[1]).start()
    extra = pltpu.make_async_copy(dxr_ref, dx_ref.at[3], copy_sem.at[2 + CHUNKS])
    extra.start()
    scats = [
        Scatter(
            plane,
            part.at[t % parts],
            sib.at[t % sibs],
            rec.at[t % sibs],
            sems,
            t * CHUNKS * (nf - 1),
            CHUNKS,
        )
        for t in range(TENSORS)
    ]
    firsts = (dq_ref, dk_ref, dv_ref)

    def total(t):
        def total_step(chunk):
            feats = tile(chunk, D // CHUNKS)
            if t < 3:
                dx_ref[t, :, feats] = scats[t].total(chunk)
            else:
                lo_ref[:, feats] = (y_ref[:, feats] + scats[t].total(chunk)).astype(BF)

        loop(CHUNKS, total_step)
        if t + sibs < TENSORS:
            for target in [plane.on(0, 1)] + [plane.on(k) for k in range(1, plane.chips)]:
                pl.semaphore_signal(
                    credit.at[t], inc=1, device_id={"fsdp": target}, device_id_type=MESH
                )

    def fetch(t, chunk):
        feats = slice(chunk * (D // CHUNKS), (chunk + 1) * (D // CHUNKS))
        return pltpu.make_async_copy(py_ref.at[:, :, feats], scats[t].part.at[:, :, feats], copy_sem.at[2 + chunk])

    for t in range(TENSORS):
        if t >= sibs:
            pl.semaphore_wait(credit.at[t - sibs], plane.chips)
        if t >= 3:
            for chunk in range(CHUNKS):
                scats[t - parts].drain(chunk)
                fetch(t, chunk).start()
        for chunk in range(CHUNKS):
            feats = slice(chunk * (D // CHUNKS), (chunk + 1) * (D // CHUNKS))
            if t < 3:
                if t >= parts:
                    scats[t - parts].drain(chunk)
                value = dot(firsts[t][...], wqkv[t, feats, :], 1, 1)
                scats[t].part[:, :, feats] = value.astype(BF).reshape(nf, tok, D // CHUNKS)
            else:
                fetch(t, chunk).wait()
            if t == 3:
                value = dot(att_ref[...], wo_ref[:, feats]).reshape(nf, tok, D // CHUNKS)
                value = value + scats[t].part[:, :, feats].astype(F32)
                scats[t].part[:, :, feats] = value.astype(BF)
            scats[t].start(chunk)
            if chunk > 0:
                scats[t].combine(chunk - 1)
            if chunk % 2:
                ticks.tick()
        scats[t].combine(CHUNKS - 1)
        if t < TENSORS:
            pltpu.make_async_copy(sources[t], stage, copy_sem.at[0]).wait()

            def grad_step(i, t=t):
                feats = tile(i, WIDTH)
                every = stage[:, :, feats].reshape(nf * tok, WIDTH)
                if t < 3:
                    grad = dot(every, firsts[t][...], 0, 0).astype(BF)
                    count = WIDTH * nf // D
                    for k in range(wide // LANES):
                        piece = grad[:, k * LANES : k * LANES + LANES]
                        piece = piece.reshape(count, D // nf, LANES)
                        grads[t, k, pl.ds(i * count, count)] = piece
                else:
                    grad = dot(att_ref[...], every, 0, 0).astype(BF)
                    for k in range(wide // LANES):
                        p_o[k, 0, :, feats] = grad[k * LANES : k * LANES + LANES]

            loop(D // WIDTH, grad_step)
            if t < 3:
                pltpu.make_async_copy(sources[t + 1], stage, copy_sem.at[0]).start()
        if t:
            total(t - 1)

    extra.wait()
    gsum[...] = jnp.zeros_like(gsum)
    steps = tok // ROWS

    def tiles_in(i, slot):
        rows = pl.ds(i * ROWS, ROWS)
        first = pltpu.make_async_copy(hist_ref.at[:, rows, :], hists.at[slot], tile_sem.at[slot])
        second = pltpu.make_async_copy(st_ref.at[:, rows, :], sts.at[slot], tile_sem.at[2 + slot])
        return first, second

    def tiles_out(i, slot):
        rows = pl.ds(i * ROWS, ROWS)
        dst = hg_ref.at[pl.ds(0, HIST - 1), rows, :]
        return pltpu.make_async_copy(hgs.at[slot], dst, tile_sem.at[4 + slot])

    def back(value, inv, gain, grad):
        scaled = grad * gain
        mean = jnp.sum(value * scaled, axis=1, keepdims=True) / D
        return inv * scaled - value * (inv * inv * inv * mean)

    def row_step(i, slot):
        rows = pl.ds(i * ROWS, ROWS)
        for copy in tiles_in(i, slot):
            copy.wait()
        if i + 1 < steps:
            for copy in tiles_in(i + 1, 1 - slot):
                copy.start()
        if i > 1:
            tiles_out(i - 2, slot).wait()
        coef = coef_ref[rows, :]
        lane = lax.broadcasted_iota(jnp.int32, (ROWS, STREAMS * HIST), 1)
        for c in range(STREAMS):
            value, inv = sts[slot, c], inv_ref[c, rows, :]
            grad = dx_ref[c, rows, :]
            gain = mgain_ref if c == STREAMS - 1 else again_ref
            gsum[c // 3] += grad * (value * inv)
            d_value = back(value, inv, gain[...], grad)
            if c == STREAMS - 1:
                d_value = d_value + g_ref[rows, :].astype(F32)
                y_ref[rows, :] = value
            ds[c] = d_value
        found = jnp.zeros((ROWS, STREAMS * HIST), F32)
        for j in range(HIST):
            sums = [jnp.zeros((ROWS, 128), F32)] * STREAMS
            for begin in range(0, D, WIDTH):
                cols = slice(begin, begin + WIDTH)
                entry = hists[slot, j, :, cols].astype(F32)
                grad = jnp.zeros((ROWS, WIDTH), F32)
                for c in range(STREAMS):
                    at = c * HIST + j
                    value = ds[c, :, cols]
                    grad = grad + coef[:, at : at + 1] * value
                    product = value * entry
                    for k in range(0, WIDTH, 128):
                        sums[c] = sums[c] + product[:, k : k + 128]
                if j < HIST - 1:
                    hgs[slot, j, :, cols] = grad.astype(BF)
                else:
                    last[rows, cols] = grad
            for c in range(STREAMS):
                value = jnp.sum(sums[c], axis=1, keepdims=True)
                found = jnp.where(lane == c * HIST + j, value, found)
        dcoef[rows, :] = found.astype(BF)
        tiles_out(i, slot).start()

    for copy in tiles_in(0, 0):
        copy.start()
    for i in range(steps):
        row_step(i, i % 2)
        if i % 2:
            ticks.tick()
    total(TENSORS - 1)
    mix_in, mix_out = mix_in_ref[...].astype(BF), mix_out_ref[...].astype(BF)
    pre, d_coef = pre_ref[...], dcoef[...]
    slope = 0.5 * (1.0 + lax.erf(pre * (0.5**0.5)))
    slope = slope + pre * jnp.exp(-0.5 * pre * pre) * 0.3989422804014327
    d_pre = (dot(d_coef, mix_out) * slope).astype(BF)
    hidden = pre.shape[1]
    sm_ref[0:hidden, :] = dot(d_pre, mixed_ref[...], 0, 0)
    dmixed[...] = dot(d_pre, mix_in)
    pltpu.make_async_copy(hist_ref.at[HIST - 1], h8, copy_sem.at[1]).wait()

    def last_step(i):
        rows = tile(i, ROWS)
        value, inv, grad = h8[rows, :].astype(F32), inv_ref[STREAMS, rows, :], dmixed[rows, :]
        gsum[2] += grad * (value * inv)
        h8[rows, :] = (last[rows, :] + back(value, inv, xgain_ref[...], grad)).astype(BF)

    loop(steps, last_step)
    end = pltpu.make_async_copy(h8, hg_ref.at[HIST - 1], copy_sem.at[1])
    end.start()
    for k in range(3):
        sm_ref[hidden + k : hidden + k + 1, :] = jnp.sum(gsum[k], axis=0, keepdims=True)
    begin = hidden + 3
    sm_ref[begin:SMALL, :] = jnp.zeros((SMALL - begin, D), F32)
    turned = dot(d_coef, act_ref[...], 0, 0)
    for k in range(STREAMS * HIST):
        at = begin + k // STREAMS
        cols = slice(k % STREAMS * (D // nf), k % STREAMS * (D // nf) + hidden)
        sm_ref[at : at + 1, cols] = turned[k : k + 1, :]
    for k in range(nf):
        sm_src[k] = sm_ref[:, k * (D // nf) : (k + 1) * (D // nf)]
    small.start()
    ticks.tick(2)
    small.across()
    ticks.tick(2)
    small.finish()
    ticks.finish()
    small.drain()
    for t in range(TENSORS - parts, TENSORS):
        loop(CHUNKS, scats[t].drain)
    end.wait()
    for i in (steps - 2, steps - 1):
        tiles_out(i, i % 2).wait()


def run_back(nf, ns, near, far):
    wo = near[5]
    tok = near[7].shape[0]
    wide = wo.shape[0]
    chips = nf // 2
    cols = D // nf
    count = TENSORS * CHUNKS * (nf - 1)
    few = 2 * (nf - 1) + ns - 1
    parts = 2 if nf <= 8 else 1
    lines = back_lines(nf, wide, near[6].shape[0])
    outs = [shape((tok, D)), shape((nf, SMALL, cols), F32), shape((HIST, tok, D))]
    return pl.pallas_call(
        partial(back_kernel, nf, ns, lines),
        out_shape=tuple(outs + lines.outs()),
        in_specs=[vmem()] * len(near) + [hbm()] * len(far),
        out_specs=(vmem(),) * 2 + (hbm(),) * 6,
        scratch_shapes=[
            pltpu.VMEM((nf, tok, D), BF),
            pltpu.VMEM((parts, nf, tok, D), BF),
            pltpu.VMEM((2, chips, tok, D), BF),
            pltpu.VMEM((2, chips - 1, tok, D), BF),
            pltpu.VMEM((3, wide // LANES, nf, D // nf, LANES), BF),
            pltpu.VMEM((wide // LANES, 1, LANES, D), BF),
            pltpu.VMEM((4, tok, D), F32),
            pltpu.VMEM((tok, D), F32),
            pltpu.VMEM((2, HIST, ROWS, D), BF),
            pltpu.VMEM((2, STREAMS, ROWS, D), F32),
            pltpu.VMEM((2, HIST - 1, ROWS, D), BF),
            pltpu.VMEM((tok, D), BF),
            pltpu.VMEM((STREAMS, ROWS, D), F32),
            pltpu.VMEM((tok, STREAMS * HIST), BF),
            pltpu.VMEM((3, ROWS, D), F32),
            pltpu.VMEM((SMALL, D), F32),
            pltpu.VMEM((nf, SMALL, cols), F32),
            pltpu.VMEM((nf, SMALL, cols), F32),
            pltpu.VMEM((ns, SMALL, cols), F32),
            pltpu.SemaphoreType.DMA((few,)),
            pltpu.SemaphoreType.DMA((few,)),
            pltpu.SemaphoreType.DMA((count,)),
            pltpu.SemaphoreType.DMA((count,)),
            pltpu.SemaphoreType.DMA((3 + CHUNKS,)),
            pltpu.SemaphoreType.DMA((6,)),
            pltpu.SemaphoreType.REGULAR((TENSORS - 2,)),
        ]
        + lines.scratch(),
        compiler_params=params(2, 63),
        name="back",
    )(*near, *far)


class Small:
    def __init__(self, plane, ns, src, mid, line, out, sems):
        self.plane, self.ns, self.src, self.mid, self.line, self.out = plane, ns, src, mid, line, out
        self.sems = sems
        self.me = lax.axis_index("seq")

    def scatter(self, step):
        target = wrap(self.plane.me + step, self.plane.nf)
        return send(
            self.src.at[target], self.mid.at[self.plane.me], self.sems, step - 1, "fsdp", target
        )

    def along(self, step):
        me = self.line.at[self.me]
        slot = self.plane.nf - 1 + step - 1
        return send(me, me, self.sems, slot, "seq", wrap(self.me + step, self.ns))

    def spread(self, step):
        me = self.out.at[self.plane.me]
        slot = self.plane.nf - 1 + self.ns - 1 + step - 1
        return send(me, me, self.sems, slot, "fsdp", wrap(self.plane.me + step, self.plane.nf))

    def start(self):
        self.mid[self.plane.me] = self.src[self.plane.me]
        for step in range(1, self.plane.nf):
            self.scatter(step).start()

    def across(self):
        for step in range(1, self.plane.nf):
            self.scatter(step).wait_recv()
        total = self.mid[0]
        for k in range(1, self.plane.nf):
            total += self.mid[k]
        self.line[self.me] = total
        for step in range(1, self.ns):
            self.along(step).start()

    def finish(self):
        for step in range(1, self.ns):
            self.along(step).wait_recv()
        total = self.line[0]
        for k in range(1, self.ns):
            total += self.line[k]
        self.out[self.plane.me] = total
        for step in range(1, self.plane.nf):
            self.spread(step).start()

    def drain(self):
        for step in range(1, self.plane.nf):
            self.spread(step).wait_recv()
        for step in range(1, self.plane.nf):
            self.scatter(step).wait_send()
            self.spread(step).wait_send()
        for step in range(1, self.ns):
            self.along(step).wait_send()


def finish_kernel(units, *refs):
    sum_in, sum_q, sum_k, sum_v, out_ref, sm_ref, sum_o = refs[:7]
    w_in, wq, wk, wv, w_out, mix_in, mix_out, again, mgain, xgain, wo = refs[7:]
    for dst, ref in ((w_in, sum_in), (wq, sum_q), (wk, sum_k), (wv, sum_v)):
        for k in range(ref.shape[0]):
            dst[:, k * LANES : (k + 1) * LANES] = ref[k, 0].astype(F32)
    part = out_ref.shape[-1]
    for k in range(out_ref.shape[1]):
        w_out[:, k * part : (k + 1) * part] = out_ref[0, k].astype(F32)
    mix_in[...] = sm_ref[0, 0:units, :]
    for k, dst in enumerate((again, mgain, xgain)):
        dst[...] = sm_ref[0, units + k : units + k + 1, :]

    @pl.when(pl.program_id(0) == 0)
    def _():
        wo[...] = sum_o[...].astype(F32)

    @pl.when(pl.program_id(0) < STREAMS)
    def _():
        mix_out[0] = sm_ref[0, units + 3 : units + 3 + HIST, 0:LANES]


def run_finish(nf, units, turned, out, small, sum_o):
    cols = D // nf
    _, pieces, width, part = out.shape
    hidden = out.shape[0] * width
    high = hidden // nf
    wide = turned[1].shape[0] * LANES
    rows = turned[0].shape[2]

    def chunks(part):
        return pl.BlockSpec((part.shape[0], 1, rows, LANES), lambda i: (0, i, 0, 0))

    def block(height, width):
        return pl.BlockSpec((height, width), lambda i: (0, i))

    return pl.pallas_call(
        partial(finish_kernel, units),
        grid=(nf,),
        out_shape=(
            shape((rows, nf * hidden), F32),
            *[shape((rows, D), F32)] * 3,
            shape((hidden, D), F32),
            shape((units, D), F32),
            shape((STREAMS, HIST, LANES), F32),
            *[shape((1, D), F32)] * 3,
            shape((sum_o.shape[0], D), F32),
        ),
        in_specs=[
            *[chunks(part) for part in turned],
            pl.BlockSpec(
                (1, pieces, high, part),
                lambda i: (i * high // width, 0, lax.rem(i, width // high), 0),
            ),
            pl.BlockSpec((1, SMALL, cols), lambda i: (i, 0, 0)),
            pl.BlockSpec((sum_o.shape[0], D), lambda i: (0, 0)),
        ],
        out_specs=(
            block(rows, hidden),
            *[block(rows, wide)] * 3,
            pl.BlockSpec((hidden // nf, D), lambda i: (i, 0)),
            block(units, cols),
            pl.BlockSpec((1, HIST, LANES), lambda i: (jnp.minimum(i, STREAMS - 1), 0, 0)),
            *[block(1, cols)] * 3,
            pl.BlockSpec((sum_o.shape[0], D), lambda i: (0, 0)),
        ),
        compiler_params=pltpu.CompilerParams(vmem_limit_bytes=62 * MIB),
        name="finish",
    )(*turned, out, small, sum_o)


def local(
    nf,
    ns,
    history,
    cotangent,
    seq_lengths,
    wq,
    wk,
    wv,
    wo,
    w_in,
    w_out,
    mix_in,
    mix_out,
    attn_gain,
    mlp_gain,
    mix_gain,
):
    hist = history[:, 0]
    tok_rows = hist.shape[1]
    tok_index = lax.axis_index("seq") * tok_rows + jnp.arange(tok_rows, dtype=jnp.int32)
    table = token_table(tok_index, seq_lengths[0])
    grad_out = cotangent[0]
    mixing = (mix_in.T, mix_out.T, attn_gain[None], mlp_gain[None], mix_gain[None])
    outs = run_forward(
        nf, ns, hist, grad_out, w_in, (wq, wk, wv), wo, w_out, table, mixing
    )
    xgs, (gg, py, wqkv, p_in, wo_low, _, _, stream, sum_out) = outs[:3], outs[3:12]
    (att, dq, dk, dv, dxr), mixed = outs[12:17], outs[17:]
    dxr = dxr.reshape(tok_rows, D)
    near = (att, dq, dk, dv, wqkv, wo_low, p_in, grad_out, *mixed, *mixing)
    far = (*xgs, gg, dxr, py, hist, stream)
    layer_out, small, history_grad, sum_in, *sums, sum_o = run_back(nf, ns, near, far)
    units = mix_in.shape[1]
    dw_in, dwq, dwk, dwv, dwout, dmix_in, dmix_out, *dgains, dwo = run_finish(
        nf, units, (sum_in, *sums), sum_out.reshape(CHUNKS, -1, *sum_out.shape[2:]), small, sum_o.reshape(wo.shape)
    )
    dmix_out = dmix_out.transpose(2, 1, 0).reshape(LANES, STREAMS * HIST)[:units]
    return (
        layer_out[None],
        history_grad[:, None],
        dwq,
        dwk,
        dwv,
        dwo,
        dw_in,
        dwout,
        dmix_in.T,
        dmix_out,
        *[grad[0] for grad in dgains],
    )


def solution(mesh):
    rows, rep = P("fsdp", None), P()
    in_specs = (
        P(None, "fsdp", "seq", None),
        P("fsdp", "seq", None),
    ) + (rows,) * 7 + (rep,) * 5
    out_specs = (
        P("fsdp", "seq", None),
        P(None, "fsdp", "seq", None),
    ) + (rows,) * 6 + (rep,) * 5
    body = partial(local, mesh.shape["fsdp"], mesh.shape["seq"])
    return jax.shard_map(body, mesh=mesh, in_specs=in_specs, out_specs=out_specs, check_vma=False)
```

```python
from functools import partial

import jax
import jax.numpy as jnp
from jax import lax
from jax.experimental import pallas as pl
from jax.experimental.pallas import tpu as pltpu
from jax.sharding import PartitionSpec as P

D = 2048
HEADS = 16
HEAD = 128
ROT = 32
HIST = 9
STREAMS = 4
EPSILON = 1e-05
NEGATIVE = -1e30
MESH = pl.DeviceIdType.MESH
BF = jnp.bfloat16
F32 = jnp.float32
MIB = 2**20


CHUNKS = 4
LANES = 128
SLOTS = 4


def token_marks(tok_index, lengths):
    first_end = lengths[..., 0]
    second_end = first_end + lengths[..., 1]
    segment = (tok_index >= first_end).astype(jnp.int32) + (tok_index >= second_end).astype(
        jnp.int32
    )
    seq_begin = jnp.where(segment == 0, 0, jnp.where(segment == 1, first_end, second_end))
    return (segment, tok_index - seq_begin)


def token_table(tok_index, lengths):
    _, place = token_marks(tok_index, lengths)
    inverse = 10000.0 ** (-jnp.arange(0, ROT, 2, dtype=F32) / ROT)
    angles = place.astype(F32)[:, None] * inverse[None, :]
    rows = place.shape[0]
    ends = jnp.stack([lengths[0], lengths[0] + lengths[1]]).astype(F32)
    ends = jnp.broadcast_to(ends[None], (rows, 2))
    rest = jnp.zeros((rows, LANES - ROT - 2), F32)
    return jnp.concatenate([jnp.cos(angles), jnp.sin(angles), ends, rest], axis=1)


def rope_planes(packed):
    lane = lax.broadcasted_iota(jnp.int32, packed.shape, 1)
    half = ROT // 2
    cosine = jnp.where(lane < ROT, pltpu.roll(packed, half, 1), 1.0)
    cosine = jnp.where(lane < half, packed, cosine)
    low = jnp.where(lane < half, -pltpu.roll(packed, HEAD - half, 1), 0.0)
    high = jnp.where((lane >= half) & (lane < ROT), packed, 0.0)
    return cosine, low, high


def dot(left_op, right_op, left_dim=1, right_dim=0):
    return lax.dot_general(
        left_op, right_op, (((left_dim,), (right_dim,)), ((), ())), preferred_element_type=F32
    )


def wrap(value, extent):
    return lax.rem(value + extent, extent)


def tile(index, extent):
    return pl.ds(pl.multiple_of(index * extent, extent), extent)


class Plane:
    def __init__(self, nf):
        self.nf = nf
        self.chips = nf // 2
        self.me = lax.axis_index("fsdp")
        self.chip = self.me // 2
        self.core = lax.rem(self.me, 2)

    def on(self, step, other=0):
        core = 1 - self.core if other else self.core
        return wrap(self.chip + step, self.chips) * 2 + core


def greet(nf, ns=1):
    barrier = pltpu.get_barrier_semaphore()
    for axis, extent in (("fsdp", nf), ("seq", ns)):
        for step in range(1, extent):
            pl.semaphore_signal(
                barrier,
                inc=1,
                device_id={axis: wrap(lax.axis_index(axis) + step, extent)},
                device_id_type=MESH,
            )
    pl.semaphore_wait(barrier, nf - 1 + ns - 1)


def send(src, dst, sems, slot, axis, target):
    return pltpu.make_async_remote_copy(
        src_ref=src,
        dst_ref=dst,
        send_sem=sems[0].at[slot],
        recv_sem=sems[1].at[slot],
        device_id={axis: target},
        device_id_type=MESH,
    )


class Gather:
    def __init__(self, plane, own, buf, sems, base):
        self.plane, self.own, self.buf, self.sems, self.base = plane, own, buf, sems, base

    def direct(self, step, slot=None):
        dst = self.buf.at[self.plane.me if slot is None else slot]
        src = self.own if slot is None else dst
        return send(src, dst, self.sems, self.base + step - 1, "fsdp", self.plane.on(step))

    def across(self, step, slot=None):
        slot = self.plane.on(-step) if slot is None else slot
        block = self.buf.at[slot]
        src = block if step else self.own
        base = self.base + self.plane.chips - 1
        return send(src, block, self.sems, base + step, "fsdp", self.plane.on(0, 1))

    def start(self):
        for step in range(1, self.plane.chips):
            self.direct(step).start()
        self.across(0).start()

    def keep(self, sem):
        return pltpu.make_async_copy(self.own, self.buf.at[self.plane.me], sem)

    def forward(self):
        for step in range(1, self.plane.chips):
            self.direct(step, self.plane.on(-step)).wait_recv()
            self.across(step).start()

    def finish(self):
        for step in range(self.plane.chips):
            self.across(step, self.plane.on(-step, 1)).wait_recv()

    def drain(self):
        for step in range(1, self.plane.chips):
            self.direct(step).wait_send()
        for step in range(self.plane.chips):
            self.across(step).wait_send()


class Turn:
    def __init__(self, plane, rows_ref, full_ref, sems, base, chunks):
        self.plane, self.sems, self.base, self.chunks = plane, sems, base, chunks
        self.rows_ref, self.full_ref = rows_ref, full_ref
        self.height = rows_ref.shape[0]
        self.width = full_ref.shape[1]
        self.part = self.width // chunks

    def copy(self, chunk, step, source=None):
        nf = self.plane.nf
        target = wrap(self.plane.me + step, nf)
        source = self.plane.me if source is None else source
        begin = pl.multiple_of(target * self.width + chunk * self.part, self.part)
        return send(
            self.rows_ref.at[:, pl.ds(begin, self.part)],
            self.full_ref.at[tile(source, self.height), tile(chunk, self.part)],
            self.sems,
            self.base + chunk * (nf - 1) + step - 1,
            "fsdp",
            target,
        )

    def start(self, chunk):
        for step in range(1, self.plane.nf):
            self.copy(chunk, step).start()

    def keep(self, sem):
        return pltpu.make_async_copy(
            self.rows_ref.at[:, tile(self.plane.me, self.width)],
            self.full_ref.at[tile(self.plane.me, self.height), :],
            sem,
        )

    def arrive(self, chunk):
        for step in range(1, self.plane.nf):
            self.copy(chunk, step, wrap(self.plane.me - step, self.plane.nf)).wait_recv()

    def drain(self, chunk):
        for step in range(1, self.plane.nf):
            self.copy(chunk, step).wait_send()


class Scatter:
    def __init__(self, plane, part, sib, rec, sems, base, chunks):
        self.plane, self.part, self.sib, self.rec = plane, part, sib, rec
        self.sems, self.base, self.chunks = sems, base, chunks
        self.width = part.shape[-1] // chunks

    def across(self, chunk, step):
        cols = tile(chunk, self.width)
        return send(
            self.part.at[self.plane.on(step, 1), :, cols],
            self.sib.at[wrap(self.plane.chip + step, self.plane.chips), :, cols],
            self.sems,
            self.base + chunk * (self.plane.nf - 1) + step,
            "fsdp",
            self.plane.on(0, 1),
        )

    def direct(self, chunk, step):
        cols = tile(chunk, self.width)
        return send(
            self.part.at[self.plane.on(step), :, cols],
            self.rec.at[step - 1, :, cols],
            self.sems,
            self.base + chunk * (self.plane.nf - 1) + self.plane.chips + step - 1,
            "fsdp",
            self.plane.on(step),
        )

    def start(self, chunk):
        for step in range(self.plane.chips):
            self.across(chunk, step).start()

    def combine(self, chunk):
        cols = tile(chunk, self.width)
        for step in range(1, self.plane.chips):
            chip = wrap(self.plane.chip + step, self.plane.chips)
            mine = self.plane.on(step)
            self.across(chunk, step).wait_recv()
            total = self.part[mine, :, cols].astype(F32) + self.sib[chip, :, cols].astype(F32)
            self.part[mine, :, cols] = total.astype(BF)
            self.direct(chunk, step).start()
        self.across(chunk, 0).wait_recv()

    def total(self, chunk):
        cols = tile(chunk, self.width)
        total = self.part[self.plane.me, :, cols].astype(F32)
        total += self.sib[self.plane.chip, :, cols].astype(F32)
        for step in range(1, self.plane.chips):
            self.direct(chunk, step).wait_recv()
            total += self.rec[step - 1, :, cols].astype(F32)
        return total

    def drain(self, chunk):
        for step in range(self.plane.chips):
            self.across(chunk, step).wait_send()
        for step in range(1, self.plane.chips):
            self.direct(chunk, step).wait_send()


def loop(extent, body):
    lax.fori_loop(0, extent, lambda i, c: (body(i), c)[1], 0)


def rows_of(ref3, begin, count):
    value = ref3[pl.ds(begin, count)]
    return value.reshape(count * value.shape[1], value.shape[2])


def vmem():
    return pl.BlockSpec(memory_space=pltpu.VMEM)


def hbm():
    return pl.BlockSpec(memory_space=pltpu.HBM)


def shape(dims, dtype=BF):
    return jax.ShapeDtypeStruct(tuple(dims), dtype)


def params(ident, limit=62):
    return pltpu.CompilerParams(
        collective_id=ident, has_side_effects=True, vmem_limit_bytes=limit * MIB
    )


ROWS = 16
WIDTH = 512


def rotated(value, planes):
    return value * planes[0] + pltpu.roll(value, HEAD - ROT // 2, 1) * planes[1] + pltpu.roll(
        value, ROT // 2, 1
    ) * planes[2]


def rotated_back(value, planes):
    return value * planes[0] - pltpu.roll(value, HEAD - ROT // 2, 1) * planes[1] - pltpu.roll(
        value, ROT // 2, 1
    ) * planes[2]


class Exchange:
    def __init__(self, ns, sems, base):
        self.ns, self.sems, self.base = ns, sems, base
        self.me = lax.axis_index("seq")

    def copy(self, src, dst, lane, step):
        return send(
            src,
            dst,
            self.sems,
            self.base + lane * (self.ns - 1) + step - 1,
            "seq",
            wrap(self.me + step, self.ns),
        )


class Line:
    def __init__(self, plane, ns, part, inward, swap, res, sems, base, turned, copy_sem, credits):
        self.plane, self.ns, self.turned = plane, ns, turned
        self.part, self.inward, self.swap, self.res = part, inward, swap, res
        self.sems, self.base, self.copy_sem, self.credits = sems, base, copy_sem, credits
        self.me = lax.axis_index("seq")
        self.side = self.me // (ns // 2)
        middle = ns // 2 - 1
        self.depth = (1 - self.side) * (middle - self.me) + self.side * (self.me - middle - 1)
        self.ends = middle
        self.in_to = self.me + 1 - 2 * self.side
        self.out_to = self.me - 1 + 2 * self.side
        self.other = ns - 1 - self.me
        self.count = res.shape[0]
        self.slots = inward.shape[0]
        if self.ends != 1 and self.slots < self.count:
            raise ValueError("slots")

    @staticmethod
    def marks(nf, turned):
        return 5 + (nf - 1 if turned else 0)

    def sem(self, chunk, kind):
        return self.base + chunk * self.marks(self.plane.nf, self.turned) + kind

    def half(self, ref, chunk, side):
        rows = ref.shape[-2] // 2
        rows = pl.ds(pl.multiple_of(side * rows, rows), rows)
        return ref.at[chunk, :, rows, :]

    def inner(self, chunk, relayed=False):
        slot = chunk % self.slots
        src = self.inward.at[slot] if relayed else self.part.at[chunk]
        return send(src, self.inward.at[slot], self.sems, self.sem(chunk, 0), "seq", self.in_to)

    def cross(self, chunk):
        slot = chunk % self.slots
        return send(
            self.half(self.inward, slot, 1 - self.side),
            self.swap.at[slot],
            self.sems,
            self.sem(chunk, 1),
            "seq",
            self.other,
        )

    def result(self):
        return self.res if self.turned else self.part

    def back_cross(self, chunk, side=None):
        side = self.side if side is None else side
        return send(
            self.half(self.result(), chunk, side),
            self.half(self.res, chunk, side),
            self.sems,
            self.sem(chunk, 2),
            "seq",
            self.other,
        )

    def outer(self, chunk, side, src):
        return send(
            self.half(src, chunk, side),
            self.half(self.res, chunk, side),
            self.sems,
            self.sem(chunk, 3) + side,
            "seq",
            self.out_to,
        )

    def spread(self, chunk, step, source=None):
        rows = self.part.shape[-2] // 2
        rows = pl.ds(pl.multiple_of(self.side * rows, rows), rows)
        target = wrap(self.plane.me + step, self.plane.nf)
        source = self.plane.me if source is None else source
        return send(
            self.part.at[chunk, target, rows, :],
            self.res.at[chunk, source, rows, :],
            self.sems,
            self.sem(chunk, 4) + step,
            "fsdp",
            target,
        )

    def keep(self, chunk):
        if self.turned:
            rows = self.part.shape[-2] // 2
            rows = pl.ds(pl.multiple_of(self.side * rows, rows), rows)
            me = self.plane.me
            src, dst = self.part.at[chunk, me, rows, :], self.res.at[chunk, me, rows, :]
        else:
            src = self.half(self.part, chunk, self.side)
            dst = self.half(self.res, chunk, self.side)
        return pltpu.make_async_copy(src, dst, self.copy_sem.at[chunk])

    def begin(self, chunk):
        if self.ends:

            @pl.when(self.depth == self.ends)
            def _():
                if chunk >= self.slots:
                    pl.semaphore_wait(self.credits.at[0], 1)
                self.inner(chunk).start()

    def relay(self, chunk, hop):
        slot = chunk % self.slots

        @pl.when(self.depth == self.ends - hop)
        def _():
            self.inner(chunk).wait_recv()
            total = self.inward[slot].astype(F32) + self.part[chunk].astype(F32)
            self.inward[slot] = total.astype(BF)
            self.inner(chunk, True).start()

    def meet(self, chunk):
        slot = chunk % self.slots

        @pl.when(self.depth == 0)
        def _():
            self.inner(chunk).wait_recv()
            theirs = self.half(self.inward, slot, 1 - self.side)
            mine = self.half(self.part, chunk, 1 - self.side)

            def step(i):
                rows = tile(i, 16)
                total = theirs[:, rows, :].astype(F32) + mine[:, rows, :].astype(F32)
                theirs[:, rows, :] = total.astype(BF)

            loop(theirs.shape[1] // 16, step)
            if chunk >= self.slots:
                pl.semaphore_wait(self.credits.at[1], 1)
            self.cross(chunk).start()

    def settle(self, chunk):
        slot = chunk % self.slots

        @pl.when(self.depth == 0)
        def _():
            self.cross(chunk).wait_recv()
            theirs = self.half(self.inward, slot, self.side)
            mine = self.half(self.part, chunk, self.side)

            def step(i):
                rows = tile(i, 16)
                total = theirs[:, rows, :].astype(F32) + mine[:, rows, :].astype(F32)
                total += self.swap[slot, :, rows, :].astype(F32)
                mine[:, rows, :] = total.astype(BF)

            loop(theirs.shape[1] // 16, step)
            self.keep(chunk).start()
            if self.turned:
                for k in range(1, self.plane.nf):
                    self.spread(chunk, k).start()
            else:
                self.hand_out(chunk)
            self.cross(chunk).wait_send()
            if chunk + self.slots < self.count:
                pl.semaphore_signal(
                    self.credits.at[0], inc=1, device_id={"seq": self.out_to}, device_id_type=MESH
                )
                pl.semaphore_signal(
                    self.credits.at[1], inc=1, device_id={"seq": self.other}, device_id_type=MESH
                )

    def hand_out(self, chunk):
        self.back_cross(chunk).start()
        if self.ends:
            self.outer(chunk, self.side, self.result()).start()

    def spread_end(self, chunk):
        @pl.when(self.depth == 0)
        def _():
            for k in range(1, self.plane.nf):
                self.spread(chunk, k, wrap(self.plane.me - k, self.plane.nf)).wait_recv()
            self.keep(chunk).wait()
            self.hand_out(chunk)

    def pass_on(self, chunk):
        @pl.when(self.depth == 0)
        def _():
            self.back_cross(chunk, 1 - self.side).wait_recv()
            if self.ends:
                self.outer(chunk, 1 - self.side, self.res).start()

    def outward_hop(self, chunk, hop):
        @pl.when(self.depth == hop)
        def _():
            for side in range(2):
                self.outer(chunk, side, self.res).wait_recv()
                self.outer(chunk, side, self.res).start()

    def pause(self, chunk):
        pass

    def phases(self):
        listed = [partial(self.relay, hop=hop) for hop in range(1, self.ends)]
        listed += [self.meet, self.settle]
        if self.turned:
            listed += [self.spread_end]
        listed += [self.pass_on]
        listed += [partial(self.outward_hop, hop=hop) for hop in range(1, self.ends)]
        return listed

    def drain(self, chunk):
        @pl.when(self.depth == 0)
        def _():
            self.back_cross(chunk).wait_send()
            if self.turned:
                for k in range(1, self.plane.nf):
                    self.spread(chunk, k).wait_send()
            else:
                self.keep(chunk).wait()

        if self.ends:

            @pl.when(self.depth == self.ends)
            def _():
                for side in range(2):
                    self.outer(chunk, side, self.res).wait_recv()

            @pl.when(self.depth < self.ends)
            def _():
                for side in range(2):
                    self.outer(chunk, side, self.res).wait_send()

            @pl.when(self.depth > 0)
            def _():
                self.inner(chunk).wait_send()


class Ticks:
    def __init__(self, jobs, lead):
        self.jobs, self.lead = jobs, lead
        self.now, self.begun = 0, 0

    def open(self):
        line, chunk = self.jobs[self.begun]
        line.begin(chunk)
        self.begun += 1

    def tick(self, times=1):
        for _ in range(times):
            while self.begun < min(len(self.jobs), self.now + self.lead + 1):
                line, chunk = self.jobs[self.begun]
                line.begin(chunk)
                self.begun += 1
            for i, (line, chunk) in enumerate(self.jobs):
                phase = self.now - i - 1
                if 0 <= phase < len(line.phases()):
                    line.phases()[phase](chunk)
            self.now += 1

    def finish(self):
        depth = max(len(line.phases()) for line, _ in self.jobs)
        while self.now < len(self.jobs) + depth:
            self.tick()
        for line, chunk in self.jobs:
            line.drain(chunk)


class Lines:
    def __init__(self, nf, kinds):
        self.nf, self.kinds = nf, kinds

    def scratch(self):
        listed = []
        for (blocks, rows, cols), count, _ in self.kinds:
            slots = min(count, SLOTS)
            listed.append(pltpu.VMEM((slots, blocks, rows, cols), BF))
            listed.append(pltpu.VMEM((slots, blocks, rows // 2, cols), BF))
            listed.append(pltpu.SemaphoreType.DMA((count,)))
            listed.append(pltpu.SemaphoreType.REGULAR((2,)))
        marks = sum(count * Line.marks(self.nf, turned) for _, count, turned in self.kinds)
        return listed + [pltpu.SemaphoreType.DMA((marks,))] * 2

    def count(self):
        return 4 * len(self.kinds) + 2

    def outs(self):
        return [shape((count,) + dims) for dims, count, _ in self.kinds]

    def build(self, plane, ns, parts, results, scratch):
        lines, base = [], 0
        sems = tuple(scratch[-2:])
        for k, (_, count, turned) in enumerate(self.kinds):
            inward, swap, copy_sem, credits = scratch[4 * k : 4 * k + 4]
            lines.append(
                Line(
                    plane,
                    ns,
                    parts[k],
                    inward,
                    swap,
                    results[k],
                    sems,
                    base,
                    turned,
                    copy_sem,
                    credits,
                )
            )
            base += count * Line.marks(self.nf, turned)
        return lines


def forward_lines(nf, wide, hidden):
    width = hidden // CHUNKS
    return Lines(nf, [((1, width, D * LANES // width), hidden // LANES, False)])


def forward_kernel(nf, ns, lines, *refs):
    hist_ref, g_ref, win_ref, wq_ref, wk_ref, wv_ref, wo_f32, wout_f32 = refs[:8]
    tab_ref, mix_in_ref, mix_out_ref, again_ref, mgain_ref, xgain_ref = refs[8:14]
    refs = refs[14:]
    (xq_out, xk_out, xv_out, gg_out, py_out, w_out, rest_in) = refs[:7]
    wo_out, wrow_out, win_out, st_out, sum_out = refs[7:12]
    att_ref, dq_ref, dk_ref, dv_ref, dxr_ref = refs[12:17]
    coef_ref, inv_ref, pre_ref, act_ref, mixed_ref = refs[17:22]
    refs = refs[22:]
    (xr, gg, wfull, hid, dup, p_out, p_in, stage, wqkv, zin, zback, dkv) = refs[:12]
    wout_ref, wo_ref, wtile, sts, lows, h8, tab, sib, rec = refs[12:21]
    send_sem, recv_sem, copy_sem = refs[21:24]
    line_refs = refs[24:]
    plane = Plane(nf)
    sems = (send_sem, recv_sem)
    tok = g_ref.shape[0]
    wide = wo_ref.shape[0]
    heads = wide // HEAD
    per = nf // ns
    slab = per * tok
    group_tok = ns * tok
    sq = lax.axis_index("seq")
    width = wfull.shape[1] // CHUNKS
    blocks = min(4, nf)
    pieces = width // LANES
    step_sems = nf - 1
    greet(nf, ns)
    (l_out,) = lines.build(plane, ns, (p_out,), (sum_out,), line_refs)
    ticks = Ticks([(l_out, chunk) for chunk in range(l_out.count)], 1)
    ag_r = Gather(plane, xr.at[plane.me], xr, sems, 0)
    ag_x = [
        Gather(plane, out.at[plane.me], out, sems, (2 + i) * step_sems)
        for i, out in enumerate((xq_out, xk_out, xv_out))
    ]
    turn = Turn(plane, win_out, wfull, sems, 5 * step_sems, CHUNKS)
    turns = [
        Turn(plane, wrow_out.at[i], wqkv.at[i], sems, (5 + CHUNKS + i) * step_sems, 1)
        for i in range(3)
    ]
    ag_t = Gather(plane, tab_ref, tab, sems, (8 + CHUNKS) * step_sems)
    scat = Scatter(plane, xr, sib, rec, sems, (9 + CHUNKS) * step_sems, CHUNKS)
    base = (9 + 2 * CHUNKS) * step_sems
    part_cols = D // pieces
    ag_gs = []
    for p in range(pieces):
        cols = slice(p * part_cols, (p + 1) * part_cols)
        at = base + (p - 1) * step_sems if p else step_sems
        ag_gs.append(Gather(plane, g_ref.at[:, cols], gg.at[:, :, cols], sems, at))
    base += (pieces - 1) * step_sems
    there = Exchange(ns, sems, base)
    home = Exchange(ns, sems, base + 4 * (ns - 1))
    late = HIST - 1
    entries = pltpu.make_async_copy(hist_ref.at[pl.ds(0, late)], stage.at[pl.ds(0, late)], copy_sem.at[5])
    newest = pltpu.make_async_copy(hist_ref.at[late], h8, copy_sem.at[6])
    newest.start()
    entries.start()
    ag_gs[0].start()
    keeps = [ag_gs[p].keep(copy_sem.at[8 + p]) for p in range(pieces)]
    keeps.append(ag_t.keep(copy_sem.at[7]))
    for keep in keeps:
        keep.start()
    high, broad = width, part_cols

    def tiles_of(src, dst, store):
        for r in range(0, src.shape[0], high):
            for c in range(0, src.shape[1], broad):
                where = (pl.ds(r, high), pl.ds(c, broad))
                casts.append((src.at[where], dst.at[where], store))

    def fetch(n):
        return pltpu.make_async_copy(casts[n][0], wtile.at[n % 2], copy_sem.at[16 + n % 2])

    def cast_all():
        stores = []
        fetch(0).start()
        fetch(1).start()
        for n, (_, dst, store) in enumerate(casts):
            fetch(n).wait()
            low = p_out.at[len(stores), 0] if store else dst

            def cast_step(i, n=n, low=low):
                rows = tile(i, ROWS)
                low[rows, :] = wtile[n % 2, rows, :].astype(BF)

            loop(high // ROWS, cast_step)
            if n + 2 < len(casts):
                fetch(n + 2).start()
            if store:
                stores.append(pltpu.make_async_copy(low, dst, copy_sem.at[18 + len(stores)]))
                stores[-1].start()
        for copy in stores:
            copy.wait()

    casts = []
    tiles_of(win_ref, win_out, True)
    cast_all()
    turn.start(0)
    keeps.append(turn.keep(copy_sem.at[1]))
    keeps[-1].start()
    newest.wait()

    def mix_step(i):
        rows = tile(i, ROWS)
        value = h8[rows, :].astype(F32)
        inv = lax.rsqrt(jnp.mean(value * value, axis=1, keepdims=True) + EPSILON)
        mixed_ref[rows, :] = (value * inv * xgain_ref[...]).astype(BF)
        inv_ref[STREAMS, rows, :] = inv

    loop(tok // ROWS, mix_step)
    pre = dot(mixed_ref[...], mix_in_ref[...].astype(BF), 1, 1)
    pre_ref[...] = pre
    act = (0.5 * pre * (1.0 + lax.erf(pre * (0.5**0.5)))).astype(BF)
    act_ref[...] = act
    coef_ref[...] = dot(act, mix_out_ref[...].astype(BF), 1, 1)
    entries.wait()

    def tiles_out(i, slot):
        rows = tile(i, ROWS)
        listed = [pltpu.make_async_copy(sts.at[slot], st_out.at[:, rows, :], copy_sem.at[26 + slot])]
        for c, out in enumerate((xq_out, xk_out, xv_out)):
            dst = out.at[plane.me, rows, :]
            sem = copy_sem.at[28 + c * 2 + slot]
            listed.append(pltpu.make_async_copy(lows.at[slot, c], dst, sem))
        return listed

    def stream_step(i):
        slot = lax.rem(i, 2)
        rows = tile(i, ROWS)

        @pl.when(i > 1)
        def _():
            for copy in tiles_out(i - 2, slot):
                copy.wait()

        coef = coef_ref[rows, :]
        squares = [jnp.zeros((ROWS, 1), F32)] * STREAMS
        for begin in range(0, D, WIDTH):
            cols = slice(begin, begin + WIDTH)
            total = [jnp.zeros((ROWS, WIDTH), F32)] * STREAMS
            for j in range(HIST):
                entry = (stage[j, rows, cols] if j < late else h8[rows, cols]).astype(F32)
                for c in range(STREAMS):
                    at = c * HIST + j
                    total[c] = total[c] + coef[:, at : at + 1] * entry
            for c in range(STREAMS):
                sts[slot, c, :, cols] = total[c]
                squares[c] = squares[c] + jnp.sum(total[c] * total[c], axis=1, keepdims=True)
        for c in range(STREAMS):
            inv = lax.rsqrt(squares[c] / D + EPSILON)
            inv_ref[c, rows, :] = inv
            gain = mgain_ref if c == STREAMS - 1 else again_ref
            normed = (sts[slot, c] * inv * gain[...]).astype(BF)
            if c < STREAMS - 1:
                lows[slot, c] = normed
            else:
                xr[plane.me, rows, :] = normed
        for copy in tiles_out(i, slot):
            copy.start()

    steps = tok // ROWS
    loop(steps, stream_step)
    ag_r.start()
    for p in range(1, pieces):
        ag_gs[p].start()
    for chunk in range(1, CHUNKS):
        turn.start(chunk)
    ag_t.start()
    for i in (steps - 2, steps - 1):
        for copy in tiles_out(i, i % 2):
            copy.wait()
    ag_x[0].start()
    casts = []
    tiles_of(wout_f32, wout_ref, False)
    tiles_of(wo_f32, wo_ref, False)
    for i, w in enumerate((wq_ref, wk_ref, wv_ref)):
        tiles_of(w, wrow_out.at[i], True)
    cast_all()
    for i in range(3):
        if i:
            ag_x[i].start()
        turns[i].start(0)
        keeps.append(turns[i].keep(copy_sem.at[2 + i]))
        keeps[-1].start()
    ag_gs[0].forward()
    ag_r.forward()
    ag_gs[0].finish()
    ag_r.finish()
    for keep in keeps:
        keep.wait()
    saves, started = [], []

    def save(src, dst):
        started.append(dst)
        saves.append(pltpu.make_async_copy(src, dst, copy_sem.at[36 + len(started)]))
        saves[-1].start()

    save(wo_ref, wo_out)

    def act(up):
        return 0.5 * (1.0 + lax.erf(up * (0.5**0.5)))

    def out_grad(chunk, p):
        cols = slice(chunk * width, chunk * width + width)

        def step(i):
            feats = pl.ds(pl.multiple_of(p * part_cols + i * WIDTH, WIDTH), WIDTH)
            every = gg[:, :, feats].reshape(nf * tok, WIDTH)
            grad = dot(hid[:, cols], every, 0, 0).astype(BF)
            p_out[chunk * pieces + p, 0, :, tile(i, WIDTH)] = grad

        loop(part_cols // WIDTH, step)

    def first_step(i):
        rows = tile(i, blocks * tok)
        up = dot(rows_of(xr, i * blocks, blocks), wfull[:, 0:width])
        hid[rows, 0:width] = (up * act(up)).astype(BF)

    turn.arrive(0)
    loop(nf // blocks, first_step)
    out_grad(0, 0)
    ticks.open()
    for p in range(1, pieces):
        ag_gs[p].forward()
        ag_gs[p].finish()
    save(gg, gg_out)

    for chunk in range(CHUNKS):
        if chunk:
            turn.arrive(chunk)
        cols = slice(chunk * width, chunk * width + width)

        def rows_step(i, cols=cols):
            rows = tile(i, blocks * tok)
            up = dot(rows_of(xr, i * blocks, blocks), wfull[:, cols])
            dh = dot(rows_of(gg, i * blocks, blocks), wout_ref[cols, :], 1, 1)
            cdf = act(up)
            slope = cdf + up * jnp.exp(-0.5 * up * up) * 0.3989422804014327
            hid[rows, cols] = (up * cdf).astype(BF)
            dup[rows, cols] = (dh * slope).astype(BF)

        loop(nf // blocks, rows_step)

        for p in range(1 if chunk == 0 else 0, pieces):
            out_grad(chunk, p)
        ticks.tick()

        def grad_step(i, cols=cols, chunk=chunk):
            feats = tile(i, WIDTH)
            every = xr[:, :, feats].reshape(nf * tok, WIDTH)
            grad = dot(every, dup[:, cols], 0, 0).astype(BF)
            count = WIDTH * nf // D
            for k in range(pieces):
                piece = grad[:, k * LANES : k * LANES + LANES].reshape(count, D // nf, LANES)
                p_in[chunk * pieces + k, pl.ds(i * count, count)] = piece

        loop(D // WIDTH, grad_step)

    save(p_in, rest_in)

    def scatter_step(chunk):
        feats = tile(chunk, D // CHUNKS)
        value = dot(dup[...], wfull[feats, :], 1, 1).astype(BF)
        xr[:, :, feats] = value.reshape(nf, tok, D // CHUNKS)
        scat.start(chunk)

    ag_r.drain()
    loop(CHUNKS, scatter_step)

    def lane(i):
        return slice(i * wide, (i + 1) * wide)

    def ship(i):
        for step in range(1, ns):
            target = wrap(sq + step, ns)
            there.copy(dup.at[tile(target, slab), lane(i)], zin.at[i, sq], i, step).start()
        zin[i, sq] = dup[tile(sq, slab), lane(i)]

    def da_step(i):
        rows = tile(i, blocks * tok)
        dup[rows, lane(3)] = dot(rows_of(gg, i * blocks, blocks), wo_ref[...], 1, 1).astype(BF)

    loop(nf // blocks, da_step)
    ship(3)
    loop(CHUNKS, scat.combine)
    ticks.tick()
    ag_t.forward()
    ag_t.finish()
    for i in range(3):
        ag_x[i].forward()
        turns[i].arrive(0)
        ag_x[i].finish()
        load = pltpu.make_async_copy(ag_x[i].buf, stage, copy_sem.at[15])
        load.start()
        load.wait()

        def lin_step(r, i=i):
            rows = tile(r, blocks * tok)
            lin = dot(rows_of(stage, r * blocks, blocks), wqkv[i])
            if i < 2:
                planes = rope_planes(rows_of(tab, r * blocks, blocks))
            for head in range(heads):
                piece = lin[:, head * HEAD : head * HEAD + HEAD]
                if i < 2:
                    piece = rotated(piece, planes)
                at = i * wide + head * HEAD
                dup[rows, at : at + HEAD] = piece.astype(BF)

        loop(nf // blocks, lin_step)
        ship(i)
        ticks.tick(2 if i < 2 else 1)
    save(wqkv, w_out)

    def out_step(i):
        feats = tile(i, WIDTH)
        value = dot(hid[...], wout_ref[:, feats]).astype(BF)
        stage[:, :, feats] = value.reshape(nf, tok, WIDTH)

    loop(D // WIDTH, out_step)
    save(stage, py_out)
    for i in range(4):
        for step in range(1, ns):
            there.copy(zin.at[i, 0], zin.at[i, wrap(sq - step, ns)], i, step).wait_recv()

    scale = HEAD ** (-0.5)
    queries = min(256, group_tok)
    q_slabs = queries // tok

    def pair_step(pair):
        grp = pair // heads
        head = lax.rem(pair, heads)
        cols = tile(head, HEAD)
        toks = tile(grp, tok)
        marks = tab[sq * per + grp, 0:1, :]
        first_end, second_end = marks[:, ROT : ROT + 1], marks[:, ROT + 1 : ROT + 2]

        def part_of(i, begin, count):
            return zin[i, pl.ds(begin, count), toks, cols].reshape(count * tok, HEAD)

        def keep_rows(i, begin, count, value):
            at = pl.ds(pl.multiple_of(i * wide + head * HEAD, HEAD), HEAD)
            for k in range(count):
                rows = pl.ds(pl.multiple_of((begin + k) * slab + grp * tok, tok), tok)
                hid[rows, at] = value[k * tok : (k + 1) * tok].astype(BF)

        keys, values = part_of(1, 0, ns), part_of(2, 0, ns)
        dkv[...] = jnp.zeros_like(dkv)

        def query_step(j):
            begin = j * q_slabs
            query, d_att = part_of(0, begin, q_slabs), part_of(3, begin, q_slabs)
            qi = j * queries + lax.broadcasted_iota(jnp.int32, (queries, group_tok), 0)
            ki = lax.broadcasted_iota(jnp.int32, (queries, group_tok), 1)
            qf, kf = qi.astype(F32), ki.astype(F32)
            seg_q = (qf >= first_end).astype(jnp.int32) + (qf >= second_end).astype(jnp.int32)
            seg_k = (kf >= first_end).astype(jnp.int32) + (kf >= second_end).astype(jnp.int32)
            allowed = (seg_q == seg_k) & (qi >= ki)
            scores = jnp.where(allowed, dot(query, keys, 1, 1) * scale, NEGATIVE)
            top = jnp.max(scores, axis=1, keepdims=True)
            expo = jnp.where(allowed, jnp.exp(scores - top), 0.0)
            prob = expo / jnp.sum(expo, axis=1, keepdims=True)
            prob_low = prob.astype(BF)
            attended = dot(prob_low, values)
            delta = jnp.sum(d_att.astype(F32) * attended, axis=1, keepdims=True)
            d_score = (prob * (dot(d_att, values, 1, 1) - delta)).astype(BF)
            d_query = dot(d_score, keys) * scale
            dkv[0] += dot(d_score, query, 0, 0)
            dkv[1] += dot(prob_low, d_att, 0, 0)
            keep_rows(0, begin, q_slabs, attended)
            keep_rows(1, begin, q_slabs, d_query)

        loop(group_tok // queries, query_step)
        keep_rows(2, 0, ns, dkv[0] * scale)
        keep_rows(3, 0, ns, dkv[1])

    loop(per * heads, pair_step)

    for i in (1, 2, 3, 0):
        for step in range(1, ns):
            target = wrap(sq + step, ns)
            src = hid.at[tile(target, slab), lane(i)]
            home.copy(src, zback.at[i, tile(sq, slab), :], i, step).start()
        zback[i, tile(sq, slab), :] = hid[tile(sq, slab), lane(i)]
    ticks.tick()
    outs = (att_ref, dq_ref, dk_ref, dv_ref)
    for i in (1, 2, 3, 0):
        for step in range(1, ns):
            source = wrap(sq - step, ns)
            dst = zback.at[i, tile(source, slab), :]
            home.copy(dst, dst, i, step).wait_recv()
        if i in (1, 2):

            def back_step(r, i=i):
                rows = tile(r, tok)
                planes = rope_planes(tab[r])
                for head in range(heads):
                    cols = slice(head * HEAD, head * HEAD + HEAD)
                    piece = zback[i, rows, cols].astype(F32)
                    piece = rotated_back(piece, planes)
                    zback[i, rows, cols] = piece.astype(BF)

            loop(nf, back_step)
        save(zback.at[i], outs[i])
        ticks.tick()

    def total_step(chunk):
        value = scat.total(chunk)
        sts[:, :, :, tile(chunk, D // CHUNKS)] = value.reshape(*sts.shape[:3], D // CHUNKS)
        scat.drain(chunk)

    loop(CHUNKS, total_step)
    save(sts, dxr_ref)
    ticks.finish()
    for gather in (*ag_gs, ag_t, *ag_x):
        gather.drain()
    for chunk in range(CHUNKS):
        turn.drain(chunk)
    for i in range(3):
        turns[i].drain(0)
    for copy in saves:
        copy.wait()
    for i in range(4):
        for step in range(1, ns):
            there.copy(zin.at[i, 0], zin.at[i, 0], i, step).wait_send()
            home.copy(zin.at[i, 0], zin.at[i, 0], i, step).wait_send()


def run_forward(nf, ns, hist, g_own, win, ws, wo, wout, table, mixing):
    tok = g_own.shape[0]
    hidden = wout.shape[0]
    wide = wo.shape[0]
    units = mixing[0].shape[0]
    lines = forward_lines(nf, wide, hidden)
    count = (8 + 2 * CHUNKS + hidden // CHUNKS // LANES) * (nf - 1) + 8 * (ns - 1)
    flat = shape((nf * tok, wide))
    block = shape((nf, tok, D))
    total = CHUNKS * (hidden // CHUNKS // LANES)
    outs = [block] * 5 + [shape((3, D, wide)), shape((total, nf, D // nf, LANES))]
    outs += [shape((wide, D)), shape((3, wide, D)), shape(win.shape)]
    outs += [shape((STREAMS, tok, D), F32)]
    slots = tok // STREAMS // ROWS
    outs += lines.outs() + [flat] * 4 + [shape((slots, STREAMS, ROWS, D), F32)]
    outs += [shape((tok, STREAMS * HIST), F32), shape((STREAMS + 1, tok, 1), F32)]
    outs += [shape((tok, units), F32), shape((tok, units)), shape((tok, D))]
    exchange = pltpu.VMEM((4, ns, nf // ns * tok, wide), BF)
    return pl.pallas_call(
        partial(forward_kernel, nf, ns, lines),
        out_shape=tuple(outs),
        in_specs=[hbm()] * 8 + [vmem()] * 6,
        out_specs=(hbm(),) * 17 + (vmem(),) * 5,
        scratch_shapes=[
            pltpu.VMEM((nf, tok, D), BF),
            pltpu.VMEM((nf, tok, D), BF),
            pltpu.VMEM((D, hidden), BF),
            pltpu.VMEM((nf * tok, hidden), BF),
            pltpu.VMEM((nf * tok, hidden), BF),
            pltpu.VMEM(lines.outs()[0].shape, BF),
            pltpu.VMEM((total, nf, D // nf, LANES), BF),
            pltpu.VMEM((nf, tok, D), BF),
            pltpu.VMEM((3, D, wide), BF),
            exchange,
            pltpu.VMEM((4, nf * tok, wide), BF),
            pltpu.VMEM((2, ns * tok, HEAD), F32),
            pltpu.VMEM((hidden, D), BF),
            pltpu.VMEM((wide, D), BF),
            pltpu.VMEM((2,) + lines.kinds[0][0][1:], F32),
            pltpu.VMEM((slots, STREAMS, ROWS, D), F32),
            pltpu.VMEM((2, STREAMS - 1, ROWS, D), BF),
            pltpu.VMEM((tok, D), BF),
            pltpu.VMEM((nf, tok, LANES), F32),
            pltpu.VMEM((nf // 2, tok, D), BF),
            pltpu.VMEM((nf // 2 - 1, tok, D), BF),
            pltpu.SemaphoreType.DMA((count,)),
            pltpu.SemaphoreType.DMA((count,)),
            pltpu.SemaphoreType.DMA((48,)),
        ]
        + lines.scratch(),
        compiler_params=params(1, 63),
        name="forward",
    )(hist, g_own, win, *ws, wo, wout, table, *mixing)


TENSORS = 4
SMALL = 112


def back_lines(nf, wide, rest):
    counts = [rest] + [wide // LANES] * 3
    kinds = [((nf, D // nf, LANES), count, True) for count in counts]
    return Lines(nf, kinds + [((1, LANES, D), wide // LANES, False)])


def back_kernel(nf, ns, lines, *refs):
    att_ref, dq_ref, dk_ref, dv_ref, wqkv, wo_ref, p_in, g_ref = refs[:8]
    coef_ref, inv_ref, pre_ref, act_ref, mixed_ref, mix_in_ref, mix_out_ref = refs[8:15]
    again_ref, mgain_ref, xgain_ref = refs[15:18]
    sources, (dxr_ref, py_ref, hist_ref, st_ref) = refs[18:22], refs[22:26]
    lo_ref, sm_out, hg_ref = refs[26:29]
    results, refs = refs[29:34], refs[34:]
    stage, part, sib, rec, grads, p_o, dx_ref, y_ref = refs[:8]
    hists, sts, hgs, h8, ds, dcoef, gsum = refs[8:15]
    sm_ref, sm_src, sm_in, sm_z, sm_sem, sm_rsem = refs[15:21]
    send_sem, recv_sem, copy_sem, tile_sem, credit = refs[21:26]
    line_refs = refs[26:]
    dmixed, last = dx_ref.at[0], dx_ref.at[1]
    plane = Plane(nf)
    sems = (send_sem, recv_sem)
    tok = lo_ref.shape[0]
    wide = wo_ref.shape[0]
    parts, sibs = part.shape[0], sib.shape[0]
    greet(nf, ns)
    built = lines.build(plane, ns, (p_in, *[grads.at[t] for t in range(3)], p_o), results, line_refs)
    jobs = []
    for line in built:
        jobs += [(line, chunk) for chunk in range(line.count)]
    ticks = Ticks(jobs, 1)
    small = Small(plane, ns, sm_src, sm_in, sm_z, sm_out, (sm_sem, sm_rsem))
    ticks.tick()
    load = pltpu.make_async_copy(sources[0], stage, copy_sem.at[0])
    load.start()
    pltpu.make_async_copy(hist_ref.at[HIST - 1], h8, copy_sem.at[1]).start()
    extra = pltpu.make_async_copy(dxr_ref, dx_ref.at[3], copy_sem.at[2 + CHUNKS])
    extra.start()
    scats = [
        Scatter(
            plane,
            part.at[t % parts],
            sib.at[t % sibs],
            rec.at[t % sibs],
            sems,
            t * CHUNKS * (nf - 1),
            CHUNKS,
        )
        for t in range(TENSORS)
    ]
    firsts = (dq_ref, dk_ref, dv_ref)

    def total(t):
        def total_step(chunk):
            feats = tile(chunk, D // CHUNKS)
            if t < 3:
                dx_ref[t, :, feats] = scats[t].total(chunk)
            else:
                lo_ref[:, feats] = (y_ref[:, feats] + scats[t].total(chunk)).astype(BF)

        loop(CHUNKS, total_step)
        if t + sibs < TENSORS:
            for target in [plane.on(0, 1)] + [plane.on(k) for k in range(1, plane.chips)]:
                pl.semaphore_signal(
                    credit.at[t], inc=1, device_id={"fsdp": target}, device_id_type=MESH
                )

    def fetch(t, chunk):
        feats = slice(chunk * (D // CHUNKS), (chunk + 1) * (D // CHUNKS))
        return pltpu.make_async_copy(py_ref.at[:, :, feats], scats[t].part.at[:, :, feats], copy_sem.at[2 + chunk])

    for t in range(TENSORS):
        if t >= sibs:
            pl.semaphore_wait(credit.at[t - sibs], plane.chips)
        if t >= 3:
            for chunk in range(CHUNKS):
                scats[t - parts].drain(chunk)
                fetch(t, chunk).start()
        for chunk in range(CHUNKS):
            feats = slice(chunk * (D // CHUNKS), (chunk + 1) * (D // CHUNKS))
            if t < 3:
                if t >= parts:
                    scats[t - parts].drain(chunk)
                value = dot(firsts[t][...], wqkv[t, feats, :], 1, 1)
                scats[t].part[:, :, feats] = value.astype(BF).reshape(nf, tok, D // CHUNKS)
            else:
                fetch(t, chunk).wait()
            if t == 3:
                value = dot(att_ref[...], wo_ref[:, feats]).reshape(nf, tok, D // CHUNKS)
                value = value + scats[t].part[:, :, feats].astype(F32)
                scats[t].part[:, :, feats] = value.astype(BF)
            scats[t].start(chunk)
            if chunk > 0:
                scats[t].combine(chunk - 1)
            if chunk % 2:
                ticks.tick()
        scats[t].combine(CHUNKS - 1)
        if t < TENSORS:
            pltpu.make_async_copy(sources[t], stage, copy_sem.at[0]).wait()

            def grad_step(i, t=t):
                feats = tile(i, WIDTH)
                every = stage[:, :, feats].reshape(nf * tok, WIDTH)
                if t < 3:
                    grad = dot(every, firsts[t][...], 0, 0).astype(BF)
                    count = WIDTH * nf // D
                    for k in range(wide // LANES):
                        piece = grad[:, k * LANES : k * LANES + LANES]
                        piece = piece.reshape(count, D // nf, LANES)
                        grads[t, k, pl.ds(i * count, count)] = piece
                else:
                    grad = dot(att_ref[...], every, 0, 0).astype(BF)
                    for k in range(wide // LANES):
                        p_o[k, 0, :, feats] = grad[k * LANES : k * LANES + LANES]

            loop(D // WIDTH, grad_step)
            if t < 3:
                pltpu.make_async_copy(sources[t + 1], stage, copy_sem.at[0]).start()
        if t:
            total(t - 1)

    extra.wait()
    gsum[...] = jnp.zeros_like(gsum)
    steps = tok // ROWS

    def tiles_in(i, slot):
        rows = pl.ds(i * ROWS, ROWS)
        first = pltpu.make_async_copy(hist_ref.at[:, rows, :], hists.at[slot], tile_sem.at[slot])
        second = pltpu.make_async_copy(st_ref.at[:, rows, :], sts.at[slot], tile_sem.at[2 + slot])
        return first, second

    def tiles_out(i, slot):
        rows = pl.ds(i * ROWS, ROWS)
        dst = hg_ref.at[pl.ds(0, HIST - 1), rows, :]
        return pltpu.make_async_copy(hgs.at[slot], dst, tile_sem.at[4 + slot])

    def back(value, inv, gain, grad):
        scaled = grad * gain
        mean = jnp.sum(value * scaled, axis=1, keepdims=True) / D
        return inv * scaled - value * (inv * inv * inv * mean)

    def row_step(i, slot):
        rows = pl.ds(i * ROWS, ROWS)
        for copy in tiles_in(i, slot):
            copy.wait()
        if i + 1 < steps:
            for copy in tiles_in(i + 1, 1 - slot):
                copy.start()
        if i > 1:
            tiles_out(i - 2, slot).wait()
        coef = coef_ref[rows, :]
        lane = lax.broadcasted_iota(jnp.int32, (ROWS, STREAMS * HIST), 1)
        for c in range(STREAMS):
            value, inv = sts[slot, c], inv_ref[c, rows, :]
            grad = dx_ref[c, rows, :]
            gain = mgain_ref if c == STREAMS - 1 else again_ref
            gsum[c // 3] += grad * (value * inv)
            d_value = back(value, inv, gain[...], grad)
            if c == STREAMS - 1:
                d_value = d_value + g_ref[rows, :].astype(F32)
                y_ref[rows, :] = value
            ds[c] = d_value
        found = jnp.zeros((ROWS, STREAMS * HIST), F32)
        for j in range(HIST):
            sums = [jnp.zeros((ROWS, 128), F32)] * STREAMS
            for begin in range(0, D, WIDTH):
                cols = slice(begin, begin + WIDTH)
                entry = hists[slot, j, :, cols].astype(F32)
                grad = jnp.zeros((ROWS, WIDTH), F32)
                for c in range(STREAMS):
                    at = c * HIST + j
                    value = ds[c, :, cols]
                    grad = grad + coef[:, at : at + 1] * value
                    product = value * entry
                    for k in range(0, WIDTH, 128):
                        sums[c] = sums[c] + product[:, k : k + 128]
                if j < HIST - 1:
                    hgs[slot, j, :, cols] = grad.astype(BF)
                else:
                    last[rows, cols] = grad
            for c in range(STREAMS):
                value = jnp.sum(sums[c], axis=1, keepdims=True)
                found = jnp.where(lane == c * HIST + j, value, found)
        dcoef[rows, :] = found.astype(BF)
        tiles_out(i, slot).start()

    for copy in tiles_in(0, 0):
        copy.start()
    for i in range(steps):
        row_step(i, i % 2)
        if i % 2:
            ticks.tick()
    total(TENSORS - 1)
    mix_in, mix_out = mix_in_ref[...].astype(BF), mix_out_ref[...].astype(BF)
    pre, d_coef = pre_ref[...], dcoef[...]
    slope = 0.5 * (1.0 + lax.erf(pre * (0.5**0.5)))
    slope = slope + pre * jnp.exp(-0.5 * pre * pre) * 0.3989422804014327
    d_pre = (dot(d_coef, mix_out) * slope).astype(BF)
    hidden = pre.shape[1]
    sm_ref[0:hidden, :] = dot(d_pre, mixed_ref[...], 0, 0)
    dmixed[...] = dot(d_pre, mix_in)
    pltpu.make_async_copy(hist_ref.at[HIST - 1], h8, copy_sem.at[1]).wait()

    def last_step(i):
        rows = tile(i, ROWS)
        value, inv, grad = h8[rows, :].astype(F32), inv_ref[STREAMS, rows, :], dmixed[rows, :]
        gsum[2] += grad * (value * inv)
        h8[rows, :] = (last[rows, :] + back(value, inv, xgain_ref[...], grad)).astype(BF)

    loop(steps, last_step)
    end = pltpu.make_async_copy(h8, hg_ref.at[HIST - 1], copy_sem.at[1])
    end.start()
    for k in range(3):
        sm_ref[hidden + k : hidden + k + 1, :] = jnp.sum(gsum[k], axis=0, keepdims=True)
    begin = hidden + 3
    sm_ref[begin:SMALL, :] = jnp.zeros((SMALL - begin, D), F32)
    turned = dot(d_coef, act_ref[...], 0, 0)
    for k in range(STREAMS * HIST):
        at = begin + k // STREAMS
        cols = slice(k % STREAMS * (D // nf), k % STREAMS * (D // nf) + hidden)
        sm_ref[at : at + 1, cols] = turned[k : k + 1, :]
    for k in range(nf):
        sm_src[k] = sm_ref[:, k * (D // nf) : (k + 1) * (D // nf)]
    small.start()
    ticks.tick(2)
    small.across()
    ticks.tick(2)
    small.finish()
    ticks.finish()
    small.drain()
    for t in range(TENSORS - parts, TENSORS):
        loop(CHUNKS, scats[t].drain)
    end.wait()
    for i in (steps - 2, steps - 1):
        tiles_out(i, i % 2).wait()


def run_back(nf, ns, near, far):
    wo = near[5]
    tok = near[7].shape[0]
    wide = wo.shape[0]
    chips = nf // 2
    cols = D // nf
    count = TENSORS * CHUNKS * (nf - 1)
    few = 2 * (nf - 1) + ns - 1
    parts = 2 if nf <= 8 else 1
    lines = back_lines(nf, wide, near[6].shape[0])
    outs = [shape((tok, D)), shape((nf, SMALL, cols), F32), shape((HIST, tok, D))]
    return pl.pallas_call(
        partial(back_kernel, nf, ns, lines),
        out_shape=tuple(outs + lines.outs()),
        in_specs=[vmem()] * len(near) + [hbm()] * len(far),
        out_specs=(vmem(),) * 2 + (hbm(),) * 6,
        scratch_shapes=[
            pltpu.VMEM((nf, tok, D), BF),
            pltpu.VMEM((parts, nf, tok, D), BF),
            pltpu.VMEM((2, chips, tok, D), BF),
            pltpu.VMEM((2, chips - 1, tok, D), BF),
            pltpu.VMEM((3, wide // LANES, nf, D // nf, LANES), BF),
            pltpu.VMEM((wide // LANES, 1, LANES, D), BF),
            pltpu.VMEM((4, tok, D), F32),
            pltpu.VMEM((tok, D), F32),
            pltpu.VMEM((2, HIST, ROWS, D), BF),
            pltpu.VMEM((2, STREAMS, ROWS, D), F32),
            pltpu.VMEM((2, HIST - 1, ROWS, D), BF),
            pltpu.VMEM((tok, D), BF),
            pltpu.VMEM((STREAMS, ROWS, D), F32),
            pltpu.VMEM((tok, STREAMS * HIST), BF),
            pltpu.VMEM((3, ROWS, D), F32),
            pltpu.VMEM((SMALL, D), F32),
            pltpu.VMEM((nf, SMALL, cols), F32),
            pltpu.VMEM((nf, SMALL, cols), F32),
            pltpu.VMEM((ns, SMALL, cols), F32),
            pltpu.SemaphoreType.DMA((few,)),
            pltpu.SemaphoreType.DMA((few,)),
            pltpu.SemaphoreType.DMA((count,)),
            pltpu.SemaphoreType.DMA((count,)),
            pltpu.SemaphoreType.DMA((3 + CHUNKS,)),
            pltpu.SemaphoreType.DMA((6,)),
            pltpu.SemaphoreType.REGULAR((TENSORS - 2,)),
        ]
        + lines.scratch(),
        compiler_params=params(2, 63),
        name="back",
    )(*near, *far)


class Small:
    def __init__(self, plane, ns, src, mid, line, out, sems):
        self.plane, self.ns, self.src, self.mid, self.line, self.out = plane, ns, src, mid, line, out
        self.sems = sems
        self.me = lax.axis_index("seq")

    def scatter(self, step):
        target = wrap(self.plane.me + step, self.plane.nf)
        return send(
            self.src.at[target], self.mid.at[self.plane.me], self.sems, step - 1, "fsdp", target
        )

    def along(self, step):
        me = self.line.at[self.me]
        slot = self.plane.nf - 1 + step - 1
        return send(me, me, self.sems, slot, "seq", wrap(self.me + step, self.ns))

    def spread(self, step):
        me = self.out.at[self.plane.me]
        slot = self.plane.nf - 1 + self.ns - 1 + step - 1
        return send(me, me, self.sems, slot, "fsdp", wrap(self.plane.me + step, self.plane.nf))

    def start(self):
        self.mid[self.plane.me] = self.src[self.plane.me]
        for step in range(1, self.plane.nf):
            self.scatter(step).start()

    def across(self):
        for step in range(1, self.plane.nf):
            self.scatter(step).wait_recv()
        total = self.mid[0]
        for k in range(1, self.plane.nf):
            total += self.mid[k]
        self.line[self.me] = total
        for step in range(1, self.ns):
            self.along(step).start()

    def finish(self):
        for step in range(1, self.ns):
            self.along(step).wait_recv()
        total = self.line[0]
        for k in range(1, self.ns):
            total += self.line[k]
        self.out[self.plane.me] = total
        for step in range(1, self.plane.nf):
            self.spread(step).start()

    def drain(self):
        for step in range(1, self.plane.nf):
            self.spread(step).wait_recv()
        for step in range(1, self.plane.nf):
            self.scatter(step).wait_send()
            self.spread(step).wait_send()
        for step in range(1, self.ns):
            self.along(step).wait_send()


def finish_kernel(units, *refs):
    sum_in, sum_q, sum_k, sum_v, out_ref, sm_ref, sum_o = refs[:7]
    w_in, wq, wk, wv, w_out, mix_in, mix_out, again, mgain, xgain, wo = refs[7:]
    for dst, ref in ((w_in, sum_in), (wq, sum_q), (wk, sum_k), (wv, sum_v)):
        for k in range(ref.shape[0]):
            dst[:, k * LANES : (k + 1) * LANES] = ref[k, 0].astype(F32)
    part = out_ref.shape[-1]
    for k in range(out_ref.shape[1]):
        w_out[:, k * part : (k + 1) * part] = out_ref[0, k].astype(F32)
    mix_in[...] = sm_ref[0, 0:units, :]
    for k, dst in enumerate((again, mgain, xgain)):
        dst[...] = sm_ref[0, units + k : units + k + 1, :]

    @pl.when(pl.program_id(0) == 0)
    def _():
        wo[...] = sum_o[...].astype(F32)

    @pl.when(pl.program_id(0) < STREAMS)
    def _():
        mix_out[0] = sm_ref[0, units + 3 : units + 3 + HIST, 0:LANES]


def run_finish(nf, units, turned, out, small, sum_o):
    cols = D // nf
    _, pieces, width, part = out.shape
    hidden = out.shape[0] * width
    high = hidden // nf
    wide = turned[1].shape[0] * LANES
    rows = turned[0].shape[2]

    def chunks(part):
        return pl.BlockSpec((part.shape[0], 1, rows, LANES), lambda i: (0, i, 0, 0))

    def block(height, width):
        return pl.BlockSpec((height, width), lambda i: (0, i))

    return pl.pallas_call(
        partial(finish_kernel, units),
        grid=(nf,),
        out_shape=(
            shape((rows, nf * hidden), F32),
            *[shape((rows, D), F32)] * 3,
            shape((hidden, D), F32),
            shape((units, D), F32),
            shape((STREAMS, HIST, LANES), F32),
            *[shape((1, D), F32)] * 3,
            shape((sum_o.shape[0], D), F32),
        ),
        in_specs=[
            *[chunks(part) for part in turned],
            pl.BlockSpec(
                (1, pieces, high, part),
                lambda i: (i * high // width, 0, lax.rem(i, width // high), 0),
            ),
            pl.BlockSpec((1, SMALL, cols), lambda i: (i, 0, 0)),
            pl.BlockSpec((sum_o.shape[0], D), lambda i: (0, 0)),
        ],
        out_specs=(
            block(rows, hidden),
            *[block(rows, wide)] * 3,
            pl.BlockSpec((hidden // nf, D), lambda i: (i, 0)),
            block(units, cols),
            pl.BlockSpec((1, HIST, LANES), lambda i: (jnp.minimum(i, STREAMS - 1), 0, 0)),
            *[block(1, cols)] * 3,
            pl.BlockSpec((sum_o.shape[0], D), lambda i: (0, 0)),
        ),
        compiler_params=pltpu.CompilerParams(vmem_limit_bytes=62 * MIB),
        name="finish",
    )(*turned, out, small, sum_o)


def local(
    nf,
    ns,
    history,
    cotangent,
    seq_lengths,
    wq,
    wk,
    wv,
    wo,
    w_in,
    w_out,
    mix_in,
    mix_out,
    attn_gain,
    mlp_gain,
    mix_gain,
):
    hist = history[:, 0]
    tok_rows = hist.shape[1]
    tok_index = lax.axis_index("seq") * tok_rows + jnp.arange(tok_rows, dtype=jnp.int32)
    table = token_table(tok_index, seq_lengths[0])
    grad_out = cotangent[0]
    mixing = (mix_in.T, mix_out.T, attn_gain[None], mlp_gain[None], mix_gain[None])
    outs = run_forward(
        nf, ns, hist, grad_out, w_in, (wq, wk, wv), wo, w_out, table, mixing
    )
    xgs, (gg, py, wqkv, p_in, wo_low, _, _, stream, sum_out) = outs[:3], outs[3:12]
    (att, dq, dk, dv, dxr), mixed = outs[12:17], outs[17:]
    dxr = dxr.reshape(tok_rows, D)
    near = (att, dq, dk, dv, wqkv, wo_low, p_in, grad_out, *mixed, *mixing)
    far = (*xgs, gg, dxr, py, hist, stream)
    layer_out, small, history_grad, sum_in, *sums, sum_o = run_back(nf, ns, near, far)
    units = mix_in.shape[1]
    dw_in, dwq, dwk, dwv, dwout, dmix_in, dmix_out, *dgains, dwo = run_finish(
        nf, units, (sum_in, *sums), sum_out.reshape(CHUNKS, -1, *sum_out.shape[2:]), small, sum_o.reshape(wo.shape)
    )
    dmix_out = dmix_out.transpose(2, 1, 0).reshape(LANES, STREAMS * HIST)[:units]
    return (
        layer_out[None],
        history_grad[:, None],
        dwq,
        dwk,
        dwv,
        dwo,
        dw_in,
        dwout,
        dmix_in.T,
        dmix_out,
        *[grad[0] for grad in dgains],
    )


def solution(mesh):
    rows, rep = P("fsdp", None), P()
    in_specs = (
        P(None, "fsdp", "seq", None),
        P("fsdp", "seq", None),
    ) + (rows,) * 7 + (rep,) * 5
    out_specs = (
        P("fsdp", "seq", None),
        P(None, "fsdp", "seq", None),
    ) + (rows,) * 6 + (rep,) * 5
    body = partial(local, mesh.shape["fsdp"], mesh.shape["seq"])
    return jax.shard_map(body, mesh=mesh, in_specs=in_specs, out_specs=out_specs, check_vma=False)
```
